32 devices in a mesh: row: 4 (over y, core), ma: 8 (over z, x).
Axes of the slice: x: 2, y: 2, z: 4, core: 2. Of those that a mesh axis runs over, the one named last changes fastest.
Arguments:
- coeffs: float32 [2, 2048, 2048], P(None, 'ma', 'row'), may hold values from -6 to 6
- legendre: bfloat16 [2048, 32, 2048], P('ma', None, 'row'), may hold values from -0.0029296875 to 0.0029296875
- alpha_table: float32 [64, 2048], P(None, 'row'), may hold values from -4 to 4
- beta_table: float32 [64, 2048], P(None, 'row'), may hold values from -4 to 4
- radial_weight: float32 [64], replicated, may hold values from 0.1 to 1
- radius_index: int32 [64], replicated, may hold values from 0 to 63
- orders: int32 [2048], replicated, may hold values from 0 to 2047, as said below
- cycle_offset: int32 [32], P('ma'), may hold values from 0 to 1
- cycle_weight: float32 [32], P('ma'), may hold values from 0.5 to 2
Outputs:
- gradient: float32 [2, 2048, 2048], P(None, 'ma', 'row')
The draws below stay inside these ranges and needn't reach their ends.
Inputs may be any that keep to these rules, and one draw needn't show every extreme that they name: orders names every order 0 to 2047 once. The orders 0 to 2047 fall into blocks of 16 consecutive ones; the 256 slots of each index of ma hold exactly two orders of each block, one of its lower half and its mirror in the upper half.
All inputs are finite; a program needn't handle non-finite values.
Results may differ from the reference program's by a relative error of at most 0.0049.
Values may be sent and summed in bfloat16 or wider, within the bound.
No kernel may reach another device: no remote copies, remote signals or barrier semaphores. Data moves between devices by JAX's collectives and lax.ppermute only.
A program may use at most 384 MiB of HBM per device.

```python
import math
import jax
import jax.numpy as jnp
from jax import lax

L = 2048
M = 2048
NPIX = 4096
NODES = 64
MDEV = 256
RADII = 64
CYCLES = 32


def draw_orders(key, part):
    device_count = M // MDEV
    block_count = MDEV // 2
    block_keys = jax.random.split(key, block_count)
    shuffles = jax.vmap(lambda subkey: jax.random.permutation(subkey, device_count))(block_keys).astype(jnp.int32)
    block_base = (2 * device_count * jnp.arange(block_count, dtype=jnp.int32))[:, None]
    lower_half = block_base + shuffles
    upper_half = block_base + 2 * device_count - 1 - shuffles
    assigned = jnp.stack([lower_half, upper_half], axis=-1)
    return jnp.transpose(assigned, (1, 0, 2)).reshape(M).astype(jnp.int32)


def plant(values, rng, low, largest):
    longest = values.shape.index(max(values.shape))
    spots = []
    for shift in (0, 1):
        where = [jax.random.randint(jax.random.fold_in(rng, axis), (), 0, length) for axis, length in enumerate(values.shape)]
        where[longest] = (where[longest] + shift) % values.shape[longest]
        spots.append(tuple(where))
    return values.at[spots[0]].set(low).at[spots[1]].set(largest)


def level_of(key, dims, pieces, low, top_value):
    loudness, own = 1.0, jax.random.fold_in(key, 6)
    for axis_at, parts in pieces:
        draws = jnp.exp(jax.random.uniform(jax.random.fold_in(own, axis_at), (parts,), jnp.float32, low / len(pieces), top_value / len(pieces)))
        loudness = loudness * jnp.repeat(draws, dims[axis_at] // parts).reshape([-1 if axis == axis_at else 1 for axis in range(len(dims))])
    return loudness


def scatter_about(stream_key, dims, deviation, bound, shards=(), kind=jnp.bfloat16):
    result = deviation * jax.random.normal(stream_key, dims, jnp.float32)
    if shards:
        result = result * level_of(stream_key, dims, shards, -0.22, 0.18)
    return jnp.clip(result, -bound, bound).astype(kind)


def setup_inputs(seed: int = 0) -> dict:
    key_list = jax.random.split(jax.random.key(seed), 10)
    return {
        "coeffs": scatter_about(key_list[0], (2, M, L), 1.0, 6.0, ((1, 8), (2, 4)), jnp.float32),
        "legendre": scatter_about(key_list[1], (M, CYCLES, L), (M * L) ** -0.5, 0.0029296875, ((0, 8), (2, 4))),
        "alpha_table": scatter_about(key_list[2], (NODES, L), 1.0, 4.0, ((1, 4),), jnp.float32),
        "beta_table": scatter_about(key_list[3], (NODES, L), 1.0, 4.0, ((1, 4),), jnp.float32),
        "radial_weight": jnp.clip(jnp.exp(jax.random.uniform(key_list[4], (NODES,), jnp.float32, math.log(0.1), math.log(1.0))), 0.1, 1.0),
        "radius_index": plant(jax.random.randint(key_list[5], (RADII,), 0, NODES), jax.random.fold_in(key_list[5], 1), 0, NODES - 1).astype(jnp.int32),
        "orders": draw_orders(jax.random.fold_in(key_list[9], 71), 0),
        "cycle_offset": plant(jax.random.randint(key_list[7], (CYCLES,), 0, 2), jax.random.fold_in(key_list[7], 1), 0, 1).astype(jnp.int32),
        "cycle_weight": jnp.clip(jnp.exp(math.log(2.0) - 1.3862944 * jax.random.uniform(key_list[8], (CYCLES,), jnp.float32) ** level_of(key_list[8], (CYCLES,), ((0, 8),), -0.2, 0.2)), 0.5, 2.0),
    }


def reference(coeffs, legendre, alpha_table, beta_table, radial_weight, radius_index, orders, cycle_offset, cycle_weight):
    degree = jnp.arange(L, dtype=jnp.int32)
    live_mask = (degree[None, :] >= orders[:, None]).astype(jnp.float32)
    filters = jnp.stack([alpha_table[radius_index], beta_table[radius_index]])
    weight = radial_weight[radius_index]
    masked = coeffs * live_mask[None]
    block_size = math.gcd(M, 64)
    block_count = M // block_size
    coeff_blocks = jnp.transpose(masked.reshape(2, block_count, block_size, L), (1, 0, 2, 3))
    legendre_blocks = legendre.reshape(block_count, block_size, CYCLES, L)

    def synth(block_pair):
        coeff_block, legendre_block = block_pair
        filtered = (filters[:, None, :, None, :] * coeff_block[None, :, None, :, :]).astype(jnp.bfloat16)
        return jnp.einsum('fcrsl,sgl->fcrsg', filtered.astype(jnp.float32), legendre_block.astype(jnp.float32), precision=lax.Precision.HIGHEST)

    harmonic = lax.map(synth, (coeff_blocks, legendre_blocks))
    harmonic = jnp.transpose(harmonic, (1, 2, 3, 0, 4, 5)).reshape(2, 2, RADII, M, CYCLES)
    rotation = (orders[:, None] * cycle_offset[None, :]).astype(jnp.float32) * (math.pi / NPIX)
    cos_turn = jnp.cos(rotation).T
    sin_turn = jnp.sin(rotation).T
    real_part = jnp.swapaxes(harmonic[:, 0], -1, -2)
    imag_part = jnp.swapaxes(harmonic[:, 1], -1, -2)
    rotated_re = cos_turn * real_part - sin_turn * imag_part
    rotated_im = sin_turn * real_part + cos_turn * imag_part
    spectrum_shape = (2, RADII, CYCLES, NPIX // 2 + 1)
    spectrum_re = jnp.zeros(spectrum_shape, rotated_re.dtype).at[..., orders].set(rotated_re)
    spectrum_im = jnp.zeros(spectrum_shape, rotated_im.dtype).at[..., orders].set(rotated_im)
    pixels = jnp.fft.irfft(lax.complex(spectrum_re, spectrum_im), n=NPIX, axis=-1) * NPIX
    products = jnp.stack([pixels[1] * pixels[1], pixels[0] * pixels[1]])
    products = products - jnp.mean(products, axis=-1, keepdims=True)
    spectra = jnp.fft.rfft(products, axis=-1)[..., orders]
    cos_part = jnp.real(spectra)
    sin_part = jnp.imag(spectra)
    cycle_scale = cycle_weight[:, None]
    analysed_re = (cos_turn * cos_part + sin_turn * sin_part) * cycle_scale
    analysed_im = (cos_turn * sin_part - sin_turn * cos_part) * cycle_scale
    analysed = jnp.stack([analysed_re, analysed_im], axis=1).astype(jnp.bfloat16)
    analysed_blocks = jnp.moveaxis(analysed.reshape(2, 2, RADII, CYCLES, block_count, block_size), 4, 0)
    alpha_weighted = weight[:, None] * filters[0]
    beta_weighted = 2.0 * weight[:, None] * filters[1]

    def adjoint(block_pair):
        analysed_block, legendre_block = block_pair
        adjoint_terms = jnp.einsum('pcrgs,sgl->pcrsl', analysed_block.astype(jnp.float32), legendre_block.astype(jnp.float32), precision=lax.Precision.HIGHEST)
        return jnp.sum(adjoint_terms[0] * alpha_weighted[None, :, None, :] + adjoint_terms[1] * beta_weighted[None, :, None, :], axis=1)

    gradient = lax.map(adjoint, (analysed_blocks, legendre_blocks))
    gradient = jnp.transpose(gradient, (1, 0, 2, 3)).reshape(2, M, L)
    return gradient * live_mask[None]
```

```python
import functools
import math

import jax
import jax.numpy as jnp
import numpy as np
from jax import lax
from jax.experimental import pallas as pl
from jax.experimental.pallas import tpu as pltpu
from jax.sharding import PartitionSpec as P

NPIX = 4096
SIDE = 64
PADDED = 136
CHUNKS = 2
MIB = 1 << 20
F32 = jnp.float32
BF16 = jnp.bfloat16


def split_table(table):
    high = table.astype(jnp.bfloat16)
    low = (table - high.astype(np.float64)).astype(jnp.bfloat16)
    return high, low


@functools.lru_cache(maxsize=None)
def fourier_tables():
    degree_a = np.arange(32).reshape(4, 1, 8)
    part = np.arange(2).reshape(1, 2, 1)
    first = np.arange(SIDE)
    spin = np.arange(2).reshape(2, 1, 1, 1, 1, 1, 1)
    order = SIDE * degree_a[None] + np.arange(SIDE).reshape(SIDE, 1, 1, 1)
    angle = (
        (2 * first.reshape(1, 1, 1, SIDE, 1, 1, 1) + spin)
        * order.reshape(1, SIDE, 1, 1, 4, 1, 8)
        % (2 * NPIX)
        * (math.pi / NPIX)
    )
    cosine, sine = np.cos(angle), np.sin(angle)
    row_part = np.arange(2).reshape(1, 1, 2, 1, 1, 1, 1)
    col_part = part.reshape(1, 1, 1, 1, 1, 2, 1)
    same = (row_part == col_part).astype(np.float64)
    cross = np.where(row_part == 1, 1.0, -1.0) * (row_part != col_part)
    doubling = np.where(order == 0, 1.0, 2.0).reshape(1, SIDE, 1, 1, 4, 1, 8)
    spread = (doubling * (same * cosine + cross * sine)).reshape(2, SIDE, 2 * SIDE, SIDE)
    gather = (same * cosine + cross * sine).reshape(2, SIDE, 2 * SIDE, SIDE)
    gather = np.swapaxes(gather, 2, 3)
    spread_parts = np.concatenate(split_table(spread), axis=3)
    gather_parts = np.concatenate(split_table(gather), axis=2)
    square = first[:, None] * first[None, :] % SIDE * (2.0 * math.pi / SIDE)
    pixel = np.concatenate(split_table(np.concatenate([np.cos(square), -np.sin(square)], axis=1)), axis=0)
    back_high, back_low = split_table(np.concatenate([np.cos(square), -np.sin(square)], axis=0))
    back = np.concatenate([back_high, back_high, back_low], axis=1)
    return spread_parts, pixel, back, gather_parts


def two_parts(value):
    high = value.astype(BF16)
    low = (value - high.astype(F32)).astype(BF16)
    return high, low


def synth_kernel(
    jb_here,
    first_step,
    info_ref,
    row_ref,
    node_ref,
    coeffs_ref,
    alpha_ref,
    beta_ref,
    legendre_ref,
    keep_ref,
    send_ref,
    filter_scr,
    weight_scr,
    legendre_scr,
    terms_scr,
    sums_scr,
    sems,
):
    step = pl.program_id(0)
    row = row_ref[0]
    radii = node_ref.shape[0]
    degrees = coeffs_ref.shape[2]
    cycles = legendre_ref.shape[1]
    owners = cycles // 4
    slots = legendre_scr.shape[0]

    def fetch(which):
        slot = lax.rem(which, slots)

        def one(place, carry):
            source = info_ref[(first_step + which) * 32 + place] >> 12
            pltpu.make_async_copy(
                legendre_ref.at[source], legendre_scr.at[slot, place], sems.at[slot]
            ).start()
            return carry

        lax.fori_loop(0, 32, one, 0)

    @pl.when(step == 0)
    def _():
        for ahead in range(min(slots - 1, jb_here)):
            fetch(ahead)
        for radius in range(radii):
            node = node_ref[radius]
            filter_scr[pl.ds(radius, 1), :] = alpha_ref[pl.ds(node, 1), :]
            filter_scr[pl.ds(radii + radius, 1), :] = beta_ref[pl.ds(node, 1), :]
        high, low = two_parts(filter_scr[...].T)
        weight_scr[:, : 2 * radii] = high
        weight_scr[:, 2 * radii :] = low

    @pl.when(step + slots - 1 < jb_here)
    def _():
        fetch(step + slots - 1)

    slot = lax.rem(step, slots)
    pltpu.make_async_copy(
        legendre_ref.at[pl.ds(0, 32)], legendre_scr.at[slot], sems.at[slot]
    ).wait()
    degree = row * degrees + lax.broadcasted_iota(jnp.int32, (1, degrees), 1)
    for group in range(4):
        half = group % 2
        for place in range(8):
            entry = info_ref[(first_step + step) * 32 + group * 8 + place]
            source = entry >> 12
            live = degree >= (entry & 4095)
            values = legendre_scr[slot, group * 8 + place].astype(F32)
            for part in range(2):
                coeff = jnp.where(live, coeffs_ref[part, pl.ds(source, 1), :], 0.0)
                high, low = two_parts(values * coeff)
                start = (part * 8 + place) * cycles
                terms_scr[half, 0, start : start + cycles, :] = high
                terms_scr[half, 1, start : start + cycles, :] = low
        both = jnp.dot(terms_scr[half, 0], weight_scr[...], preferred_element_type=F32)
        rest = jnp.dot(
            terms_scr[half, 1], weight_scr[:, : 2 * radii], preferred_element_type=F32
        )
        sums_scr[half] = both[:, : 2 * radii] + both[:, 2 * radii :] + rest
        for owner in range(owners):
            for away in range(4):
                cycle = 4 * owner + (row ^ away)
                piece = sums_scr[half, pl.ds(cycle, 16, stride=cycles), :]
                target = send_ref if away % 2 else keep_ref
                target[away // 2, owner, 0, group * 16 : group * 16 + 16, :] = piece


def synth(chunk, chunks, info, row, radius_index, coeffs, alpha_table, beta_table, legendre):
    orders_here, cycles, degrees = legendre.shape
    jb_here = orders_here // 32 // chunks
    owners = cycles // 4
    radii = radius_index.shape[0]
    out = jax.ShapeDtypeStruct((2, owners, jb_here, 64, 2 * radii), F32)
    out_spec = pl.BlockSpec((2, owners, 1, 64, 2 * radii), lambda t, *_: (0, 0, t, 0, 0))
    whole = lambda shape: pl.BlockSpec(shape, lambda t, *_: (0,) * len(shape))
    slots = min(3, jb_here)
    return pl.pallas_call(
        functools.partial(synth_kernel, jb_here, chunk * jb_here),
        grid_spec=pltpu.PrefetchScalarGridSpec(
            num_scalar_prefetch=3,
            grid=(jb_here,),
            in_specs=[
                whole(coeffs.shape),
                whole(alpha_table.shape),
                whole(beta_table.shape),
                pl.BlockSpec(memory_space=pl.ANY),
            ],
            out_specs=[out_spec, out_spec],
            scratch_shapes=[
                pltpu.VMEM((2 * radii, degrees), F32),
                pltpu.VMEM((degrees, 4 * radii), BF16),
                pltpu.VMEM((slots, 32, cycles, degrees), BF16),
                pltpu.VMEM((2, 2, 16 * cycles, degrees), BF16),
                pltpu.VMEM((2, 16 * cycles, 2 * radii), F32),
                pltpu.SemaphoreType.DMA((slots,)),
            ],
        ),
        out_shape=[out, out],
        compiler_params=pltpu.CompilerParams(vmem_limit_bytes=48 * MIB),
        cost_estimate=pl.CostEstimate(
            flops=16 * jb_here * 4 * cycles * degrees * 2 * radii * 2 * 4,
            bytes_accessed=jb_here * (32 * cycles * degrees * 2 + 2 * 2 * owners * 64 * 2 * radii * 4),
            transcendentals=0,
        ),
        name="synth",
    )(info, row, radius_index, coeffs, alpha_table, beta_table, legendre)


def cycle_kernel(device_count, chunks, offset_ref, row_ref, weight_ref, *refs):
    pieces = refs[:chunks]
    place_ref, spread_ref, pixel_ref, back_ref, gather_ref = refs[chunks : chunks + 5]
    outs = refs[chunks + 5 : 2 * chunks + 5]
    middle_scr, product_scr, back_scr = refs[2 * chunks + 5 :]
    jb_here = pieces[0].shape[1]
    scale = weight_ref[row_ref[0]]
    lane = lax.broadcasted_iota(jnp.int32, (SIDE, 128), 1)

    for chunk in range(chunks):

        def spread_step(step, carry, chunk=chunk):
            block = chunk * jb_here + step
            for spot in range(device_count):
                picked = jnp.zeros((SIDE, 128), BF16)
                for peer in range(device_count):
                    picked = jnp.where(
                        place_ref[peer, block] == spot, pieces[chunk][peer, step], picked
                    )
                low_order = block * device_count + spot
                stage = jnp.dot(
                    spread_ref[0, low_order],
                    jnp.concatenate([picked, picked], axis=0),
                    preferred_element_type=F32,
                )
                middle_scr[pl.ds(low_order * PADDED, 128), :] = stage
            return carry

        lax.fori_loop(0, jb_here, spread_step, 0)

    def pixel_step(step, total):
        for inner in range(8):
            first = step * 8 + inner
            column = jnp.concatenate(
                [
                    middle_scr[pl.ds(first, SIDE, stride=PADDED), :],
                    middle_scr[pl.ds(first + SIDE, SIDE, stride=PADDED), :],
                ],
                axis=0,
            )
            high, low = two_parts(column)
            stage = jnp.dot(
                pixel_ref[...], jnp.concatenate([high, low], axis=1), preferred_element_type=F32
            )
            field = stage[:SIDE, :128] + stage[:SIDE, 128:] + stage[SIDE:, :128]
            other = pltpu.roll(field, 64, 1)
            product = other * jnp.where(lane < 64, other, field)
            product_scr[first] = product
            total = total + jnp.sum(product.reshape(8, 8, 128), axis=0)
        return total

    total = lax.fori_loop(0, SIDE // 8, pixel_step, jnp.zeros((8, 128), F32))
    mean = jnp.sum(total, axis=0, keepdims=True) * (1.0 / NPIX)

    def back_step(step, carry):
        for inner in range(8):
            first = step * 8 + inner
            high, low = two_parts(product_scr[first] - mean)
            back_scr[pl.ds(first * PADDED, 128), :] = jnp.dot(
                back_ref[...],
                jnp.concatenate([high, low, high], axis=0),
                preferred_element_type=F32,
            )
        return carry

    lax.fori_loop(0, SIDE // 8, back_step, 0)

    for chunk in range(chunks):

        def gather_step(step, carry, chunk=chunk):
            block = chunk * jb_here + step
            found = []
            for spot in range(device_count):
                low_order = block * device_count + spot
                column = jnp.concatenate(
                    [
                        back_scr[pl.ds(low_order, SIDE, stride=PADDED), :],
                        back_scr[pl.ds(low_order + SIDE, SIDE, stride=PADDED), :],
                    ],
                    axis=0,
                )
                high, low = two_parts(column)
                stage = jnp.dot(
                    gather_ref[0, low_order],
                    jnp.concatenate([high, low], axis=1),
                    preferred_element_type=F32,
                )
                value = stage[:SIDE, :128] + stage[:SIDE, 128:] + stage[SIDE:, :128]
                found.append((value * scale).astype(BF16))
            for peer in range(device_count):
                place = place_ref[peer, block]
                picked = found[0]
                for spot in range(1, device_count):
                    picked = jnp.where(place == spot, found[spot], picked)
                outs[chunk][peer, step] = picked
            return carry

        lax.fori_loop(0, jb_here, gather_step, 0)


def cycle_work(pieces, places, offset, row, cycle_weight):
    chunks = len(pieces)
    device_count, jb_here = pieces[0].shape[:2]
    spread, pixel, back, gather = [jnp.asarray(table) for table in fourier_tables()]
    whole = lambda shape: pl.BlockSpec(shape, lambda t, *_: (0,) * len(shape))
    chosen = pl.BlockSpec((1,) + spread.shape[1:], lambda t, off, row: (off[row[0]], 0, 0, 0))
    chosen_back = pl.BlockSpec((1,) + gather.shape[1:], lambda t, off, row: (off[row[0]], 0, 0, 0))
    return pl.pallas_call(
        functools.partial(cycle_kernel, device_count, chunks),
        grid_spec=pltpu.PrefetchScalarGridSpec(
            num_scalar_prefetch=2,
            grid=(1,),
            in_specs=[pl.BlockSpec(memory_space=pltpu.SMEM)]
            + [whole(piece.shape) for piece in pieces]
            + [whole(places.shape), chosen, whole(pixel.shape), whole(back.shape), chosen_back],
            out_specs=[whole(piece.shape) for piece in pieces],
            scratch_shapes=[
                pltpu.VMEM((SIDE * PADDED, 128), F32),
                pltpu.VMEM((SIDE, SIDE, 128), F32),
                pltpu.VMEM((SIDE * PADDED, 128), F32),
            ],
        ),
        out_shape=[jax.ShapeDtypeStruct(piece.shape, BF16) for piece in pieces],
        compiler_params=pltpu.CompilerParams(vmem_limit_bytes=48 * MIB),
        cost_estimate=pl.CostEstimate(
            flops=4 * SIDE * 128 * 256 * 256 * 2, bytes_accessed=8 * MIB, transcendentals=0
        ),
        name="cycle_work",
    )(offset, row, cycle_weight, *pieces, places, spread, pixel, back, gather)


def adjoint_kernel(
    jb_here,
    first_step,
    info_ref,
    row_ref,
    node_ref,
    radial_ref,
    alpha_ref,
    beta_ref,
    own_ref,
    core_ref,
    far_ref,
    corner_ref,
    legendre_ref,
    earlier_ref,
    out_ref,
    filter_scr,
    weight_scr,
    legendre_scr,
    rows_scr,
    terms_scr,
    sems,
):
    step = pl.program_id(0)
    row = row_ref[0]
    radii = node_ref.shape[0]
    degrees = out_ref.shape[2]
    cycles = legendre_ref.shape[1]
    owners = cycles // 4
    slots = legendre_scr.shape[0]

    def fetch(which):
        slot = lax.rem(which, slots)

        def one(place, carry):
            source = info_ref[(first_step + which) * 32 + place] >> 12
            pltpu.make_async_copy(
                legendre_ref.at[source], legendre_scr.at[slot, place], sems.at[slot]
            ).start()
            return carry

        lax.fori_loop(0, 32, one, 0)

    @pl.when(step == 0)
    def _():
        for ahead in range(min(slots - 1, jb_here)):
            fetch(ahead)
        if earlier_ref is not None:
            out_ref[...] = earlier_ref[...]
        for radius in range(radii):
            node = node_ref[radius]
            scale = radial_ref[node]
            filter_scr[pl.ds(radius, 1), :] = scale * alpha_ref[pl.ds(node, 1), :]
            filter_scr[pl.ds(radii + radius, 1), :] = (2.0 * scale) * beta_ref[pl.ds(node, 1), :]
        high, low = two_parts(filter_scr[...])
        weight_scr[: 2 * radii, :] = high
        weight_scr[2 * radii :, :] = low

    @pl.when(step + slots - 1 < jb_here)
    def _():
        fetch(step + slots - 1)

    slot = lax.rem(step, slots)
    pltpu.make_async_copy(
        legendre_ref.at[pl.ds(0, 32)], legendre_scr.at[slot], sems.at[slot]
    ).wait()
    degree = row * degrees + lax.broadcasted_iota(jnp.int32, (1, degrees), 1)
    sources = (own_ref, core_ref, far_ref, corner_ref)
    for group in range(4):
        half = group % 2
        for owner in range(owners):
            for away in range(4):
                cycle = 4 * owner + (row ^ away)
                piece = sources[away][owner, 0, group * 16 : group * 16 + 16, :]
                rows_scr[half, pl.ds(cycle, 16, stride=cycles), :] = piece.astype(F32)
        rows = rows_scr[half].astype(BF16)
        terms_scr[half] = jnp.dot(
            jnp.concatenate([rows, rows], axis=1), weight_scr[...], preferred_element_type=F32
        )
        for place in range(8):
            entry = info_ref[(first_step + step) * 32 + group * 8 + place]
            target = entry >> 12
            live = degree >= (entry & 4095)
            values = legendre_scr[slot, group * 8 + place].astype(F32)
            for part in range(2):
                start = (part * 8 + place) * cycles
                summed = jnp.sum(
                    terms_scr[half, start : start + cycles, :] * values, axis=0, keepdims=True
                )
                out_ref[part, pl.ds(target, 1), :] = jnp.where(live, summed, 0.0)


def adjoint(
    chunk, chunks, info, row, radius_index, radial_weight, alpha_table, beta_table, pieces, legendre, earlier
):
    orders_here, cycles, degrees = legendre.shape
    jb_here = orders_here // 32 // chunks
    owners = cycles // 4
    radii = radius_index.shape[0]
    out = jax.ShapeDtypeStruct((2, orders_here, degrees), F32)
    whole = lambda shape: pl.BlockSpec(shape, lambda t, *_: (0,) * len(shape))
    piece_spec = pl.BlockSpec((owners, 1, 64, 2 * radii), lambda t, *_: (0, t, 0, 0))
    slots = min(3, jb_here)
    body = functools.partial(adjoint_kernel, jb_here, chunk * jb_here)
    operands = [info, row, radius_index, radial_weight, alpha_table, beta_table, *pieces, legendre]
    in_specs = [
        pl.BlockSpec(memory_space=pltpu.SMEM),
        whole(alpha_table.shape),
        whole(beta_table.shape),
        piece_spec,
        piece_spec,
        piece_spec,
        piece_spec,
        pl.BlockSpec(memory_space=pl.ANY),
    ]
    if earlier is None:
        kernel = lambda *refs: body(*refs[:11], None, *refs[11:])
    else:
        kernel = body
        operands.append(earlier)
        in_specs.append(whole(earlier.shape))
    return pl.pallas_call(
        kernel,
        grid_spec=pltpu.PrefetchScalarGridSpec(
            num_scalar_prefetch=3,
            grid=(jb_here,),
            in_specs=in_specs,
            out_specs=whole(out.shape),
            scratch_shapes=[
                pltpu.VMEM((2 * radii, degrees), F32),
                pltpu.VMEM((4 * radii, degrees), BF16),
                pltpu.VMEM((slots, 32, cycles, degrees), BF16),
                pltpu.VMEM((2, 16 * cycles, 2 * radii), F32),
                pltpu.VMEM((2, 16 * cycles, degrees), F32),
                pltpu.SemaphoreType.DMA((slots,)),
            ],
        ),
        out_shape=out,
        compiler_params=pltpu.CompilerParams(vmem_limit_bytes=56 * MIB),
        cost_estimate=pl.CostEstimate(
            flops=16 * jb_here * 4 * cycles * degrees * 2 * radii * 2 * 2,
            bytes_accessed=jb_here * (32 * cycles * degrees * 2 + 4 * owners * 64 * 2 * radii * 2),
            transcendentals=0,
        ),
        name="adjoint",
    )(*operands)


def slot_tables(orders, device_count, ma_id):
    local_orders = orders.shape[0] // device_count
    blocks = local_orders // 32
    position = jnp.arange(local_orders, dtype=jnp.int32)
    wanted = blocks * (position % 32) + position // 32
    by_device = orders.reshape(device_count, local_orders)
    mine = lax.dynamic_slice_in_dim(orders, ma_id * local_orders, local_orders)
    info = jnp.sum(
        jnp.where(mine[None, :] // device_count == wanted[:, None], position[None, :] * 4096 + mine[None, :], 0),
        axis=1,
    )
    place = jnp.sum(
        jnp.where(
            by_device[:, None, :] // device_count == wanted[None, :, None],
            by_device[:, None, :] % device_count,
            0,
        ),
        axis=2,
    )
    place = place.reshape(device_count, blocks, 4, 1, 8, 1)
    place = jnp.broadcast_to(place, (device_count, blocks, 4, 2, 8, 128))
    return info, place.reshape(device_count, blocks, 64, 128).astype(BF16)


def body(
    coeffs,
    legendre,
    alpha_table,
    beta_table,
    radial_weight,
    radius_index,
    orders,
    cycle_offset,
    cycle_weight,
):
    row_id = lax.axis_index("row")
    ma_id = lax.axis_index("ma")
    device_count = lax.axis_size("ma")
    row_count = lax.axis_size("row")
    row = row_id.reshape(1).astype(jnp.int32)
    info, places = slot_tables(orders, device_count, ma_id)
    core_pairs = [(i, i ^ 1) for i in range(row_count)]
    far_pairs = [(i, i ^ 2) for i in range(row_count)]
    chunks = min(CHUNKS, coeffs.shape[1] // 32)
    arrived = []
    for chunk in range(chunks):
        keep, send = synth(
            chunk, chunks, info, row, radius_index, coeffs, alpha_table, beta_table, legendre
        )
        other = lax.ppermute(send, "row", core_pairs)
        outgoing = (keep[1] + other[1]).astype(BF16)
        incoming = lax.ppermute(outgoing, "row", far_pairs)
        summed = (keep[0] + other[0] + incoming.astype(F32)).astype(BF16)
        arrived.append(lax.all_to_all(summed, "ma", split_axis=0, concat_axis=0, tiled=True))
    analysed = cycle_work(arrived, places, cycle_offset, row, cycle_weight)
    gradient = None
    for chunk in range(chunks):
        own = lax.all_to_all(analysed[chunk], "ma", split_axis=0, concat_axis=0, tiled=True)
        far = lax.ppermute(own, "row", far_pairs)
        core = lax.ppermute(own, "row", core_pairs)
        corner = lax.ppermute(far, "row", core_pairs)
        gradient = adjoint(
            chunk,
            chunks,
            info,
            row,
            radius_index,
            radial_weight,
            alpha_table,
            beta_table,
            (own, core, far, corner),
            legendre,
            gradient,
        )
    return gradient


def solution(mesh):
    in_specs = (
        P(None, "ma", "row"),
        P("ma", None, "row"),
        P(None, "row"),
        P(None, "row"),
        P(),
        P(),
        P(),
        P("ma"),
        P("ma"),
    )
    out_specs = P(None, "ma", "row")
    return jax.shard_map(body, mesh=mesh, in_specs=in_specs, out_specs=out_specs, check_vma=False)
```

```python
import functools
import math

import jax
import jax.numpy as jnp
import numpy as np
from jax import lax
from jax.experimental import pallas as pl
from jax.experimental.pallas import tpu as pltpu
from jax.sharding import PartitionSpec as P

NPIX = 4096
SIDE = 64
PADDED = 136
CHUNKS = 4
MIB = 1 << 20
F32 = jnp.float32
BF16 = jnp.bfloat16


def split_table(table):
    high = table.astype(jnp.bfloat16)
    low = (table - high.astype(np.float64)).astype(jnp.bfloat16)
    return high, low


@functools.lru_cache(maxsize=None)
def fourier_tables():
    degree_a = np.arange(32).reshape(4, 1, 8)
    part = np.arange(2).reshape(1, 2, 1)
    first = np.arange(SIDE)
    spin = np.arange(2).reshape(2, 1, 1, 1, 1, 1, 1)
    order = SIDE * degree_a[None] + np.arange(SIDE).reshape(SIDE, 1, 1, 1)
    angle = (
        (2 * first.reshape(1, 1, 1, SIDE, 1, 1, 1) + spin)
        * order.reshape(1, SIDE, 1, 1, 4, 1, 8)
        % (2 * NPIX)
        * (math.pi / NPIX)
    )
    cosine, sine = np.cos(angle), np.sin(angle)
    row_part = np.arange(2).reshape(1, 1, 2, 1, 1, 1, 1)
    col_part = part.reshape(1, 1, 1, 1, 1, 2, 1)
    same = (row_part == col_part).astype(np.float64)
    cross = np.where(row_part == 1, 1.0, -1.0) * (row_part != col_part)
    doubling = np.where(order == 0, 1.0, 2.0).reshape(1, SIDE, 1, 1, 4, 1, 8)
    spread = (doubling * (same * cosine + cross * sine)).reshape(2, SIDE, 2 * SIDE, SIDE)
    gather = (same * cosine + cross * sine).reshape(2, SIDE, 2 * SIDE, SIDE)
    gather = np.swapaxes(gather, 2, 3)
    spread_parts = np.concatenate(split_table(spread), axis=3)
    gather_parts = np.concatenate(split_table(gather), axis=2)
    square = first[:, None] * first[None, :] % SIDE * (2.0 * math.pi / SIDE)
    pixel = np.concatenate(split_table(np.concatenate([np.cos(square), -np.sin(square)], axis=1)), axis=0)
    back_high, back_low = split_table(np.concatenate([np.cos(square), -np.sin(square)], axis=0))
    back = np.concatenate([back_high, back_high, back_low], axis=1)
    return spread_parts, pixel, back, gather_parts


def two_parts(value):
    high = value.astype(BF16)
    low = (value - high.astype(F32)).astype(BF16)
    return high, low


def whole(shape):
    return pl.BlockSpec(shape, lambda t, *_: (0,) * len(shape))


def anywhere():
    return pl.BlockSpec(memory_space=pl.ANY)


def fetch_group(first, legendre_ref, legendre_scr, sems, info_ref, step, group):
    for place in range(8):
        source = info_ref[(first + step) * 32 + group * 8 + place] >> 12
        pltpu.make_async_copy(
            legendre_ref.at[source], legendre_scr.at[step, group * 8 + place], sems.at[step, group]
        ).start()


def await_group(legendre_ref, legendre_scr, sems, step, group):
    pltpu.make_async_copy(
        legendre_ref.at[pl.ds(0, 8)],
        legendre_scr.at[step, pl.ds(group * 8, 8)],
        sems.at[step, group],
    ).wait()


def weights_kernel(
    node_ref, radial_ref, alpha_ref, beta_ref, synth_ref, adjoint_ref, filter_scr, weighted_scr
):
    radii = node_ref.shape[0]
    for radius in range(radii):
        node = node_ref[radius]
        scale = radial_ref[node]
        alpha = alpha_ref[pl.ds(node, 1), :]
        beta = beta_ref[pl.ds(node, 1), :]
        filter_scr[pl.ds(radius, 1), :] = alpha
        filter_scr[pl.ds(radii + radius, 1), :] = beta
        weighted_scr[pl.ds(radius, 1), :] = scale * alpha
        weighted_scr[pl.ds(radii + radius, 1), :] = (2.0 * scale) * beta
    high, low = two_parts(filter_scr[...].T)
    synth_ref[:, : 2 * radii] = high
    synth_ref[:, 2 * radii :] = low
    high, low = two_parts(weighted_scr[...])
    adjoint_ref[: 2 * radii, :] = high
    adjoint_ref[2 * radii :, :] = low


def filter_weights(radius_index, radial_weight, alpha_table, beta_table):
    radii = radius_index.shape[0]
    degrees = alpha_table.shape[1]
    return pl.pallas_call(
        weights_kernel,
        grid_spec=pltpu.PrefetchScalarGridSpec(
            num_scalar_prefetch=1,
            grid=(1,),
            in_specs=[
                pl.BlockSpec(memory_space=pltpu.SMEM),
                whole(alpha_table.shape),
                whole(beta_table.shape),
            ],
            out_specs=[whole((degrees, 4 * radii)), whole((4 * radii, degrees))],
            scratch_shapes=[pltpu.VMEM((2 * radii, degrees), F32)] * 2,
        ),
        out_shape=[
            jax.ShapeDtypeStruct((degrees, 4 * radii), BF16),
            jax.ShapeDtypeStruct((4 * radii, degrees), BF16),
        ],
        compiler_params=pltpu.CompilerParams(vmem_limit_bytes=16 * MIB),
        name="filter_weights",
    )(radius_index, radial_weight, alpha_table, beta_table)


def synth_kernel(
    jb_here,
    first,
    info_ref,
    where_ref,
    coeffs_ref,
    weight_ref,
    legendre_ref,
    order_ref,
    keep_ref,
    send_ref,
    coeffs_scr,
    weight_scr,
    legendre_scr,
    terms_even,
    terms_odd,
    sums_even,
    sums_odd,
    sems,
    input_sems,
):
    step = pl.program_id(0)
    row = where_ref[0]
    device = where_ref[1]
    degrees = coeffs_ref.shape[2]
    cycles = legendre_ref.shape[1]
    owners = cycles // 4
    lanes = weight_ref.shape[1] // 2
    coeffs_copy = pltpu.make_async_copy(coeffs_ref, coeffs_scr, input_sems.at[0])
    weight_copy = pltpu.make_async_copy(weight_ref, weight_scr, input_sems.at[1])

    @pl.when(step == 0)
    def _():
        coeffs_copy.start()
        for group in range(4):
            fetch_group(first, legendre_ref, legendre_scr, sems, info_ref, step, group)
        weight_copy.start()
        coeffs_copy.wait()
        weight_copy.wait()

    degree = row * degrees + lax.broadcasted_iota(jnp.int32, (1, degrees), 1)

    def build(group, terms):
        await_group(legendre_ref, legendre_scr, sems, step, group)
        for place in range(8):
            entry = info_ref[(first + step) * 32 + group * 8 + place]
            source = entry >> 12
            live = degree >= (entry & 4095)
            values = legendre_scr[step, group * 8 + place].astype(F32)
            for part in range(2):
                coeff = jnp.where(live, coeffs_scr[part, pl.ds(source, 1), :], 0.0)
                high, low = two_parts(values * coeff)
                start = (part * 8 + place) * cycles
                terms[0, start : start + cycles, :] = high
                terms[1, start : start + cycles, :] = low

    terms = (terms_even, terms_odd)
    sums = (sums_even, sums_odd)
    build(0, terms[0])
    for group in range(4):
        half = group % 2
        if group < 3:
            build(group + 1, terms[1 - half])

        @pl.when(step + 1 < jb_here)
        def _():
            fetch_group(first, legendre_ref, legendre_scr, sems, info_ref, step + 1, group)

        both = jnp.dot(terms[half][0], weight_scr[...], preferred_element_type=F32)
        rest = jnp.dot(terms[half][1], weight_scr[:, :lanes], preferred_element_type=F32)
        sums[half][...] = both[:, :lanes] + both[:, lanes:] + rest
        for distance in range(owners):
            owner = device ^ distance
            for away in range(4):
                cycle = 4 * owner + (row ^ away)
                piece = sums[half][pl.ds(cycle, 16, stride=cycles), :]
                target = send_ref if away % 2 else keep_ref
                target[away // 2, distance, 0, group * 16 : group * 16 + 16, :] = piece


def synth(chunk, chunks, info, where, coeffs, weight, legendre, order):
    orders_here, cycles, degrees = legendre.shape
    jb_here = orders_here // 32 // chunks
    owners = cycles // 4
    lanes = weight.shape[1] // 2
    out = jax.ShapeDtypeStruct((2, owners, jb_here, 64, lanes), F32)
    out_spec = pl.BlockSpec((2, owners, 1, 64, lanes), lambda t, *_: (0, 0, t, 0, 0))
    return pl.pallas_call(
        functools.partial(synth_kernel, jb_here, chunk * jb_here),
        grid_spec=pltpu.PrefetchScalarGridSpec(
            num_scalar_prefetch=2,
            grid=(jb_here,),
            in_specs=[anywhere(), anywhere(), anywhere(), anywhere()],
            out_specs=[out_spec, out_spec],
            scratch_shapes=[
                pltpu.VMEM(coeffs.shape, F32),
                pltpu.VMEM(weight.shape, BF16),
                pltpu.VMEM((jb_here, 32, cycles, degrees), BF16),
                pltpu.VMEM((2, 16 * cycles, degrees), BF16),
                pltpu.VMEM((2, 16 * cycles, degrees), BF16),
                pltpu.VMEM((16 * cycles, lanes), F32),
                pltpu.VMEM((16 * cycles, lanes), F32),
                pltpu.SemaphoreType.DMA((jb_here, 4)),
                pltpu.SemaphoreType.DMA((2,)),
            ],
        ),
        out_shape=[out, out],
        compiler_params=pltpu.CompilerParams(vmem_limit_bytes=48 * MIB),
        cost_estimate=pl.CostEstimate(
            flops=16 * jb_here * 4 * cycles * degrees * lanes * 2 * 4,
            bytes_accessed=jb_here * (32 * cycles * degrees * 2 + 2 * 2 * owners * 64 * lanes * 4),
            transcendentals=0,
        ),
        name="synth",
    )(info, where, coeffs, weight, legendre, order)


def core_sum_kernel(keep_ref, other_ref, order_ref, out_ref):
    out_ref[...] = (keep_ref[0] + other_ref[0]).astype(BF16)


def core_sum(keep, other, order):
    shape = keep.shape[1:]
    half = pl.BlockSpec((1,) + shape, lambda t: (1,) + (0,) * len(shape))
    return pl.pallas_call(
        core_sum_kernel,
        grid=(1,),
        in_specs=[half, half, anywhere()],
        out_specs=pl.BlockSpec(shape, lambda t: (0,) * len(shape)),
        out_shape=jax.ShapeDtypeStruct(shape, BF16),
        compiler_params=pltpu.CompilerParams(vmem_limit_bytes=16 * MIB),
        name="core_sum",
    )(keep, other, order)


def full_sum_kernel(keep_ref, other_ref, incoming_ref, order_ref, *outs):
    for distance, out in enumerate(outs):
        total = keep_ref[0, distance] + other_ref[0, distance]
        out[...] = (total + incoming_ref[distance].astype(F32)).astype(BF16)


def full_sum(keep, other, incoming, order):
    shape = keep.shape[1:]
    half = pl.BlockSpec((1,) + shape, lambda t: (0,) * (1 + len(shape)))
    piece = pl.BlockSpec(shape[1:], lambda t: (0,) * len(shape[1:]))
    return pl.pallas_call(
        full_sum_kernel,
        grid=(1,),
        in_specs=[half, half, pl.BlockSpec(shape, lambda t: (0,) * len(shape)), anywhere()],
        out_specs=[piece] * shape[0],
        out_shape=[jax.ShapeDtypeStruct(shape[1:], BF16)] * shape[0],
        compiler_params=pltpu.CompilerParams(vmem_limit_bytes=16 * MIB),
        name="full_sum",
    )(keep, other, incoming, order)


def join_kernel(order_ref, *refs):
    for distance, piece in enumerate(refs[:-1]):
        refs[-1][distance] = piece[...]


def join(pieces, order):
    shape = pieces[0].shape
    full = (len(pieces),) + shape
    piece = pl.BlockSpec(shape, lambda t: (0,) * len(shape))
    return pl.pallas_call(
        join_kernel,
        grid=(1,),
        in_specs=[anywhere()] + [piece] * len(pieces),
        out_specs=pl.BlockSpec(full, lambda t: (0,) * len(full)),
        out_shape=jax.ShapeDtypeStruct(full, BF16),
        compiler_params=pltpu.CompilerParams(vmem_limit_bytes=16 * MIB),
        name="join",
    )(order, *pieces)


def cycle_kernel(device_count, chunks, offset_ref, where_ref, weight_ref, *refs):
    pieces = [refs[c * device_count : (c + 1) * device_count] for c in range(chunks)]
    count = chunks * device_count
    place_ref, spread_ref, pixel_ref, back_ref, gather_ref = refs[count : count + 5]
    outs = refs[count + 5 : 2 * count + 5]
    outs = [outs[c * device_count : (c + 1) * device_count] for c in range(chunks)]
    spread_scr, gather_scr, middle_scr, product_scr, back_scr, sems = refs[2 * count + 5 :]
    jb_here = pieces[0][0].shape[0]
    turned = offset_ref[where_ref[0]]
    scale = weight_ref[where_ref[0]]
    lane = lax.broadcasted_iota(jnp.int32, (SIDE, 128), 1)

    def spread_copy(block):
        rows = pl.ds(block * device_count, device_count)
        return pltpu.make_async_copy(
            spread_ref.at[turned, rows], spread_scr.at[rows], sems.at[block]
        )

    gather_copy = pltpu.make_async_copy(
        gather_ref.at[turned], gather_scr, sems.at[chunks * jb_here]
    )
    for block in range(chunks * jb_here):
        spread_copy(block).start()
    gather_copy.start()

    for chunk in range(chunks):

        def spread_step(step, carry, chunk=chunk):
            block = chunk * jb_here + step
            spread_copy(block).wait()

            def one(spot):
                picked = jnp.zeros((SIDE, 128), BF16)
                for peer in range(device_count):
                    picked = jnp.where(
                        place_ref[peer, block] == lax.convert_element_type(spot, BF16),
                        pieces[chunk][peer][step],
                        picked,
                    )
                low_order = block * device_count + spot
                stage = jnp.dot(
                    spread_scr[low_order],
                    jnp.concatenate([picked, picked], axis=0),
                    preferred_element_type=F32,
                )
                middle_scr[pl.ds(low_order * PADDED, 128), :] = stage

            if device_count <= 8:
                for spot in range(device_count):
                    one(spot)
            else:
                lax.fori_loop(0, device_count, lambda s, x: (one(s), x)[1], 0)
            return carry

        lax.fori_loop(0, jb_here, spread_step, 0)

    def pixel_step(step, total):
        for inner in range(8):
            first = step * 8 + inner
            column = jnp.concatenate(
                [
                    middle_scr[pl.ds(first, SIDE, stride=PADDED), :],
                    middle_scr[pl.ds(first + SIDE, SIDE, stride=PADDED), :],
                ],
                axis=0,
            )
            high, low = two_parts(column)
            stage = jnp.dot(
                pixel_ref[...], jnp.concatenate([high, low], axis=1), preferred_element_type=F32
            )
            field = stage[:SIDE, :128] + stage[:SIDE, 128:] + stage[SIDE:, :128]
            other = pltpu.roll(field, 64, 1)
            product = other * jnp.where(lane < 64, other, field)
            product_scr[first] = product
            total = total + jnp.sum(product.reshape(8, 8, 128), axis=0)
        return total

    total = lax.fori_loop(0, SIDE // 8, pixel_step, jnp.zeros((8, 128), F32))
    mean = jnp.sum(total, axis=0, keepdims=True) * (1.0 / NPIX)

    def back_step(step, carry):
        for inner in range(8):
            first = step * 8 + inner
            high, low = two_parts(product_scr[first] - mean)
            back_scr[pl.ds(first * PADDED, 128), :] = jnp.dot(
                back_ref[...],
                jnp.concatenate([high, low, high], axis=0),
                preferred_element_type=F32,
            )
        return carry

    lax.fori_loop(0, SIDE // 8, back_step, 0)
    gather_copy.wait()

    for chunk in range(chunks):

        def gather_step(step, carry, chunk=chunk):
            block = chunk * jb_here + step

            def one(spot):
                low_order = block * device_count + spot
                column = jnp.concatenate(
                    [
                        back_scr[pl.ds(low_order, SIDE, stride=PADDED), :],
                        back_scr[pl.ds(low_order + SIDE, SIDE, stride=PADDED), :],
                    ],
                    axis=0,
                )
                high, low = two_parts(column)
                stage = jnp.dot(
                    gather_scr[low_order],
                    jnp.concatenate([high, low], axis=1),
                    preferred_element_type=F32,
                )
                value = stage[:SIDE, :128] + stage[:SIDE, 128:] + stage[SIDE:, :128]
                return (value * scale).astype(BF16)

            if device_count <= 8:
                found = [one(spot) for spot in range(device_count)]
                for peer in range(device_count):
                    place = place_ref[peer, block]
                    picked = found[0]
                    for spot in range(1, device_count):
                        picked = jnp.where(place == spot, found[spot], picked)
                    outs[chunk][peer][step] = picked
            else:

                def spot_step(spot, carry):
                    value = one(spot)
                    for peer in range(device_count):
                        outs[chunk][peer][step] = jnp.where(
                            place_ref[peer, block] == lax.convert_element_type(spot, BF16),
                            value,
                            outs[chunk][peer][step],
                        )
                    return carry

                lax.fori_loop(0, device_count, spot_step, 0)
            return carry

        lax.fori_loop(0, jb_here, gather_step, 0)


def cycle_work(pieces, places, offset, where, cycle_weight):
    chunks = len(pieces)
    device_count = len(pieces[0])
    shape = pieces[0][0].shape
    flat = [piece for chunk in pieces for piece in chunk]
    spread, pixel, back, gather = [jnp.asarray(table) for table in fourier_tables()]
    result = pl.pallas_call(
        functools.partial(cycle_kernel, device_count, chunks),
        grid_spec=pltpu.PrefetchScalarGridSpec(
            num_scalar_prefetch=2,
            grid=(1,),
            in_specs=[pl.BlockSpec(memory_space=pltpu.SMEM)]
            + [whole(shape)] * len(flat)
            + [whole(places.shape), anywhere(), whole(pixel.shape), whole(back.shape), anywhere()],
            out_specs=[whole(shape)] * len(flat),
            scratch_shapes=[
                pltpu.VMEM(spread.shape[1:], BF16),
                pltpu.VMEM(gather.shape[1:], BF16),
                pltpu.VMEM((SIDE * PADDED, 128), F32),
                pltpu.VMEM((SIDE, SIDE, 128), F32),
                pltpu.VMEM((SIDE * PADDED, 128), F32),
                pltpu.SemaphoreType.DMA((chunks * shape[0] + 1,)),
            ],
        ),
        out_shape=[jax.ShapeDtypeStruct(shape, BF16)] * len(flat),
        compiler_params=pltpu.CompilerParams(vmem_limit_bytes=48 * MIB),
        cost_estimate=pl.CostEstimate(
            flops=4 * SIDE * 128 * 256 * 256 * 2, bytes_accessed=8 * MIB, transcendentals=0
        ),
        name="cycle_work",
    )(offset, where, cycle_weight, *flat, places, spread, pixel, back, gather)
    return [result[c * device_count : (c + 1) * device_count] for c in range(chunks)]


def adjoint_kernel(jb_here, first, earlier_count, info_ref, where_ref, *refs):
    own_ref, core_ref, far_ref, corner_ref, weight_ref, legendre_ref, order_ref = refs[:7]
    earlier = refs[7 : 7 + earlier_count]
    out_ref = refs[7 + earlier_count]
    (
        weight_scr,
        legendre_scr,
        values_even,
        values_odd,
        terms_even,
        terms_odd,
        sorted_scr,
        sems,
        input_sem,
    ) = refs[8 + earlier_count :]
    step = pl.program_id(0)
    row = where_ref[0]
    device = where_ref[1]
    degrees = weight_ref.shape[1]
    cycles = legendre_ref.shape[1]
    owners = cycles // 4
    last = earlier_count > 0
    weight_copy = pltpu.make_async_copy(weight_ref, weight_scr, input_sem.at[0])

    def scatter(base, rows_ref, count):
        for place in range(count):
            target = info_ref[base + place] >> 12
            for part in range(2):
                out_ref[part, pl.ds(target, 1), :] = rows_ref[part, place : place + 1, :]

    @pl.when(step == 0)
    def _():
        weight_copy.start()
        for group in range(4):
            fetch_group(first, legendre_ref, legendre_scr, sems, info_ref, step, group)
        for index, rows_ref in enumerate(earlier):
            scatter(index * jb_here * 32, rows_ref, jb_here * 32)
        weight_copy.wait()

    degree = row * degrees + lax.broadcasted_iota(jnp.int32, (8, degrees), 1)
    sublane = lax.broadcasted_iota(jnp.int32, (8, degrees), 0)
    sources = (own_ref, core_ref, far_ref, corner_ref)
    values = (values_even, values_odd)
    terms = (terms_even, terms_odd)

    def multiply(group, out):
        rows = jnp.concatenate(
            [
                source[:, 0, group * 16 : group * 16 + 16, :].reshape(owners * 16, source.shape[3])
                for source in sources
            ],
            axis=0,
        )
        out[...] = jnp.dot(
            jnp.concatenate([rows, rows], axis=1), weight_scr[...], preferred_element_type=F32
        )

    def widen(group, out):
        await_group(legendre_ref, legendre_scr, sems, step, group)
        for place in range(8):
            start = place * (cycles + 8)
            wide = legendre_scr[step, group * 8 + place].astype(F32)
            for tile in range(degrees // 128):
                out[tile, start : start + cycles, :] = wide[:, tile * 128 : tile * 128 + 128]

    multiply(0, terms[0])
    widen(0, values[0])
    for group in range(4):
        half = group % 2
        if group < 3:
            multiply(group + 1, terms[1 - half])
            widen(group + 1, values[1 - half])

        @pl.when(step + 1 < jb_here)
        def _():
            fetch_group(first, legendre_ref, legendre_scr, sems, info_ref, step + 1, group)

        total = [jnp.zeros((8, degrees), F32), jnp.zeros((8, degrees), F32)]
        for away in range(4):
            for distance in range(owners):
                cycle = 4 * (device ^ distance) + (row ^ away)
                factor = jnp.concatenate(
                    [
                        values[half][tile, pl.ds(cycle, 8, stride=cycles + 8), :]
                        for tile in range(degrees // 128)
                    ],
                    axis=1,
                )
                start = (away * owners + distance) * 16
                for part in range(2):
                    at = start + part * 8
                    total[part] = total[part] + terms[half][at : at + 8, :] * factor
        lowest = jnp.zeros((8, degrees), jnp.int32)
        for place in range(8):
            entry = info_ref[(first + step) * 32 + group * 8 + place]
            lowest = jnp.where(sublane == place, entry & 4095, lowest)
        for part in range(2):
            masked = jnp.where(degree >= lowest, total[part], 0.0)
            if last:
                sorted_scr[part, group * 8 : group * 8 + 8, :] = masked
            else:
                out_ref[part, group * 8 : group * 8 + 8, :] = masked
    if last:
        scatter((first + step) * 32, sorted_scr, 32)


def adjoint(chunk, chunks, info, where, weight, pieces, legendre, earlier, order):
    orders_here, cycles, degrees = legendre.shape
    jb_here = orders_here // 32 // chunks
    owners = cycles // 4
    lanes = weight.shape[0] // 2
    piece_spec = pl.BlockSpec((owners, 1, 64, lanes), lambda t, *_: (0, t, 0, 0))
    if earlier:
        out = jax.ShapeDtypeStruct((2, orders_here, degrees), F32)
        out_spec = whole(out.shape)
    else:
        out = jax.ShapeDtypeStruct((2, 32 * jb_here, degrees), F32)
        out_spec = pl.BlockSpec((2, 32, degrees), lambda t, *_: (0, t, 0))
    return pl.pallas_call(
        functools.partial(adjoint_kernel, jb_here, chunk * jb_here, len(earlier)),
        grid_spec=pltpu.PrefetchScalarGridSpec(
            num_scalar_prefetch=2,
            grid=(jb_here,),
            in_specs=[piece_spec] * 4
            + [anywhere()] * 3
            + [whole((2, 32 * jb_here, degrees))] * len(earlier),
            out_specs=out_spec,
            scratch_shapes=[
                pltpu.VMEM(weight.shape, BF16),
                pltpu.VMEM((jb_here, 32, cycles, degrees), BF16),
                pltpu.VMEM((degrees // 128, 8 * (cycles + 8), 128), F32),
                pltpu.VMEM((degrees // 128, 8 * (cycles + 8), 128), F32),
                pltpu.VMEM((16 * cycles, degrees), F32),
                pltpu.VMEM((16 * cycles, degrees), F32),
                pltpu.VMEM((2, 32, degrees), F32),
                pltpu.SemaphoreType.DMA((jb_here, 4)),
                pltpu.SemaphoreType.DMA((1,)),
            ],
        ),
        out_shape=out,
        compiler_params=pltpu.CompilerParams(vmem_limit_bytes=48 * MIB),
        cost_estimate=pl.CostEstimate(
            flops=16 * jb_here * 4 * cycles * degrees * lanes * 2 * 2,
            bytes_accessed=jb_here * (32 * cycles * degrees * 2 + 4 * owners * 64 * lanes * 2),
            transcendentals=0,
        ),
        name="adjoint",
    )(info, where, *pieces, weight, legendre, order, *earlier)


def slot_tables(orders, device_count, ma_id):
    local_orders = orders.shape[0] // device_count
    blocks = local_orders // 32
    position = jnp.arange(local_orders, dtype=jnp.int32)
    wanted = blocks * (position % 32) + position // 32
    by_device = orders.reshape(device_count, local_orders)
    by_device = by_device[jnp.arange(device_count, dtype=jnp.int32) ^ ma_id]
    mine = lax.dynamic_slice_in_dim(orders, ma_id * local_orders, local_orders)
    info = jnp.sum(
        jnp.where(mine[None, :] // device_count == wanted[:, None], position[None, :] * 4096 + mine[None, :], 0),
        axis=1,
    )
    place = jnp.sum(
        jnp.where(
            by_device[:, None, :] // device_count == wanted[None, :, None],
            by_device[:, None, :] % device_count,
            0,
        ),
        axis=2,
    )
    place = place.reshape(device_count, blocks, 4, 1, 8, 1)
    place = jnp.broadcast_to(place, (device_count, blocks, 4, 2, 8, 128))
    return info, place.reshape(device_count, blocks, 64, 128).astype(BF16)


def body(
    coeffs,
    legendre,
    alpha_table,
    beta_table,
    radial_weight,
    radius_index,
    orders,
    cycle_offset,
    cycle_weight,
):
    row_id = lax.axis_index("row")
    ma_id = lax.axis_index("ma")
    device_count = lax.axis_size("ma")
    row_count = lax.axis_size("row")
    where = jnp.stack([row_id, ma_id]).astype(jnp.int32)
    info, places = slot_tables(orders, device_count, ma_id)
    synth_weight, adjoint_weight = filter_weights(
        radius_index, radial_weight, alpha_table, beta_table
    )
    core_pairs = [(i, i ^ 1) for i in range(row_count)]
    far_pairs = [(i, i ^ 2) for i in range(row_count)]
    chunks = min(CHUNKS, coeffs.shape[1] // 32)

    def exchange(pieces):
        return [pieces[0]] + [
            lax.ppermute(pieces[d], "ma", [(i, i ^ d) for i in range(device_count)])
            for d in range(1, device_count)
        ]

    kept, others, outgoing = [], [], []
    for chunk in range(chunks):
        order = outgoing[chunk - 2] if chunk >= 2 else info
        keep, send = synth(chunk, chunks, info, where, coeffs, synth_weight, legendre, order)
        kept.append(keep)
        others.append(lax.ppermute(send, "row", core_pairs))
        if chunk >= 1:
            outgoing.append(core_sum(kept[chunk - 1], others[chunk - 1], keep))
    outgoing.append(core_sum(kept[-1], others[-1], info))
    arrived = []
    for chunk in range(chunks):
        incoming = lax.ppermute(outgoing[chunk], "row", far_pairs)
        order = kept[-1] if chunk == 0 else outgoing[-1]
        arrived.append(exchange(full_sum(kept[chunk], others[chunk], incoming, order)))
    analysed = cycle_work(arrived, places, cycle_offset, where, cycle_weight)
    owned = []
    returned = [exchange(pieces) for pieces in analysed]
    for chunk in range(chunks):
        owned.append(join(returned[chunk], info if chunk == 0 else owned[-1]))
    gradient = []
    for chunk in range(chunks):
        own = owned[chunk]
        far = lax.ppermute(own, "row", far_pairs)
        core = lax.ppermute(own, "row", core_pairs)
        corner = lax.ppermute(far, "row", core_pairs)
        last = chunk == chunks - 1
        result = adjoint(
            chunk,
            chunks,
            info,
            where,
            adjoint_weight,
            (own, core, far, corner),
            legendre,
            gradient if last else [],
            owned[min(chunk + 2, chunks - 1)],
        )
        gradient.append(result)
    return gradient[-1]


def solution(mesh):
    in_specs = (
        P(None, "ma", "row"),
        P("ma", None, "row"),
        P(None, "row"),
        P(None, "row"),
        P(),
        P(),
        P(),
        P("ma"),
        P("ma"),
    )
    out_specs = P(None, "ma", "row")
    return jax.shard_map(body, mesh=mesh, in_specs=in_specs, out_specs=out_specs, check_vma=False)
```

```python
import functools
import math

import jax
import jax.numpy as jnp
import numpy as np
from jax import lax
from jax.experimental import pallas as pl
from jax.experimental.pallas import tpu as pltpu
from jax.sharding import PartitionSpec as P

NPIX = 4096
SIDE = 64
PADDED = 136
CHUNKS = 4
GROUPS = 2
MIB = 1 << 20
F32 = jnp.float32
BF16 = jnp.bfloat16


def split_table(table):
    high = table.astype(jnp.bfloat16)
    low = (table - high.astype(np.float64)).astype(jnp.bfloat16)
    return high, low


@functools.lru_cache(maxsize=None)
def fourier_tables():
    degree_a = np.arange(32).reshape(4, 1, 8)
    part = np.arange(2).reshape(1, 2, 1)
    first = np.arange(SIDE)
    spin = np.arange(2).reshape(2, 1, 1, 1, 1, 1, 1)
    order = SIDE * degree_a[None] + np.arange(SIDE).reshape(SIDE, 1, 1, 1)
    angle = (
        (2 * first.reshape(1, 1, 1, SIDE, 1, 1, 1) + spin)
        * order.reshape(1, SIDE, 1, 1, 4, 1, 8)
        % (2 * NPIX)
        * (math.pi / NPIX)
    )
    cosine, sine = np.cos(angle), np.sin(angle)
    row_part = np.arange(2).reshape(1, 1, 2, 1, 1, 1, 1)
    col_part = part.reshape(1, 1, 1, 1, 1, 2, 1)
    same = (row_part == col_part).astype(np.float64)
    cross = np.where(row_part == 1, 1.0, -1.0) * (row_part != col_part)
    doubling = np.where(order == 0, 1.0, 2.0).reshape(1, SIDE, 1, 1, 4, 1, 8)
    spread = (doubling * (same * cosine + cross * sine)).reshape(2, SIDE, 2 * SIDE, SIDE)
    gather = (same * cosine + cross * sine).reshape(2, SIDE, 2 * SIDE, SIDE)
    gather = np.swapaxes(gather, 2, 3)
    spread_parts = np.concatenate(split_table(spread), axis=3)
    gather_parts = np.concatenate(split_table(gather), axis=2)
    square = first[:, None] * first[None, :] % SIDE * (2.0 * math.pi / SIDE)
    pixel = np.concatenate(split_table(np.concatenate([np.cos(square), -np.sin(square)], axis=1)), axis=0)
    back_high, back_low = split_table(np.concatenate([np.cos(square), -np.sin(square)], axis=0))
    back = np.concatenate([back_high, back_high, back_low, back_low], axis=1)
    return spread_parts, pixel, back, gather_parts


def two_parts(value):
    high = value.astype(BF16)
    low = (value - high.astype(F32)).astype(BF16)
    return high, low


def whole(shape):
    return pl.BlockSpec(shape, lambda t, *_: (0,) * len(shape))


def anywhere():
    return pl.BlockSpec(memory_space=pl.ANY)


def fetch_all(first, jb_here, legendre_ref, legendre_scr, sems, info_ref):
    def fetch_group(index, carry):
        step = index // 4
        group = lax.rem(index, 4)
        for place in range(8):
            source = info_ref[first * 32 + index * 8 + place] >> 12
            pltpu.make_async_copy(
                legendre_ref.at[source],
                legendre_scr.at[step, group * 8 + place],
                sems.at[step, group],
            ).start()
        return carry

    lax.fori_loop(0, 4 * jb_here, fetch_group, 0)


def await_group(legendre_ref, legendre_scr, sems, step, group):
    pltpu.make_async_copy(
        legendre_ref.at[pl.ds(0, 8)],
        legendre_scr.at[step, pl.ds(group * 8, 8)],
        sems.at[step, group],
    ).wait()


def weights_kernel(node_ref, radial_ref, alpha_ref, beta_ref, filter_ref, adjoint_ref, weighted_scr):
    radii = node_ref.shape[0]
    for radius in range(radii):
        node = node_ref[radius]
        scale = radial_ref[node]
        alpha = alpha_ref[pl.ds(node, 1), :]
        beta = beta_ref[pl.ds(node, 1), :]
        filter_ref[pl.ds(radius, 1), :] = alpha
        filter_ref[pl.ds(radii + radius, 1), :] = beta
        weighted_scr[pl.ds(radius, 1), :] = scale * alpha
        weighted_scr[pl.ds(radii + radius, 1), :] = (2.0 * scale) * beta
    high, low = two_parts(weighted_scr[...])
    adjoint_ref[: 2 * radii, :] = high
    adjoint_ref[2 * radii :, :] = low


def filter_weights(radius_index, radial_weight, alpha_table, beta_table):
    radii = radius_index.shape[0]
    degrees = alpha_table.shape[1]
    return pl.pallas_call(
        weights_kernel,
        grid_spec=pltpu.PrefetchScalarGridSpec(
            num_scalar_prefetch=1,
            grid=(1,),
            in_specs=[
                pl.BlockSpec(memory_space=pltpu.SMEM),
                whole(alpha_table.shape),
                whole(beta_table.shape),
            ],
            out_specs=[whole((2 * radii, degrees)), whole((4 * radii, degrees))],
            scratch_shapes=[pltpu.VMEM((2 * radii, degrees), F32)],
        ),
        out_shape=[
            jax.ShapeDtypeStruct((2 * radii, degrees), F32),
            jax.ShapeDtypeStruct((4 * radii, degrees), BF16),
        ],
        compiler_params=pltpu.CompilerParams(vmem_limit_bytes=16 * MIB),
        name="filter_weights",
    )(radius_index, radial_weight, alpha_table, beta_table)


def synth_kernel(
    jb_here,
    first,
    info_ref,
    where_ref,
    coeffs_ref,
    filter_ref,
    legendre_ref,
    *refs,
):
    (
        keep_ref,
        send_ref,
        coeffs_scr,
        filter_scr,
        legendre_scr,
        sums_scr,
        sems,
        input_sems,
    ) = refs[-8:]
    step = pl.program_id(0)
    row = where_ref[0]
    degrees = coeffs_ref.shape[2]
    cycles = legendre_ref.shape[1]
    owners = cycles // 4
    lanes = filter_ref.shape[0]
    coeffs_copy = pltpu.make_async_copy(coeffs_ref, coeffs_scr, input_sems.at[0])
    filter_copy = pltpu.make_async_copy(filter_ref, filter_scr, input_sems.at[1])

    @pl.when(step == 0)
    def _():
        filter_copy.start()
        coeffs_copy.start()
        fetch_all(first, jb_here, legendre_ref, legendre_scr, sems, info_ref)
        filter_copy.wait()
        coeffs_copy.wait()

    degree = row * degrees + lax.broadcasted_iota(jnp.int32, (1, degrees), 1)

    def one_group(group, carry):
        await_group(legendre_ref, legendre_scr, sems, step, group)
        for place in range(8):
            entry = info_ref[(first + step) * 32 + group * 8 + place]
            source = entry >> 12
            live = degree >= (entry & 4095)
            filtered = jnp.concatenate(
                [
                    (
                        filter_scr[...]
                        * jnp.where(live, coeffs_scr[part, pl.ds(source, 1), :], 0.0)
                    ).astype(BF16)
                    for part in range(2)
                ],
                axis=0,
            )
            summed = lax.dot_general(
                legendre_scr[step, group * 8 + place],
                filtered,
                (((1,), (1,)), ((), ())),
                preferred_element_type=F32,
            )
            for part in range(2):
                start = (part * 8 + place) * cycles
                sums_scr[start : start + cycles, :] = summed[:, part * lanes : (part + 1) * lanes]
        for owner in range(owners):
            for away in range(4):
                cycle = 4 * owner + (row ^ away)
                piece = sums_scr[pl.ds(cycle, 16, stride=cycles), :]
                target = send_ref if away % 2 else keep_ref
                target[away // 2, owner, 0, pl.ds(pl.multiple_of(group * 16, 16), 16), :] = (
                    piece.astype(target.dtype)
                )
        return carry

    lax.fori_loop(0, 4, one_group, 0)


def synth(chunk, chunks, info, where, coeffs, filters, legendre, order):
    orders_here, cycles, degrees = legendre.shape
    jb_here = orders_here // 32 // chunks
    owners = cycles // 4
    lanes = filters.shape[0]
    shape = (2, owners, jb_here, 64, lanes)
    out_spec = pl.BlockSpec((2, owners, 1, 64, lanes), lambda t, *_: (0, 0, t, 0, 0))
    return pl.pallas_call(
        functools.partial(synth_kernel, jb_here, chunk * jb_here),
        grid_spec=pltpu.PrefetchScalarGridSpec(
            num_scalar_prefetch=2,
            grid=(jb_here,),
            in_specs=[anywhere()] * (3 + len(order)),
            out_specs=[out_spec, out_spec],
            scratch_shapes=[
                pltpu.VMEM(coeffs.shape, F32),
                pltpu.VMEM(filters.shape, F32),
                pltpu.VMEM((jb_here, 32, cycles, degrees), BF16),
                pltpu.VMEM((16 * cycles, lanes), F32),
                pltpu.SemaphoreType.DMA((jb_here, 4)),
                pltpu.SemaphoreType.DMA((2,)),
            ],
        ),
        out_shape=[jax.ShapeDtypeStruct(shape, F32), jax.ShapeDtypeStruct(shape, BF16)],
        compiler_params=pltpu.CompilerParams(vmem_limit_bytes=32 * MIB),
        cost_estimate=pl.CostEstimate(
            flops=16 * jb_here * 4 * cycles * degrees * lanes * 2 * 4,
            bytes_accessed=jb_here * (32 * cycles * degrees * 2 + 2 * 2 * owners * 64 * lanes * 3),
            transcendentals=0,
        ),
        name="synth",
    )(info, where, coeffs, filters, legendre, *order)


def core_sum_kernel(keep_ref, other_ref, order_ref, out_ref):
    out_ref[...] = (keep_ref[0] + other_ref[0].astype(F32)).astype(BF16)


def core_sum(keep, other, order):
    shape = keep.shape[1:]
    half = pl.BlockSpec((1,) + shape, lambda t: (1,) + (0,) * len(shape))
    return pl.pallas_call(
        core_sum_kernel,
        grid=(1,),
        in_specs=[half, half, anywhere()],
        out_specs=pl.BlockSpec(shape, lambda t: (0,) * len(shape)),
        out_shape=jax.ShapeDtypeStruct(shape, BF16),
        compiler_params=pltpu.CompilerParams(vmem_limit_bytes=16 * MIB),
        cost_estimate=pl.CostEstimate(flops=10**10, bytes_accessed=MIB, transcendentals=0),
        name="core_sum",
    )(keep, other, order)


def full_sum_kernel(order_ref, *refs):
    out_ref = refs[-1]
    start = 0
    for index in range(0, len(refs) - 1, 3):
        keep_ref, other_ref, incoming_ref = refs[index : index + 3]
        count = incoming_ref.shape[1]
        total = keep_ref[0] + other_ref[0].astype(F32) + incoming_ref[...].astype(F32)
        out_ref[:, start : start + count] = total.astype(BF16)
        start += count


def full_sum(chunks, order):
    operands, specs, count = [], [anywhere()], 0
    for keep, other, incoming in chunks:
        shape = incoming.shape
        half = pl.BlockSpec((1,) + shape, lambda t: (0, 0, 0, 0, 0))
        operands += [keep, other, incoming]
        specs += [half, half, pl.BlockSpec(shape, lambda t: (0, 0, 0, 0))]
        count += shape[1]
    full = (shape[0], count) + shape[2:]
    return pl.pallas_call(
        full_sum_kernel,
        grid=(1,),
        in_specs=specs,
        out_specs=pl.BlockSpec(full, lambda t: (0, 0, 0, 0)),
        out_shape=jax.ShapeDtypeStruct(full, BF16),
        compiler_params=pltpu.CompilerParams(vmem_limit_bytes=24 * MIB),
        cost_estimate=pl.CostEstimate(flops=10**10, bytes_accessed=MIB, transcendentals=0),
        name="full_sum",
    )(order, *operands)


def cycle_kernel(device_count, chunks, offset_ref, where_ref, weight_ref, *refs):
    pieces = refs[:chunks]
    count = chunks
    place_ref, spread_ref, pixel_ref, back_ref, gather_ref = refs[count : count + 5]
    outs = refs[count + 5 : 2 * count + 5]
    spread_scr, gather_scr, middle_scr, product_scr, back_scr, sems = refs[2 * count + 5 :]
    jb_here = pieces[0].shape[1]
    turned = offset_ref[where_ref[0]]
    scale = weight_ref[where_ref[0]]
    lane = lax.broadcasted_iota(jnp.int32, (SIDE, 128), 1)

    def spread_copy(block):
        rows = pl.ds(block * device_count, device_count)
        return pltpu.make_async_copy(
            spread_ref.at[turned, rows], spread_scr.at[rows], sems.at[block]
        )

    gather_copy = pltpu.make_async_copy(
        gather_ref.at[turned], gather_scr, sems.at[chunks * jb_here]
    )
    for block in range(chunks * jb_here):
        spread_copy(block).start()
    gather_copy.start()

    for chunk in range(chunks):

        def spread_step(step, carry, chunk=chunk):
            block = chunk * jb_here + step
            spread_copy(block).wait()

            def one(spot):
                picked = jnp.zeros((SIDE, 128), BF16)
                for peer in range(device_count):
                    picked = jnp.where(
                        place_ref[peer, block] == lax.convert_element_type(spot, BF16),
                        pieces[chunk][peer, step],
                        picked,
                    )
                low_order = block * device_count + spot
                stage = jnp.dot(
                    spread_scr[low_order],
                    jnp.concatenate([picked, picked], axis=0),
                    preferred_element_type=F32,
                )
                middle_scr[pl.ds(low_order * PADDED, 128), :] = stage

            if device_count <= 8:
                for spot in range(device_count):
                    one(spot)
            else:
                lax.fori_loop(0, device_count, lambda s, x: (one(s), x)[1], 0)
            return carry

        lax.fori_loop(0, jb_here, spread_step, 0)

    def pixel_step(step, total):
        for inner in range(8):
            first = step * 8 + inner
            column = jnp.concatenate(
                [
                    middle_scr[pl.ds(first, SIDE, stride=PADDED), :],
                    middle_scr[pl.ds(first + SIDE, SIDE, stride=PADDED), :],
                ],
                axis=0,
            )
            high, low = two_parts(column)
            stage = jnp.dot(
                pixel_ref[...], jnp.concatenate([high, low], axis=1), preferred_element_type=F32
            )
            field = stage[:SIDE, :128] + stage[:SIDE, 128:] + stage[SIDE:, :128]
            other = pltpu.roll(field, 64, 1)
            product = other * jnp.where(lane < 64, other, field)
            product_scr[first] = product
            total = total + jnp.sum(product.reshape(8, 8, 128), axis=0)
        return total

    total = lax.fori_loop(0, SIDE // 8, pixel_step, jnp.zeros((8, 128), F32))
    mean = jnp.sum(total, axis=0, keepdims=True) * (1.0 / NPIX)

    def back_step(step, carry):
        for inner in range(8):
            first = step * 8 + inner
            high, low = two_parts(product_scr[first] - mean)
            back_scr[pl.ds(first * PADDED, 128), :] = jnp.dot(
                back_ref[...],
                jnp.concatenate([high, low, high, low], axis=0),
                preferred_element_type=F32,
            )
        return carry

    lax.fori_loop(0, SIDE // 8, back_step, 0)
    gather_copy.wait()

    for chunk in range(chunks):

        def gather_step(step, carry, chunk=chunk):
            block = chunk * jb_here + step

            def one(spot):
                low_order = block * device_count + spot
                column = jnp.concatenate(
                    [
                        back_scr[pl.ds(low_order, SIDE, stride=PADDED), :],
                        back_scr[pl.ds(low_order + SIDE, SIDE, stride=PADDED), :],
                    ],
                    axis=0,
                )
                high, low = two_parts(column)
                stage = jnp.dot(
                    gather_scr[low_order],
                    jnp.concatenate([high, low], axis=1),
                    preferred_element_type=F32,
                )
                value = stage[:SIDE, :128] + stage[:SIDE, 128:] + stage[SIDE:, :128]
                return (value * scale).astype(BF16)

            if device_count <= 8:
                found = [one(spot) for spot in range(device_count)]
                for peer in range(device_count):
                    place = place_ref[peer, block]
                    picked = found[0]
                    for spot in range(1, device_count):
                        picked = jnp.where(place == spot, found[spot], picked)
                    outs[chunk][peer, step] = picked
            else:

                def spot_step(spot, carry):
                    value = one(spot)
                    for peer in range(device_count):
                        outs[chunk][peer, step] = jnp.where(
                            place_ref[peer, block] == lax.convert_element_type(spot, BF16),
                            value,
                            outs[chunk][peer, step],
                        )
                    return carry

                lax.fori_loop(0, device_count, spot_step, 0)
            return carry

        lax.fori_loop(0, jb_here, gather_step, 0)


def cycle_work(pieces, places, offset, where, cycle_weight):
    chunks = len(pieces)
    shape = pieces[0].shape
    device_count = shape[0]
    flat = list(pieces)
    spread, pixel, back, gather = [jnp.asarray(table) for table in fourier_tables()]
    return pl.pallas_call(
        functools.partial(cycle_kernel, device_count, chunks),
        grid_spec=pltpu.PrefetchScalarGridSpec(
            num_scalar_prefetch=2,
            grid=(1,),
            in_specs=[pl.BlockSpec(memory_space=pltpu.SMEM)]
            + [whole(shape)] * len(flat)
            + [whole(places.shape), anywhere(), whole(pixel.shape), whole(back.shape), anywhere()],
            out_specs=[whole(shape)] * len(flat),
            scratch_shapes=[
                pltpu.VMEM(spread.shape[1:], BF16),
                pltpu.VMEM(gather.shape[1:], BF16),
                pltpu.VMEM((SIDE * PADDED, 128), F32),
                pltpu.VMEM((SIDE, SIDE, 128), F32),
                pltpu.VMEM((SIDE * PADDED, 128), F32),
                pltpu.SemaphoreType.DMA((chunks * shape[1] + 1,)),
            ],
        ),
        out_shape=[jax.ShapeDtypeStruct(shape, BF16)] * len(flat),
        compiler_params=pltpu.CompilerParams(vmem_limit_bytes=48 * MIB),
        cost_estimate=pl.CostEstimate(
            flops=4 * SIDE * 128 * 256 * 256 * 2, bytes_accessed=8 * MIB, transcendentals=0
        ),
        name="cycle_work",
    )(offset, where, cycle_weight, *flat, places, spread, pixel, back, gather)


def adjoint_kernel(jb_here, first, earlier_count, info_ref, where_ref, *refs):
    own_ref, core_ref, far_ref, corner_ref, weight_ref, legendre_ref, order_ref = refs[:7]
    earlier = refs[7 : 7 + earlier_count]
    out_ref = refs[7 + earlier_count]
    (
        weight_scr,
        legendre_scr,
        values_even,
        values_odd,
        terms_even,
        terms_odd,
        sorted_scr,
        sems,
        input_sem,
    ) = refs[8 + earlier_count :]
    step = pl.program_id(0)
    row = where_ref[0]
    degrees = weight_ref.shape[1]
    cycles = legendre_ref.shape[1]
    owners = cycles // 4
    last = earlier_count > 0
    weight_copy = pltpu.make_async_copy(weight_ref, weight_scr, input_sem.at[0])

    def scatter(base, rows_ref, count):
        def eight(block, carry):
            start = pl.multiple_of(block * 8, 8)
            rows = [rows_ref[part, pl.ds(start, 8), :] for part in range(2)]
            for place in range(8):
                target = info_ref[base + start + place] >> 12
                for part in range(2):
                    out_ref[part, pl.ds(target, 1), :] = rows[part][place : place + 1, :]
            return carry

        lax.fori_loop(0, count // 8, eight, 0)

    @pl.when(step == 0)
    def _():
        weight_copy.start()
        fetch_all(first, jb_here, legendre_ref, legendre_scr, sems, info_ref)
        for index, rows_ref in enumerate(earlier):
            scatter(index * jb_here * 32, rows_ref, jb_here * 32)
        weight_copy.wait()

    degree = row * degrees + lax.broadcasted_iota(jnp.int32, (8, degrees), 1)
    sublane = lax.broadcasted_iota(jnp.int32, (8, degrees), 0)
    sources = (own_ref, core_ref, far_ref, corner_ref)
    values = (values_even, values_odd)
    terms = (terms_even, terms_odd)

    def multiply(group, out):
        rows = jnp.concatenate(
            [
                source[:, 0, group * 16 : group * 16 + 16, :].reshape(owners * 16, source.shape[3])
                for source in sources
            ],
            axis=0,
        )
        out[...] = jnp.dot(
            jnp.concatenate([rows, rows], axis=1), weight_scr[...], preferred_element_type=F32
        )

    def widen(group, out):
        await_group(legendre_ref, legendre_scr, sems, step, group)
        for place in range(8):
            start = place * (cycles + 8)
            wide = legendre_scr[step, group * 8 + place].astype(F32)
            for tile in range(degrees // 128):
                out[tile, start : start + cycles, :] = wide[:, tile * 128 : tile * 128 + 128]

    multiply(0, terms[0])
    widen(0, values[0])
    for group in range(4):
        half = group % 2
        if group < 3:
            multiply(group + 1, terms[1 - half])
            widen(group + 1, values[1 - half])

        total = [jnp.zeros((8, degrees), F32), jnp.zeros((8, degrees), F32)]
        for away in range(4):
            for owner in range(owners):
                cycle = 4 * owner + (row ^ away)
                factor = jnp.concatenate(
                    [
                        values[half][tile, pl.ds(cycle, 8, stride=cycles + 8), :]
                        for tile in range(degrees // 128)
                    ],
                    axis=1,
                )
                start = (away * owners + owner) * 16
                for part in range(2):
                    at = start + part * 8
                    total[part] = total[part] + terms[half][at : at + 8, :] * factor
        lowest = jnp.zeros((8, degrees), jnp.int32)
        for place in range(8):
            entry = info_ref[(first + step) * 32 + group * 8 + place]
            lowest = jnp.where(sublane == place, entry & 4095, lowest)
        for part in range(2):
            masked = jnp.where(degree >= lowest, total[part], 0.0)
            if last:
                sorted_scr[part, group * 8 : group * 8 + 8, :] = masked
            else:
                out_ref[part, group * 8 : group * 8 + 8, :] = masked
    if last:
        scatter((first + step) * 32, sorted_scr, 32)


def adjoint(chunk, chunks, info, where, weight, pieces, legendre, earlier, order):
    orders_here, cycles, degrees = legendre.shape
    jb_here = orders_here // 32 // chunks
    owners = cycles // 4
    lanes = weight.shape[0] // 2
    piece_spec = pl.BlockSpec((owners, 1, 64, lanes), lambda t, *_: (0, t, 0, 0))
    if earlier:
        out = jax.ShapeDtypeStruct((2, orders_here, degrees), F32)
        out_spec = whole(out.shape)
    else:
        out = jax.ShapeDtypeStruct((2, 32 * jb_here, degrees), F32)
        out_spec = pl.BlockSpec((2, 32, degrees), lambda t, *_: (0, t, 0))
    return pl.pallas_call(
        functools.partial(adjoint_kernel, jb_here, chunk * jb_here, len(earlier)),
        grid_spec=pltpu.PrefetchScalarGridSpec(
            num_scalar_prefetch=2,
            grid=(jb_here,),
            in_specs=[piece_spec] * 4
            + [anywhere()] * 3
            + [whole((2, 32 * jb_here, degrees))] * len(earlier),
            out_specs=out_spec,
            scratch_shapes=[
                pltpu.VMEM(weight.shape, BF16),
                pltpu.VMEM((jb_here, 32, cycles, degrees), BF16),
                pltpu.VMEM((degrees // 128, 8 * (cycles + 8), 128), F32),
                pltpu.VMEM((degrees // 128, 8 * (cycles + 8), 128), F32),
                pltpu.VMEM((16 * cycles, degrees), F32),
                pltpu.VMEM((16 * cycles, degrees), F32),
                pltpu.VMEM((2, 32, degrees), F32),
                pltpu.SemaphoreType.DMA((jb_here, 4)),
                pltpu.SemaphoreType.DMA((1,)),
            ],
        ),
        out_shape=out,
        compiler_params=pltpu.CompilerParams(vmem_limit_bytes=48 * MIB),
        cost_estimate=pl.CostEstimate(
            flops=16 * jb_here * 4 * cycles * degrees * lanes * 2 * 2,
            bytes_accessed=jb_here * (32 * cycles * degrees * 2 + 4 * owners * 64 * lanes * 2),
            transcendentals=0,
        ),
        name="adjoint",
    )(info, where, *pieces, weight, legendre, order, *earlier)


def slot_tables(orders, device_count, ma_id):
    local_orders = orders.shape[0] // device_count
    blocks = local_orders // 32
    position = jnp.arange(local_orders, dtype=jnp.int32)
    wanted = blocks * (position % 32) + position // 32
    by_device = orders.reshape(device_count, local_orders)
    mine = lax.dynamic_slice_in_dim(orders, ma_id * local_orders, local_orders)
    info = jnp.sum(
        jnp.where(mine[None, :] // device_count == wanted[:, None], position[None, :] * 4096 + mine[None, :], 0),
        axis=1,
    )
    place = jnp.sum(
        jnp.where(
            by_device[:, None, :] // device_count == wanted[None, :, None],
            by_device[:, None, :] % device_count,
            0,
        ),
        axis=2,
    )
    place = place.reshape(device_count, blocks, 4, 1, 8, 1)
    place = jnp.broadcast_to(place, (device_count, blocks, 4, 2, 8, 128))
    return info, place.reshape(device_count, blocks, 64, 128).astype(BF16)


def body(
    coeffs,
    legendre,
    alpha_table,
    beta_table,
    radial_weight,
    radius_index,
    orders,
    cycle_offset,
    cycle_weight,
):
    row_id = lax.axis_index("row")
    ma_id = lax.axis_index("ma")
    device_count = lax.axis_size("ma")
    row_count = lax.axis_size("row")
    where = jnp.stack([row_id, ma_id]).astype(jnp.int32)
    info, places = slot_tables(orders, device_count, ma_id)
    synth_weight, adjoint_weight = filter_weights(
        radius_index, radial_weight, alpha_table, beta_table
    )
    core_pairs = [(i, i ^ 1) for i in range(row_count)]
    far_pairs = [(i, i ^ 2) for i in range(row_count)]
    chunks = min(CHUNKS, coeffs.shape[1] // 32)

    groups = min(GROUPS, chunks)
    size = chunks // groups
    kept, others, outgoing, incoming, arrived = [], [], [], [], []

    def launch(chunk, order):
        keep, send = synth(chunk, chunks, info, where, coeffs, synth_weight, legendre, order)
        kept.append(keep)
        others.append(lax.ppermute(send, "row", core_pairs))

    def pass_on(chunk, order):
        outgoing.append(core_sum(kept[chunk], others[chunk], order))
        incoming.append(lax.ppermute(outgoing[chunk], "row", far_pairs))

    def deliver(group, order):
        own = slice(group * size, (group + 1) * size)
        summed = full_sum(list(zip(kept[own], others[own], incoming[own])), order)
        arrived.append(lax.all_to_all(summed, "ma", split_axis=0, concat_axis=0, tiled=True))
        return summed

    if chunks == 4:
        launch(0, [])
        launch(1, [])
        pass_on(0, kept[1])
        info, places = lax.optimization_barrier((info, places))
        launch(2, [outgoing[0]])
        pass_on(1, kept[2])
        pass_on(2, outgoing[1])
        launch(3, [outgoing[2], incoming[0]])
        summed = deliver(0, kept[3])
        pass_on(3, summed)
        deliver(1, outgoing[3])
    else:
        for chunk in range(chunks):
            launch(chunk, [])
        for chunk in range(chunks):
            pass_on(chunk, kept[-1])
        for group in range(groups):
            deliver(group, outgoing[-1])
    analysed = cycle_work(arrived, places, cycle_offset, where, cycle_weight)
    own = [
        lax.all_to_all(piece, "ma", split_axis=0, concat_axis=0, tiled=True) for piece in analysed
    ]
    far, gradient = [], []
    for group in range(groups):
        far.append(lax.ppermute(own[group], "row", far_pairs))
        if group + 1 < groups:
            far[group], own[group + 1] = lax.optimization_barrier((far[group], own[group + 1]))
    for group in range(groups):
        if gradient:
            far[group], gradient[-1] = lax.optimization_barrier((far[group], gradient[-1]))
        core = lax.ppermute(own[group], "row", core_pairs)
        corner = lax.ppermute(far[group], "row", core_pairs)
        gradient.append(
            adjoint(
                group,
                groups,
                info,
                where,
                adjoint_weight,
                (own[group], core, far[group], corner),
                legendre,
                gradient if group == groups - 1 else [],
                info,
            )
        )
    return gradient[-1]


def solution(mesh):
    in_specs = (
        P(None, "ma", "row"),
        P("ma", None, "row"),
        P(None, "row"),
        P(None, "row"),
        P(),
        P(),
        P(),
        P("ma"),
        P("ma"),
    )
    out_specs = P(None, "ma", "row")
    return jax.shard_map(body, mesh=mesh, in_specs=in_specs, out_specs=out_specs, check_vma=False)
```

```python
import functools
import math

import jax
import jax.numpy as jnp
import numpy as np
from jax import lax
from jax.experimental import pallas as pl
from jax.experimental.pallas import tpu as pltpu
from jax.sharding import PartitionSpec as P

NPIX = 4096
SIDE = 64
PADDED = 136
CHUNKS = 4
GROUPS = 2
BLOCK = 16
MIB = 1 << 20
F32 = jnp.float32
BF16 = jnp.bfloat16


def split_table(table):
    high = table.astype(jnp.bfloat16)
    low = (table - high.astype(np.float64)).astype(jnp.bfloat16)
    return high, low


@functools.lru_cache(maxsize=None)
def fourier_tables():
    first = np.arange(SIDE)
    spin = np.arange(2).reshape(2, 1, 1, 1, 1, 1)
    order = SIDE * np.arange(32)[None, :] + np.arange(SIDE)[:, None]
    order = order.reshape(1, SIDE, 1, 1, 1, 32)
    angle = (2 * first.reshape(1, 1, 1, SIDE, 1, 1) + spin) * order % (2 * NPIX) * (math.pi / NPIX)
    cosine, sine = np.cos(angle), np.sin(angle)
    row_part = np.arange(2).reshape(1, 1, 2, 1, 1, 1)
    col_part = np.arange(2).reshape(1, 1, 1, 1, 2, 1)
    same = (row_part == col_part).astype(np.float64)
    cross = np.where(row_part == 1, 1.0, -1.0) * (row_part != col_part)
    doubling = np.where(order == 0, 1.0, 2.0)
    spread = (doubling * (same * cosine + cross * sine)).reshape(2, SIDE, 2 * SIDE, SIDE)
    gather = (same * cosine + cross * sine).reshape(2, SIDE, 2 * SIDE, SIDE)
    gather = np.swapaxes(gather, 2, 3)
    spread_parts = np.concatenate(split_table(spread), axis=3)
    gather_parts = np.concatenate(split_table(gather), axis=2)
    square = first[:, None] * first[None, :] % SIDE * (2.0 * math.pi / SIDE)
    pixel = np.concatenate(split_table(np.concatenate([np.cos(square), -np.sin(square)], axis=1)), axis=0)
    back_high, back_low = split_table(np.concatenate([np.cos(square), -np.sin(square)], axis=0))
    back = np.concatenate([back_high, back_high, back_low, back_low], axis=1)
    return spread_parts, pixel, back, gather_parts


def two_parts(value):
    high = value.astype(BF16)
    low = (value - high.astype(F32)).astype(BF16)
    return high, low


def whole(shape):
    return pl.BlockSpec(shape, lambda t, *_: (0,) * len(shape))


def anywhere():
    return pl.BlockSpec(memory_space=pl.ANY)


def hbm():
    return pl.BlockSpec(memory_space=pltpu.HBM)


def weights_kernel(
    node_ref,
    radial_ref,
    alpha_ref,
    beta_ref,
    synth_ref,
    adjoint_ref,
    alpha_scr,
    beta_scr,
    filter_scr,
    weighted_scr,
    sems,
):
    copies = [
        pltpu.make_async_copy(alpha_ref, alpha_scr, sems.at[0]),
        pltpu.make_async_copy(beta_ref, beta_scr, sems.at[1]),
    ]
    for copy in copies:
        copy.start()
    for copy in copies:
        copy.wait()
    radii = node_ref.shape[0]

    def gather(radius, carry):
        node = node_ref[radius]
        scale = radial_ref[node]
        alpha = alpha_scr[pl.ds(node, 1), :]
        beta = beta_scr[pl.ds(node, 1), :]
        filter_scr[pl.ds(radius, 1), :] = alpha
        filter_scr[pl.ds(radii + radius, 1), :] = beta
        weighted_scr[pl.ds(radius, 1), :] = scale * alpha
        weighted_scr[pl.ds(radii + radius, 1), :] = (2.0 * scale) * beta
        return carry

    lax.fori_loop(0, radii, gather, 0, unroll=8)
    high, low = two_parts(filter_scr[...].T)
    synth_ref[:, : 2 * radii] = high
    synth_ref[:, 2 * radii :] = low
    high, low = two_parts(weighted_scr[...])
    adjoint_ref[: 2 * radii, :] = high
    adjoint_ref[2 * radii :, :] = low


def filter_weights(radius_index, radial_weight, alpha_table, beta_table):
    radii = radius_index.shape[0]
    degrees = alpha_table.shape[1]
    return pl.pallas_call(
        weights_kernel,
        grid_spec=pltpu.PrefetchScalarGridSpec(
            num_scalar_prefetch=2,
            grid=(1,),
            in_specs=[hbm(), hbm()],
            out_specs=[whole((degrees, 4 * radii)), whole((4 * radii, degrees))],
            scratch_shapes=[pltpu.VMEM(alpha_table.shape, F32)] * 2
            + [pltpu.VMEM((2 * radii, degrees), F32)] * 2
            + [pltpu.SemaphoreType.DMA((2,))],
        ),
        out_shape=[
            jax.ShapeDtypeStruct((degrees, 4 * radii), BF16),
            jax.ShapeDtypeStruct((4 * radii, degrees), BF16),
        ],
        compiler_params=pltpu.CompilerParams(vmem_limit_bytes=56 * MIB),
        name="filter_weights",
    )(radius_index, radial_weight, alpha_table, beta_table)


def synth_kernel(
    first, order_ref, where_ref, coeffs_ref, weight_ref, legendre_ref, *refs
):
    keep_ref, send_ref, terms_scr, sums_scr = refs[-4:]
    step = pl.program_id(0)
    row = where_ref[0]
    base = where_ref[1] + first + step * BLOCK
    degrees = coeffs_ref.shape[2]
    cycles = legendre_ref.shape[1]
    owners = cycles // 4
    lanes = weight_ref.shape[1] // 2
    degree = row * degrees + lax.broadcasted_iota(jnp.int32, (1, degrees), 1)
    for slot in range(BLOCK):
        live = degree >= order_ref[base + slot]
        values = legendre_ref[slot].astype(F32)
        for part in range(2):
            coeff = jnp.where(live, coeffs_ref[part, slot : slot + 1, :], 0.0)
            high, low = two_parts(values * coeff)
            start = (part * BLOCK + slot) * cycles
            terms_scr[0, start : start + cycles, :] = high
            terms_scr[1, start : start + cycles, :] = low
    for part in range(2):
        rows = slice(part * BLOCK * cycles, (part + 1) * BLOCK * cycles)
        both = jnp.dot(terms_scr[0, rows], weight_ref[...], preferred_element_type=F32)
        rest = jnp.dot(terms_scr[1, rows], weight_ref[:, :lanes], preferred_element_type=F32)
        sums_scr[rows, :] = both[:, :lanes] + both[:, lanes:] + rest
    for part in range(2):
        for owner in range(owners):
            for away in range(4):
                cycle = 4 * owner + (row ^ away)
                piece = sums_scr[pl.ds(part * BLOCK * cycles + cycle, BLOCK, stride=cycles), :]
                target = send_ref if away % 2 else keep_ref
                target[away // 2, owner, :, part * lanes : (part + 1) * lanes] = piece


def synth(chunk, chunks, orders, where, coeffs, weight, legendre, order):
    orders_here, cycles, degrees = legendre.shape
    count = orders_here // chunks
    steps = count // BLOCK
    start = chunk * steps
    owners = cycles // 4
    lanes = weight.shape[1] // 2
    out = jax.ShapeDtypeStruct((2, owners, count, 2 * lanes), F32)
    out_spec = pl.BlockSpec((2, owners, BLOCK, 2 * lanes), lambda t, *_: (0, 0, t, 0))
    return pl.pallas_call(
        functools.partial(synth_kernel, chunk * count),
        grid_spec=pltpu.PrefetchScalarGridSpec(
            num_scalar_prefetch=2,
            grid=(steps,),
            in_specs=[
                pl.BlockSpec((2, BLOCK, degrees), lambda t, *_: (0, start + t, 0)),
                whole(weight.shape),
                pl.BlockSpec((BLOCK, cycles, degrees), lambda t, *_: (start + t, 0, 0)),
            ]
            + [anywhere()] * len(order),
            out_specs=[out_spec, out_spec],
            scratch_shapes=[
                pltpu.VMEM((2, 2 * BLOCK * cycles, degrees), BF16),
                pltpu.VMEM((2 * BLOCK * cycles, lanes), F32),
            ],
        ),
        out_shape=[out, out],
        compiler_params=pltpu.CompilerParams(vmem_limit_bytes=56 * MIB),
        cost_estimate=pl.CostEstimate(
            flops=2 * count * cycles * degrees * lanes * 2 * 4,
            bytes_accessed=count * (cycles * degrees * 2 + 2 * cycles * lanes * 4),
            transcendentals=0,
        ),
        name="synth",
    )(orders, where, coeffs, weight, legendre, *order)


def core_sum_kernel(keep_ref, other_ref, order_ref, out_ref):
    out_ref[...] = (keep_ref[0] + other_ref[0]).astype(BF16)


def core_sum(keep, other, order):
    shape = keep.shape[1:]
    half = pl.BlockSpec((1,) + shape, lambda t: (1, 0, 0, 0))
    return pl.pallas_call(
        core_sum_kernel,
        grid=(1,),
        in_specs=[half, half, anywhere()],
        out_specs=pl.BlockSpec(shape, lambda t: (0, 0, 0)),
        out_shape=jax.ShapeDtypeStruct(shape, BF16),
        compiler_params=pltpu.CompilerParams(vmem_limit_bytes=16 * MIB),
        cost_estimate=pl.CostEstimate(flops=4 * 10**10, bytes_accessed=MIB, transcendentals=0),
        name="core_sum",
    )(keep, other, order)


def full_sum_kernel(order_ref, *refs):
    out_ref = refs[-1]
    start = 0
    for index in range(0, len(refs) - 1, 3):
        keep_ref, other_ref, incoming_ref = refs[index : index + 3]
        count = incoming_ref.shape[1]
        total = keep_ref[0] + other_ref[0] + incoming_ref[...].astype(F32)
        out_ref[:, start : start + count] = total.astype(BF16)
        start += count


def full_sum(chunks, order):
    operands, specs, count = [], [anywhere()], 0
    for keep, other, incoming in chunks:
        shape = incoming.shape
        half = pl.BlockSpec((1,) + shape, lambda t: (0, 0, 0, 0))
        operands += [keep, other, incoming]
        specs += [half, half, pl.BlockSpec(shape, lambda t: (0, 0, 0))]
        count += shape[1]
    full = (shape[0], count, shape[2])
    return pl.pallas_call(
        full_sum_kernel,
        grid=(1,),
        in_specs=specs,
        out_specs=pl.BlockSpec(full, lambda t: (0, 0, 0)),
        out_shape=jax.ShapeDtypeStruct(full, BF16),
        compiler_params=pltpu.CompilerParams(vmem_limit_bytes=24 * MIB),
        cost_estimate=pl.CostEstimate(flops=4 * 10**10, bytes_accessed=MIB, transcendentals=0),
        name="full_sum",
    )(order, *operands)


def cycle_kernel(device_count, groups, offset_ref, where_ref, weight_ref, *refs):
    pieces = refs[:groups]
    place_ref, sort_ref, unsort_ref, spread_ref, pixel_ref, back_ref, gather_ref = refs[
        groups : groups + 7
    ]
    outs = refs[groups + 7 : 2 * groups + 7]
    spread_scr, gather_scr, sorted_scr, middle_scr, product_scr, back_scr, sems = refs[
        2 * groups + 7 :
    ]
    blocks = place_ref.shape[1]
    count = pieces[0].shape[1]
    lanes = pieces[0].shape[2] // 2
    turned = offset_ref[where_ref[0]]
    scale = weight_ref[where_ref[0]]
    lane = lax.broadcasted_iota(jnp.int32, (SIDE, lanes), 1)

    def spread_copy(block):
        rows = pl.ds(block * device_count, device_count)
        return pltpu.make_async_copy(
            spread_ref.at[turned, rows], spread_scr.at[rows], sems.at[block]
        )

    gather_copy = pltpu.make_async_copy(gather_ref.at[turned], gather_scr, sems.at[blocks])
    for block in range(blocks):
        spread_copy(block).start()
    gather_copy.start()

    def sort_step(peer, carry):
        slots = jnp.concatenate([piece[peer] for piece in pieces], axis=0)
        sorted_scr[peer] = jnp.dot(
            sort_ref[peer], slots, preferred_element_type=F32
        ).astype(BF16)
        return carry

    lax.fori_loop(0, device_count, sort_step, 0, unroll=2)

    def spread_step(block, carry):
        spread_copy(block).wait()
        rows = pl.ds(pl.multiple_of(block * 32, 32), 32)

        def one(spot):
            picked = jnp.zeros((32, 2 * lanes), BF16)
            for peer in range(device_count):
                place = place_ref[peer, block]
                picked = jnp.where(
                    place == lax.convert_element_type(spot, BF16),
                    sorted_scr[peer, rows, :],
                    picked,
                )
            low_order = block * device_count + spot
            column = jnp.concatenate([picked[:, :lanes], picked[:, lanes:]], axis=0)
            stage = jnp.dot(
                spread_scr[low_order],
                jnp.concatenate([column, column], axis=0),
                preferred_element_type=F32,
            )
            middle_scr[pl.ds(low_order * PADDED, 2 * SIDE), :] = stage

        if device_count <= 8:
            for spot in range(device_count):
                one(spot)
        else:
            lax.fori_loop(0, device_count, lambda s, x: (one(s), x)[1], 0)
        return carry

    lax.fori_loop(0, blocks, spread_step, 0)

    def pixel_step(step, total):
        for inner in range(8):
            first = step * 8 + inner
            column = jnp.concatenate(
                [
                    middle_scr[pl.ds(first, SIDE, stride=PADDED), :],
                    middle_scr[pl.ds(first + SIDE, SIDE, stride=PADDED), :],
                ],
                axis=0,
            )
            high, low = two_parts(column)
            stage = jnp.dot(
                pixel_ref[...], jnp.concatenate([high, low], axis=1), preferred_element_type=F32
            )
            field = stage[:SIDE, :lanes] + stage[:SIDE, lanes:] + stage[SIDE:, :lanes]
            other = pltpu.roll(field, lanes // 2, 1)
            product = other * jnp.where(lane < lanes // 2, other, field)
            product_scr[first] = product
            total = total + jnp.sum(product.reshape(8, 8, lanes), axis=0)
        return total

    total = lax.fori_loop(0, SIDE // 8, pixel_step, jnp.zeros((8, lanes), F32))
    mean = jnp.sum(total, axis=0, keepdims=True) * (1.0 / NPIX)

    def back_step(step, carry):
        for inner in range(8):
            first = step * 8 + inner
            high, low = two_parts(product_scr[first] - mean)
            back_scr[pl.ds(first * PADDED, 2 * SIDE), :] = jnp.dot(
                back_ref[...],
                jnp.concatenate([high, low, high, low], axis=0),
                preferred_element_type=F32,
            )
        return carry

    lax.fori_loop(0, SIDE // 8, back_step, 0)
    gather_copy.wait()

    def gather_step(block, carry):
        rows = pl.ds(pl.multiple_of(block * 32, 32), 32)

        def one(spot):
            low_order = block * device_count + spot
            column = jnp.concatenate(
                [
                    back_scr[pl.ds(low_order, SIDE, stride=PADDED), :],
                    back_scr[pl.ds(low_order + SIDE, SIDE, stride=PADDED), :],
                ],
                axis=0,
            )
            high, low = two_parts(column)
            stage = jnp.dot(
                gather_scr[low_order],
                jnp.concatenate([high, low], axis=1),
                preferred_element_type=F32,
            )
            value = stage[:SIDE, :lanes] + stage[:SIDE, lanes:] + stage[SIDE:, :lanes]
            value = (value * scale).astype(BF16)
            return jnp.concatenate([value[:32], value[32:]], axis=1)

        if device_count <= 8:
            found = [one(spot) for spot in range(device_count)]
            for peer in range(device_count):
                place = place_ref[peer, block]
                picked = found[0]
                for spot in range(1, device_count):
                    picked = jnp.where(place == spot, found[spot], picked)
                sorted_scr[peer, rows, :] = picked
        else:

            def spot_step(spot, carry):
                value = one(spot)
                for peer in range(device_count):
                    sorted_scr[peer, rows, :] = jnp.where(
                        place_ref[peer, block] == lax.convert_element_type(spot, BF16),
                        value,
                        sorted_scr[peer, rows, :],
                    )
                return carry

            lax.fori_loop(0, device_count, spot_step, 0)
        return carry

    lax.fori_loop(0, blocks, gather_step, 0)

    def unsort_step(peer, carry):
        slots = jnp.dot(
            unsort_ref[peer], sorted_scr[peer], preferred_element_type=F32
        ).astype(BF16)
        for group in range(groups):
            outs[group][peer] = slots[group * count : (group + 1) * count]
        return carry

    lax.fori_loop(0, device_count, unsort_step, 0, unroll=2)


def cycle_work(pieces, places, sort, unsort, offset, where, cycle_weight):
    groups = len(pieces)
    device_count, count, lanes = pieces[0].shape
    spread, pixel, back, gather = [jnp.asarray(table) for table in fourier_tables()]
    tables = [places, sort, unsort]
    return pl.pallas_call(
        functools.partial(cycle_kernel, device_count, groups),
        grid_spec=pltpu.PrefetchScalarGridSpec(
            num_scalar_prefetch=2,
            grid=(1,),
            in_specs=[pl.BlockSpec(memory_space=pltpu.SMEM)]
            + [whole(piece.shape) for piece in pieces]
            + [whole(table.shape) for table in tables]
            + [hbm(), whole(pixel.shape), whole(back.shape), hbm()],
            out_specs=[whole(piece.shape) for piece in pieces],
            scratch_shapes=[
                pltpu.VMEM(spread.shape[1:], BF16),
                pltpu.VMEM(gather.shape[1:], BF16),
                pltpu.VMEM((device_count, groups * count, lanes), BF16),
                pltpu.VMEM((SIDE * PADDED, lanes // 2), F32),
                pltpu.VMEM((SIDE, SIDE, lanes // 2), F32),
                pltpu.VMEM((SIDE * PADDED, lanes // 2), F32),
                pltpu.SemaphoreType.DMA((places.shape[1] + 1,)),
            ],
        ),
        out_shape=[jax.ShapeDtypeStruct(piece.shape, BF16) for piece in pieces],
        compiler_params=pltpu.CompilerParams(vmem_limit_bytes=48 * MIB),
        cost_estimate=pl.CostEstimate(
            flops=4 * SIDE * 128 * 256 * 256 * 2, bytes_accessed=8 * MIB, transcendentals=0
        ),
        name="cycle_work",
    )(offset, where, cycle_weight, *pieces, *tables, spread, pixel, back, gather)


def adjoint_kernel(
    first, order_ref, where_ref, own_ref, core_ref, far_ref, corner_ref, weight_ref, legendre_ref, *refs
):
    out_ref, values_scr, terms_scr = refs[-3:]
    step = pl.program_id(0)
    row = where_ref[0]
    base = where_ref[1] + first + step * BLOCK
    degrees = weight_ref.shape[1]
    cycles = legendre_ref.shape[1]
    owners = cycles // 4
    lanes = weight_ref.shape[0] // 2
    pitch = cycles + 8
    tiles = degrees // 128
    degree = row * degrees + lax.broadcasted_iota(jnp.int32, (8, degrees), 1)
    sublane = lax.broadcasted_iota(jnp.int32, (8, degrees), 0)
    for slot in range(BLOCK):
        wide = legendre_ref[slot].astype(F32)
        for tile in range(tiles):
            values_scr[tile, slot * pitch : slot * pitch + cycles, :] = wide[
                :, tile * 128 : tile * 128 + 128
            ]
    sources = (own_ref, core_ref, far_ref, corner_ref)
    quarter = owners * BLOCK
    for part in range(2):
        for away in range(4):
            rows = sources[away][:, :, part * lanes : (part + 1) * lanes].reshape(quarter, lanes)
            start = (part * 4 + away) * quarter
            terms_scr[start : start + quarter, :] = jnp.dot(
                jnp.concatenate([rows, rows], axis=1), weight_ref[...], preferred_element_type=F32
            )
    for half in range(BLOCK // 8):
        total = [jnp.zeros((8, degrees), F32), jnp.zeros((8, degrees), F32)]
        for away in range(4):
            for owner in range(owners):
                cycle = 4 * owner + (row ^ away)
                factor = jnp.concatenate(
                    [
                        values_scr[tile, pl.ds(half * 8 * pitch + cycle, 8, stride=pitch), :]
                        for tile in range(tiles)
                    ],
                    axis=1,
                )
                for part in range(2):
                    at = (part * 4 + away) * quarter + owner * BLOCK + half * 8
                    total[part] = total[part] + terms_scr[at : at + 8, :] * factor
        lowest = jnp.zeros((8, degrees), jnp.int32)
        for slot in range(8):
            lowest = jnp.where(sublane == slot, order_ref[base + half * 8 + slot], lowest)
        for part in range(2):
            out_ref[part, half * 8 : half * 8 + 8, :] = jnp.where(
                degree >= lowest, total[part], 0.0
            )


def adjoint(chunk, chunks, orders, where, weight, pieces, legendre, earlier):
    orders_here, cycles, degrees = legendre.shape
    count = orders_here // chunks
    steps = count // BLOCK
    start = chunk * steps
    owners = cycles // 4
    lanes = weight.shape[0] // 2
    piece_spec = pl.BlockSpec((owners, BLOCK, 2 * lanes), lambda t, *_: (0, t, 0))
    out = jax.ShapeDtypeStruct((2, orders_here, degrees), F32)
    return pl.pallas_call(
        functools.partial(adjoint_kernel, chunk * count),
        grid_spec=pltpu.PrefetchScalarGridSpec(
            num_scalar_prefetch=2,
            grid=(steps,),
            in_specs=[piece_spec] * 4
            + [
                whole(weight.shape),
                pl.BlockSpec((BLOCK, cycles, degrees), lambda t, *_: (start + t, 0, 0)),
            ]
            + [anywhere()] * len(earlier),
            out_specs=pl.BlockSpec((2, BLOCK, degrees), lambda t, *_: (0, start + t, 0)),
            scratch_shapes=[
                pltpu.VMEM((degrees // 128, BLOCK * (cycles + 8), 128), F32),
                pltpu.VMEM((2 * BLOCK * cycles, degrees), F32),
            ],
        ),
        out_shape=out,
        input_output_aliases={8: 0} if earlier else {},
        compiler_params=pltpu.CompilerParams(vmem_limit_bytes=48 * MIB),
        cost_estimate=pl.CostEstimate(
            flops=2 * count * cycles * degrees * lanes * 2 * 2,
            bytes_accessed=count * (cycles * degrees * 2 + 2 * cycles * lanes * 2),
            transcendentals=0,
        ),
        name="adjoint",
    )(orders, where, *pieces, weight, legendre, *earlier)


def slot_tables(orders, device_count):
    local_orders = orders.shape[0] // device_count
    blocks = local_orders // 32
    by_device = orders.reshape(device_count, local_orders)
    block = by_device // device_count
    position = 32 * (block % blocks) + block // blocks
    wanted = jnp.arange(local_orders, dtype=jnp.int32)
    sort = position[:, None, :] == wanted[None, :, None]
    unsort = position[:, :, None] == wanted[None, None, :]
    place = jnp.sum(jnp.where(sort, (by_device % device_count)[:, None, :], 0), axis=2)
    place = place.reshape(device_count, blocks, 32, 1)
    place = jnp.broadcast_to(place, (device_count, blocks, 32, 256))
    return place.astype(BF16), sort.astype(BF16), unsort.astype(BF16)


def body(
    coeffs,
    legendre,
    alpha_table,
    beta_table,
    radial_weight,
    radius_index,
    orders,
    cycle_offset,
    cycle_weight,
):
    row_id = lax.axis_index("row")
    ma_id = lax.axis_index("ma")
    device_count = lax.axis_size("ma")
    row_count = lax.axis_size("row")
    local_orders = coeffs.shape[1]
    where = jnp.stack([row_id, ma_id * local_orders]).astype(jnp.int32)
    places, sort, unsort = slot_tables(orders, device_count)
    synth_weight, adjoint_weight = filter_weights(
        radius_index, radial_weight, alpha_table, beta_table
    )
    core_pairs = [(i, i ^ 1) for i in range(row_count)]
    far_pairs = [(i, i ^ 2) for i in range(row_count)]
    chunks = min(CHUNKS, local_orders // 32)
    groups = min(GROUPS, chunks)
    size = chunks // groups
    kept, others, outgoing, incoming, arrived = [], [], [], [], []

    def launch(chunk, order):
        keep, send = synth(chunk, chunks, orders, where, coeffs, synth_weight, legendre, order)
        kept.append(keep)
        others.append(lax.ppermute(send, "row", core_pairs))

    def pass_on(chunk, order):
        outgoing.append(core_sum(kept[chunk], others[chunk], order))
        incoming.append(lax.ppermute(outgoing[chunk], "row", far_pairs))

    def deliver(group, order):
        own = slice(group * size, (group + 1) * size)
        summed = full_sum(list(zip(kept[own], others[own], incoming[own])), order)
        arrived.append(lax.all_to_all(summed, "ma", split_axis=0, concat_axis=0, tiled=True))
        return summed

    if chunks == 4:
        launch(0, [])
        launch(1, [])
        pass_on(0, kept[1])
        places, sort, unsort, ready = lax.optimization_barrier(
            (places, sort, unsort, outgoing[0])
        )
        launch(2, [ready])
        pass_on(1, kept[2])
        pass_on(2, outgoing[1])
        launch(3, [outgoing[2], incoming[0]])
        summed = deliver(0, kept[3])
        pass_on(3, summed)
        deliver(1, outgoing[3])
    else:
        for chunk in range(chunks):
            launch(chunk, [])
        for chunk in range(chunks):
            pass_on(chunk, kept[-1])
        for group in range(groups):
            deliver(group, outgoing[-1])
    analysed = cycle_work(arrived, places, sort, unsort, cycle_offset, where, cycle_weight)
    own = [
        lax.all_to_all(piece, "ma", split_axis=0, concat_axis=0, tiled=True) for piece in analysed
    ]
    far, gradient = [], []
    for group in range(groups):
        far.append(lax.ppermute(own[group], "row", far_pairs))
        if group + 1 < groups:
            far[group], own[group + 1] = lax.optimization_barrier((far[group], own[group + 1]))
    for group in range(groups):
        if gradient:
            far[group], gradient[-1] = lax.optimization_barrier((far[group], gradient[-1]))
        core = lax.ppermute(own[group], "row", core_pairs)
        corner = lax.ppermute(far[group], "row", core_pairs)
        gradient.append(
            adjoint(
                group,
                groups,
                orders,
                where,
                adjoint_weight,
                (own[group], core, far[group], corner),
                legendre,
                gradient[-1:],
            )
        )
    return gradient[-1]


def solution(mesh):
    in_specs = (
        P(None, "ma", "row"),
        P("ma", None, "row"),
        P(None, "row"),
        P(None, "row"),
        P(),
        P(),
        P(),
        P("ma"),
        P("ma"),
    )
    out_specs = P(None, "ma", "row")
    return jax.shard_map(body, mesh=mesh, in_specs=in_specs, out_specs=out_specs, check_vma=False)
```

```python
import functools
import math

import jax
import jax.numpy as jnp
import numpy as np
from jax import lax
from jax.experimental import pallas as pl
from jax.experimental.pallas import tpu as pltpu
from jax.sharding import PartitionSpec as P

NPIX = 4096
SIDE = 64
PADDED = 136
CHUNKS = 4
GROUPS = 2
SYNTH_BLOCK = 16
BLOCK = 32
MIB = 1 << 20
F32 = jnp.float32
BF16 = jnp.bfloat16


def split_table(table):
    high = table.astype(jnp.bfloat16)
    low = (table - high.astype(np.float64)).astype(jnp.bfloat16)
    return high, low


@functools.lru_cache(maxsize=None)
def fourier_tables():
    first = np.arange(SIDE)
    spin = np.arange(2).reshape(2, 1, 1, 1, 1, 1)
    order = SIDE * np.arange(32)[None, :] + np.arange(SIDE)[:, None]
    order = order.reshape(1, SIDE, 1, 1, 1, 32)
    angle = (2 * first.reshape(1, 1, 1, SIDE, 1, 1) + spin) * order % (2 * NPIX) * (math.pi / NPIX)
    cosine, sine = np.cos(angle), np.sin(angle)
    row_part = np.arange(2).reshape(1, 1, 2, 1, 1, 1)
    col_part = np.arange(2).reshape(1, 1, 1, 1, 2, 1)
    same = (row_part == col_part).astype(np.float64)
    cross = np.where(row_part == 1, 1.0, -1.0) * (row_part != col_part)
    doubling = np.where(order == 0, 1.0, 2.0)
    spread = (doubling * (same * cosine + cross * sine)).reshape(2, SIDE, 2 * SIDE, SIDE)
    gather = (same * cosine + cross * sine).reshape(2, SIDE, 2 * SIDE, SIDE)
    gather = np.swapaxes(gather, 2, 3)
    spread_parts = np.concatenate(split_table(spread), axis=3)
    gather_parts = np.concatenate(split_table(gather), axis=2)
    square = first[:, None] * first[None, :] % SIDE * (2.0 * math.pi / SIDE)
    pixel = np.concatenate(split_table(np.concatenate([np.cos(square), -np.sin(square)], axis=1)), axis=0)
    back_high, back_low = split_table(np.concatenate([np.cos(square), -np.sin(square)], axis=0))
    back = np.concatenate([back_high, back_high, back_low, back_low], axis=1)
    return spread_parts, pixel, back, gather_parts


def two_parts(value):
    high = value.astype(BF16)
    low = (value - high.astype(F32)).astype(BF16)
    return high, low


def whole(shape):
    return pl.BlockSpec(shape, lambda t, *_: (0,) * len(shape))


def anywhere():
    return pl.BlockSpec(memory_space=pl.ANY)


def hbm():
    return pl.BlockSpec(memory_space=pltpu.HBM)


def weights_kernel(
    node_ref,
    radial_ref,
    alpha_ref,
    beta_ref,
    synth_ref,
    adjoint_ref,
    alpha_scr,
    beta_scr,
    filter_scr,
    weighted_scr,
    sems,
):
    copies = [
        pltpu.make_async_copy(alpha_ref, alpha_scr, sems.at[0]),
        pltpu.make_async_copy(beta_ref, beta_scr, sems.at[1]),
    ]
    for copy in copies:
        copy.start()
    for copy in copies:
        copy.wait()
    radii = node_ref.shape[0]

    def gather(radius, carry):
        node = node_ref[radius]
        scale = radial_ref[node]
        alpha = alpha_scr[pl.ds(node, 1), :]
        beta = beta_scr[pl.ds(node, 1), :]
        filter_scr[pl.ds(radius, 1), :] = alpha
        filter_scr[pl.ds(radii + radius, 1), :] = beta
        weighted_scr[pl.ds(radius, 1), :] = scale * alpha
        weighted_scr[pl.ds(radii + radius, 1), :] = (2.0 * scale) * beta
        return carry

    lax.fori_loop(0, radii, gather, 0, unroll=8)
    high, low = two_parts(filter_scr[...].T)
    synth_ref[:, : 2 * radii] = high
    synth_ref[:, 2 * radii :] = low
    high, low = two_parts(weighted_scr[...])
    adjoint_ref[: 2 * radii, :] = high
    adjoint_ref[2 * radii :, :] = low


def filter_weights(radius_index, radial_weight, alpha_table, beta_table):
    radii = radius_index.shape[0]
    degrees = alpha_table.shape[1]
    return pl.pallas_call(
        weights_kernel,
        grid_spec=pltpu.PrefetchScalarGridSpec(
            num_scalar_prefetch=2,
            grid=(1,),
            in_specs=[hbm(), hbm()],
            out_specs=[whole((degrees, 4 * radii)), whole((4 * radii, degrees))],
            scratch_shapes=[pltpu.VMEM(alpha_table.shape, F32)] * 2
            + [pltpu.VMEM((2 * radii, degrees), F32)] * 2
            + [pltpu.SemaphoreType.DMA((2,))],
        ),
        out_shape=[
            jax.ShapeDtypeStruct((degrees, 4 * radii), BF16),
            jax.ShapeDtypeStruct((4 * radii, degrees), BF16),
        ],
        compiler_params=pltpu.CompilerParams(vmem_limit_bytes=56 * MIB),
        name="filter_weights",
    )(radius_index, radial_weight, alpha_table, beta_table)


def synth_kernel(
    first, order_ref, where_ref, coeffs_ref, weight_ref, legendre_ref, *refs
):
    keep_ref, send_ref, terms_even, terms_odd, sums_even, sums_odd = refs[-6:]
    step = pl.program_id(0)
    row = where_ref[0]
    base = where_ref[1] + first + step * SYNTH_BLOCK
    degrees = coeffs_ref.shape[2]
    cycles = legendre_ref.shape[1]
    owners = cycles // 4
    lanes = weight_ref.shape[1] // 2
    degree = row * degrees + lax.broadcasted_iota(jnp.int32, (1, degrees), 1)
    for group in range(SYNTH_BLOCK // 8):
        terms = terms_odd if group % 2 else terms_even
        sums = sums_odd if group % 2 else sums_even
        for place in range(8):
            slot = group * 8 + place
            live = degree >= order_ref[base + slot]
            values = legendre_ref[slot].astype(F32)
            for part in range(2):
                coeff = jnp.where(live, coeffs_ref[part, slot : slot + 1, :], 0.0)
                high, low = two_parts(values * coeff)
                start = (part * 8 + place) * cycles
                terms[0, start : start + cycles, :] = high
                terms[1, start : start + cycles, :] = low
        both = jnp.dot(terms[0], weight_ref[...], preferred_element_type=F32)
        rest = jnp.dot(terms[1], weight_ref[:, :lanes], preferred_element_type=F32)
        sums[...] = both[:, :lanes] + both[:, lanes:] + rest
        for part in range(2):
            for owner in range(owners):
                for away in range(4):
                    cycle = 4 * owner + (row ^ away)
                    piece = sums[pl.ds(part * 8 * cycles + cycle, 8, stride=cycles), :]
                    target = send_ref if away % 2 else keep_ref
                    target[
                        away // 2,
                        owner,
                        group * 8 : group * 8 + 8,
                        part * lanes : (part + 1) * lanes,
                    ] = piece


def synth(chunk, chunks, orders, where, coeffs, weight, legendre):
    orders_here, cycles, degrees = legendre.shape
    count = orders_here // chunks
    steps = count // SYNTH_BLOCK
    start = chunk * steps
    owners = cycles // 4
    lanes = weight.shape[1] // 2
    out = jax.ShapeDtypeStruct((2, owners, count, 2 * lanes), F32)
    out_spec = pl.BlockSpec((2, owners, SYNTH_BLOCK, 2 * lanes), lambda t, *_: (0, 0, t, 0))
    return pl.pallas_call(
        functools.partial(synth_kernel, chunk * count),
        grid_spec=pltpu.PrefetchScalarGridSpec(
            num_scalar_prefetch=2,
            grid=(steps,),
            in_specs=[
                pl.BlockSpec((2, SYNTH_BLOCK, degrees), lambda t, *_: (0, start + t, 0)),
                whole(weight.shape),
                pl.BlockSpec((SYNTH_BLOCK, cycles, degrees), lambda t, *_: (start + t, 0, 0)),
            ],
            out_specs=[out_spec, out_spec],
            scratch_shapes=[
                pltpu.VMEM((2, 16 * cycles, degrees), BF16),
                pltpu.VMEM((2, 16 * cycles, degrees), BF16),
                pltpu.VMEM((16 * cycles, lanes), F32),
                pltpu.VMEM((16 * cycles, lanes), F32),
            ],
        ),
        out_shape=[out, out],
        compiler_params=pltpu.CompilerParams(vmem_limit_bytes=50 * MIB),
        cost_estimate=pl.CostEstimate(
            flops=2 * count * cycles * degrees * lanes * 2 * 4,
            bytes_accessed=count * (cycles * degrees * 2 + 2 * cycles * lanes * 4),
            transcendentals=0,
        ),
        name="synth",
    )(orders, where, coeffs, weight, legendre)


def core_sum_kernel(keep_ref, other_ref, token_ref, out_ref):
    out_ref[...] = (keep_ref[0] + other_ref[0]).astype(BF16)


def core_sum(keep, other, order):
    shape = keep.shape[1:]
    half = pl.BlockSpec((1,) + shape, lambda t: (1, 0, 0, 0))
    return pl.pallas_call(
        core_sum_kernel,
        grid=(1,),
        in_specs=[half, half, pl.BlockSpec(memory_space=pltpu.SMEM)],
        out_specs=pl.BlockSpec(shape, lambda t: (0, 0, 0)),
        out_shape=jax.ShapeDtypeStruct(shape, BF16),
        compiler_params=pltpu.CompilerParams(vmem_limit_bytes=16 * MIB),
        cost_estimate=pl.CostEstimate(flops=4 * 10**10, bytes_accessed=MIB, transcendentals=0),
        name="core_sum",
    )(keep, other, order)


def full_sum_kernel(token_ref, *refs):
    out_ref = refs[-1]
    start = 0
    for index in range(0, len(refs) - 1, 3):
        keep_ref, other_ref, incoming_ref = refs[index : index + 3]
        count = incoming_ref.shape[1]
        total = keep_ref[0] + other_ref[0] + incoming_ref[...].astype(F32)
        out_ref[:, start : start + count] = total.astype(BF16)
        start += count


def full_sum(chunks, order):
    operands, specs, count = [], [pl.BlockSpec(memory_space=pltpu.SMEM)], 0
    for keep, other, incoming in chunks:
        shape = incoming.shape
        half = pl.BlockSpec((1,) + shape, lambda t: (0, 0, 0, 0))
        operands += [keep, other, incoming]
        specs += [half, half, pl.BlockSpec(shape, lambda t: (0, 0, 0))]
        count += shape[1]
    full = (shape[0], count, shape[2])
    return pl.pallas_call(
        full_sum_kernel,
        grid=(1,),
        in_specs=specs,
        out_specs=pl.BlockSpec(full, lambda t: (0, 0, 0)),
        out_shape=jax.ShapeDtypeStruct(full, BF16),
        compiler_params=pltpu.CompilerParams(vmem_limit_bytes=16 * MIB),
        cost_estimate=pl.CostEstimate(flops=4 * 10**10, bytes_accessed=MIB, transcendentals=0),
        name="full_sum",
    )(order, *operands)


def cycle_kernel(groups, sizes, offset_ref, where_ref, weight_ref, *refs):
    pieces = refs[:groups]
    place_ref, sort_ref, unsort_ref, spread_ref, pixel_ref, back_ref, gather_ref = refs[
        groups : groups + 7
    ]
    outs = refs[groups + 7 : groups + 7 + len(sizes)]
    spread_scr, gather_scr, sorted_scr, middle_scr, product_scr, back_scr, sems = refs[-7:]
    device_count, blocks = place_ref.shape[:2]
    lanes = pieces[0].shape[2] // 2
    turned = offset_ref[where_ref[0]]
    scale = weight_ref[where_ref[0]]
    lane = lax.broadcasted_iota(jnp.int32, (SIDE, lanes), 1)

    def spread_copy(block):
        rows = pl.ds(block * device_count, device_count)
        return pltpu.make_async_copy(
            spread_ref.at[turned, rows], spread_scr.at[rows], sems.at[block]
        )

    gather_copy = pltpu.make_async_copy(gather_ref.at[turned], gather_scr, sems.at[blocks])
    for block in range(blocks):
        spread_copy(block).start()
    gather_copy.start()

    def sort_step(peer, carry):
        slots = jnp.concatenate([piece[peer] for piece in pieces], axis=0)
        sorted_scr[peer] = jnp.dot(
            sort_ref[peer], slots, preferred_element_type=F32
        ).astype(BF16)
        return carry

    lax.fori_loop(0, device_count, sort_step, 0, unroll=2)

    def spread_step(block, carry):
        spread_copy(block).wait()
        rows = pl.ds(pl.multiple_of(block * 32, 32), 32)

        def one(spot):
            picked = jnp.zeros((32, 2 * lanes), BF16)
            for peer in range(device_count):
                place = place_ref[peer, block]
                picked = jnp.where(
                    place == lax.convert_element_type(spot, BF16),
                    sorted_scr[peer, rows, :],
                    picked,
                )
            low_order = block * device_count + spot
            column = jnp.concatenate([picked[:, :lanes], picked[:, lanes:]], axis=0)
            stage = jnp.dot(
                spread_scr[low_order],
                jnp.concatenate([column, column], axis=0),
                preferred_element_type=F32,
            )
            middle_scr[pl.ds(low_order * PADDED, 2 * SIDE), :] = stage

        if device_count <= 8:
            for spot in range(device_count):
                one(spot)
        else:
            lax.fori_loop(0, device_count, lambda s, x: (one(s), x)[1], 0)
        return carry

    lax.fori_loop(0, blocks, spread_step, 0)

    def pixel_step(step, total):
        for inner in range(8):
            first = step * 8 + inner
            column = jnp.concatenate(
                [
                    middle_scr[pl.ds(first, SIDE, stride=PADDED), :],
                    middle_scr[pl.ds(first + SIDE, SIDE, stride=PADDED), :],
                ],
                axis=0,
            )
            high, low = two_parts(column)
            stage = jnp.dot(
                pixel_ref[...], jnp.concatenate([high, low], axis=1), preferred_element_type=F32
            )
            field = stage[:SIDE, :lanes] + stage[:SIDE, lanes:] + stage[SIDE:, :lanes]
            other = pltpu.roll(field, lanes // 2, 1)
            product = other * jnp.where(lane < lanes // 2, other, field)
            product_scr[first] = product
            total = total + jnp.sum(product.reshape(8, 8, lanes), axis=0)
        return total

    total = lax.fori_loop(0, SIDE // 8, pixel_step, jnp.zeros((8, lanes), F32))
    mean = jnp.sum(total, axis=0, keepdims=True) * (1.0 / NPIX)

    def back_step(step, carry):
        for inner in range(8):
            first = step * 8 + inner
            high, low = two_parts(product_scr[first] - mean)
            back_scr[pl.ds(first * PADDED, 2 * SIDE), :] = jnp.dot(
                back_ref[...],
                jnp.concatenate([high, low, high, low], axis=0),
                preferred_element_type=F32,
            )
        return carry

    lax.fori_loop(0, SIDE // 8, back_step, 0)
    gather_copy.wait()

    def gather_step(block, carry):
        rows = pl.ds(pl.multiple_of(block * 32, 32), 32)

        def one(spot):
            low_order = block * device_count + spot
            column = jnp.concatenate(
                [
                    back_scr[pl.ds(low_order, SIDE, stride=PADDED), :],
                    back_scr[pl.ds(low_order + SIDE, SIDE, stride=PADDED), :],
                ],
                axis=0,
            )
            high, low = two_parts(column)
            stage = jnp.dot(
                gather_scr[low_order],
                jnp.concatenate([high, low], axis=1),
                preferred_element_type=F32,
            )
            value = stage[:SIDE, :lanes] + stage[:SIDE, lanes:] + stage[SIDE:, :lanes]
            value = (value * scale).astype(BF16)
            return jnp.concatenate([value[:32], value[32:]], axis=1)

        if device_count <= 8:
            found = [one(spot) for spot in range(device_count)]
            for peer in range(device_count):
                place = place_ref[peer, block]
                picked = found[0]
                for spot in range(1, device_count):
                    picked = jnp.where(place == spot, found[spot], picked)
                sorted_scr[peer, rows, :] = picked
        else:

            def spot_step(spot, carry):
                value = one(spot)
                for peer in range(device_count):
                    sorted_scr[peer, rows, :] = jnp.where(
                        place_ref[peer, block] == lax.convert_element_type(spot, BF16),
                        value,
                        sorted_scr[peer, rows, :],
                    )
                return carry

            lax.fori_loop(0, device_count, spot_step, 0)
        return carry

    lax.fori_loop(0, blocks, gather_step, 0)

    def unsort_step(peer, carry):
        slots = jnp.dot(
            unsort_ref[peer], sorted_scr[peer], preferred_element_type=F32
        ).astype(BF16)
        start = 0
        for out, size in zip(outs, sizes):
            out[peer] = slots[start : start + size]
            start += size
        return carry

    lax.fori_loop(0, device_count, unsort_step, 0, unroll=2)


def cycle_work(pieces, sizes, places, sort, unsort, offset, where, cycle_weight):
    groups = len(pieces)
    device_count, count, lanes = pieces[0].shape
    out_shapes = [(device_count, size, lanes) for size in sizes]
    spread, pixel, back, gather = [jnp.asarray(table) for table in fourier_tables()]
    tables = [places, sort, unsort]
    return pl.pallas_call(
        functools.partial(cycle_kernel, groups, sizes),
        grid_spec=pltpu.PrefetchScalarGridSpec(
            num_scalar_prefetch=2,
            grid=(1,),
            in_specs=[pl.BlockSpec(memory_space=pltpu.SMEM)]
            + [whole(piece.shape) for piece in pieces]
            + [whole(table.shape) for table in tables]
            + [hbm(), whole(pixel.shape), whole(back.shape), hbm()],
            out_specs=[whole(shape) for shape in out_shapes],
            scratch_shapes=[
                pltpu.VMEM(spread.shape[1:], BF16),
                pltpu.VMEM(gather.shape[1:], BF16),
                pltpu.VMEM((device_count, groups * count, lanes), BF16),
                pltpu.VMEM((SIDE * PADDED, lanes // 2), F32),
                pltpu.VMEM((SIDE, SIDE, lanes // 2), F32),
                pltpu.VMEM((SIDE * PADDED, lanes // 2), F32),
                pltpu.SemaphoreType.DMA((places.shape[1] + 1,)),
            ],
        ),
        out_shape=[jax.ShapeDtypeStruct(shape, BF16) for shape in out_shapes],
        compiler_params=pltpu.CompilerParams(vmem_limit_bytes=40 * MIB),
        cost_estimate=pl.CostEstimate(
            flops=4 * SIDE * 128 * 256 * 256 * 2, bytes_accessed=8 * MIB, transcendentals=0
        ),
        name="cycle_work",
    )(offset, where, cycle_weight, *pieces, *tables, spread, pixel, back, gather)


def adjoint_kernel(
    first, order_ref, where_ref, own_ref, core_ref, far_ref, corner_ref, weight_ref, legendre_ref, *refs
):
    out_ref, values_even, values_odd, terms_even, terms_odd = refs[-5:]
    step = pl.program_id(0)
    row = where_ref[0]
    base = where_ref[1] + first + step * BLOCK
    degrees = weight_ref.shape[1]
    cycles = legendre_ref.shape[1]
    owners = cycles // 4
    lanes = weight_ref.shape[0] // 2
    pitch = cycles + 8
    tiles = degrees // 128
    quarter = owners * 16
    degree = row * degrees + lax.broadcasted_iota(jnp.int32, (8, degrees), 1)
    sublane = lax.broadcasted_iota(jnp.int32, (8, degrees), 0)
    sources = (own_ref, core_ref, far_ref, corner_ref)
    for group in range(BLOCK // 16):
        values_scr = values_odd if group % 2 else values_even
        terms_scr = terms_odd if group % 2 else terms_even
        for place in range(16):
            wide = legendre_ref[group * 16 + place].astype(F32)
            for tile in range(tiles):
                values_scr[tile, place * pitch : place * pitch + cycles, :] = wide[
                    :, tile * 128 : tile * 128 + 128
                ]
        for part in range(2):
            for away in range(4):
                rows = sources[away][
                    :, group * 16 : group * 16 + 16, part * lanes : (part + 1) * lanes
                ].reshape(quarter, lanes)
                start = (part * 4 + away) * quarter
                terms_scr[start : start + quarter, :] = jnp.dot(
                    jnp.concatenate([rows, rows], axis=1),
                    weight_ref[...],
                    preferred_element_type=F32,
                )
        for half in range(2):
            total = [jnp.zeros((8, degrees), F32), jnp.zeros((8, degrees), F32)]
            for away in range(4):
                for owner in range(owners):
                    cycle = 4 * owner + (row ^ away)
                    factor = jnp.concatenate(
                        [
                            values_scr[tile, pl.ds(half * 8 * pitch + cycle, 8, stride=pitch), :]
                            for tile in range(tiles)
                        ],
                        axis=1,
                    )
                    for part in range(2):
                        at = (part * 4 + away) * quarter + owner * 16 + half * 8
                        total[part] = total[part] + terms_scr[at : at + 8, :] * factor
            lowest = jnp.zeros((8, degrees), jnp.int32)
            first_slot = group * 16 + half * 8
            for place in range(8):
                lowest = jnp.where(sublane == place, order_ref[base + first_slot + place], lowest)
            for part in range(2):
                out_ref[part, first_slot : first_slot + 8, :] = jnp.where(
                    degree >= lowest, total[part], 0.0
                )


def adjoint(first, orders, where, weight, pieces, legendre, earlier):
    orders_here, cycles, degrees = legendre.shape
    count = pieces[0].shape[1]
    steps = count // BLOCK
    start = first // BLOCK
    owners = cycles // 4
    lanes = weight.shape[0] // 2
    piece_spec = pl.BlockSpec((owners, BLOCK, 2 * lanes), lambda t, *_: (0, t, 0))
    out = jax.ShapeDtypeStruct((2, orders_here, degrees), F32)
    return pl.pallas_call(
        functools.partial(adjoint_kernel, first),
        grid_spec=pltpu.PrefetchScalarGridSpec(
            num_scalar_prefetch=2,
            grid=(steps,),
            in_specs=[piece_spec] * 4
            + [
                whole(weight.shape),
                pl.BlockSpec((BLOCK, cycles, degrees), lambda t, *_: (start + t, 0, 0)),
            ]
            + [anywhere()] * len(earlier),
            out_specs=pl.BlockSpec((2, BLOCK, degrees), lambda t, *_: (0, start + t, 0)),
            scratch_shapes=[
                pltpu.VMEM((degrees // 128, 16 * (cycles + 8), 128), F32),
                pltpu.VMEM((degrees // 128, 16 * (cycles + 8), 128), F32),
                pltpu.VMEM((32 * cycles, degrees), F32),
                pltpu.VMEM((32 * cycles, degrees), F32),
            ],
        ),
        out_shape=out,
        input_output_aliases={8: 0} if earlier else {},
        compiler_params=pltpu.CompilerParams(vmem_limit_bytes=40 * MIB),
        cost_estimate=pl.CostEstimate(
            flops=2 * count * cycles * degrees * lanes * 2 * 2,
            bytes_accessed=count * (cycles * degrees * 2 + 2 * cycles * lanes * 2),
            transcendentals=0,
        ),
        name="adjoint",
    )(orders, where, *pieces, weight, legendre, *earlier)


def slot_tables(orders, device_count):
    local_orders = orders.shape[0] // device_count
    blocks = local_orders // 32
    by_device = orders.reshape(device_count, local_orders)
    block = by_device // device_count
    position = 32 * (block % blocks) + block // blocks
    wanted = jnp.arange(local_orders, dtype=jnp.int32)
    sort = position[:, None, :] == wanted[None, :, None]
    unsort = position[:, :, None] == wanted[None, None, :]
    place = jnp.sum(jnp.where(sort, (by_device % device_count)[:, None, :], 0), axis=2)
    place = place.reshape(device_count, blocks, 32, 1)
    place = jnp.broadcast_to(place, (device_count, blocks, 32, 256))
    return place.astype(BF16), sort.astype(BF16), unsort.astype(BF16)


def body(
    coeffs,
    legendre,
    alpha_table,
    beta_table,
    radial_weight,
    radius_index,
    orders,
    cycle_offset,
    cycle_weight,
):
    row_id = lax.axis_index("row")
    ma_id = lax.axis_index("ma")
    device_count = lax.axis_size("ma")
    row_count = lax.axis_size("row")
    local_orders = coeffs.shape[1]
    where = jnp.stack([row_id, ma_id * local_orders]).astype(jnp.int32)
    places, sort, unsort = slot_tables(orders, device_count)
    synth_weight, adjoint_weight = filter_weights(
        radius_index, radial_weight, alpha_table, beta_table
    )
    core_pairs = [(i, i ^ 1) for i in range(row_count)]
    far_pairs = [(i, i ^ 2) for i in range(row_count)]
    chunks = min(CHUNKS, local_orders // 32)
    groups = min(GROUPS, chunks)
    size = chunks // groups
    kept, others, outgoing, incoming, arrived = [], [], [], [], []

    def after(*values):
        return lax.optimization_barrier((where, *values))[0]

    def launch(chunk, token):
        keep, send = synth(chunk, chunks, orders, token, coeffs, synth_weight, legendre)
        kept.append(keep)
        others.append(lax.ppermute(send, "row", core_pairs))

    def pass_on(chunk, token):
        outgoing.append(core_sum(kept[chunk], others[chunk], token))
        incoming.append(lax.ppermute(outgoing[chunk], "row", far_pairs))

    def deliver(group, token):
        own = slice(group * size, (group + 1) * size)
        summed = full_sum(list(zip(kept[own], others[own], incoming[own])), token)
        arrived.append(lax.all_to_all(summed, "ma", split_axis=0, concat_axis=0, tiled=True))
        return summed

    if chunks == 4:
        launch(0, where)
        launch(1, where)
        pass_on(0, after(kept[1]))
        places, sort, unsort, token = lax.optimization_barrier((places, sort, unsort, where))
        launch(2, lax.optimization_barrier((token, outgoing[0]))[0])
        pass_on(1, after(kept[2]))
        pass_on(2, after(outgoing[1]))
        launch(3, after(outgoing[2], incoming[0]))
        summed = deliver(0, after(kept[3]))
        pass_on(3, after(summed))
        deliver(1, after(outgoing[3]))
    else:
        for chunk in range(chunks):
            launch(chunk, where)
        for chunk in range(chunks):
            pass_on(chunk, after(kept[-1]))
        for group in range(groups):
            deliver(group, after(outgoing[-1]))
    units = local_orders // 32
    early = 32 * ((5 * units) // 8)
    sizes = (early, local_orders - early)
    analysed = cycle_work(
        arrived, sizes, places, sort, unsort, cycle_offset, where, cycle_weight
    )
    own = [
        lax.all_to_all(piece, "ma", split_axis=0, concat_axis=0, tiled=True) for piece in analysed
    ]
    far = lax.ppermute(own[0], "row", far_pairs)
    far, second = lax.optimization_barrier((far, own[1]))
    gradient, first = [], 0
    for own_part, far_part in ((own[0], far), (second, None)):
        if far_part is None:
            far_part = lax.ppermute(own_part, "row", far_pairs)
        if gradient:
            far_part, gradient[-1] = lax.optimization_barrier((far_part, gradient[-1]))
        core = lax.ppermute(own_part, "row", core_pairs)
        corner = lax.ppermute(far_part, "row", core_pairs)
        gradient.append(
            adjoint(
                first,
                orders,
                where,
                adjoint_weight,
                (own_part, core, far_part, corner),
                legendre,
                gradient[-1:],
            )
        )
        first += own_part.shape[1]
    return gradient[-1]


def solution(mesh):
    in_specs = (
        P(None, "ma", "row"),
        P("ma", None, "row"),
        P(None, "row"),
        P(None, "row"),
        P(),
        P(),
        P(),
        P("ma"),
        P("ma"),
    )
    out_specs = P(None, "ma", "row")
    return jax.shard_map(body, mesh=mesh, in_specs=in_specs, out_specs=out_specs, check_vma=False)
```

```python
import functools
import math

import jax
import jax.numpy as jnp
import numpy as np
from jax import lax
from jax.experimental import pallas as pl
from jax.experimental.pallas import tpu as pltpu
from jax.sharding import PartitionSpec as P

NPIX = 4096
SIDE = 64
PADDED = 136
SYNTH_BLOCK = 16
BLOCK = 32
MIB = 1 << 20
F32 = jnp.float32
BF16 = jnp.bfloat16


def split_table(table):
    high = table.astype(jnp.bfloat16)
    low = (table - high.astype(np.float64)).astype(jnp.bfloat16)
    return high, low


@functools.lru_cache(maxsize=None)
def fourier_tables():
    first = np.arange(SIDE)
    spin = np.arange(2).reshape(2, 1, 1, 1, 1, 1)
    order = SIDE * np.arange(32)[None, :] + np.arange(SIDE)[:, None]
    order = order.reshape(1, SIDE, 1, 1, 1, 32)
    angle = (2 * first.reshape(1, 1, 1, SIDE, 1, 1) + spin) * order % (2 * NPIX) * (math.pi / NPIX)
    cosine, sine = np.cos(angle), np.sin(angle)
    row_part = np.arange(2).reshape(1, 1, 2, 1, 1, 1)
    col_part = np.arange(2).reshape(1, 1, 1, 1, 2, 1)
    same = (row_part == col_part).astype(np.float64)
    cross = np.where(row_part == 1, 1.0, -1.0) * (row_part != col_part)
    doubling = np.where(order == 0, 1.0, 2.0)
    spread = (doubling * (same * cosine + cross * sine)).reshape(2, SIDE, 2 * SIDE, SIDE)
    gather = (same * cosine + cross * sine).reshape(2, SIDE, 2 * SIDE, SIDE)
    gather = np.swapaxes(gather, 2, 3)
    spread_parts = np.concatenate(split_table(spread), axis=3)
    gather_parts = np.concatenate(split_table(gather), axis=2)
    square = first[:, None] * first[None, :] % SIDE * (2.0 * math.pi / SIDE)
    pixel = np.concatenate(split_table(np.concatenate([np.cos(square), -np.sin(square)], axis=1)), axis=0)
    back_high, back_low = split_table(np.concatenate([np.cos(square), -np.sin(square)], axis=0))
    back = np.concatenate([back_high, back_high, back_low, back_low], axis=1)
    return spread_parts, pixel, back, gather_parts


def two_parts(value):
    high = value.astype(BF16)
    low = (value - high.astype(F32)).astype(BF16)
    return high, low


def whole(shape):
    return pl.BlockSpec(shape, lambda t, *_: (0,) * len(shape))


def anywhere():
    return pl.BlockSpec(memory_space=pl.ANY)


def hbm():
    return pl.BlockSpec(memory_space=pltpu.HBM)


def weights_kernel(
    node_ref,
    radial_ref,
    alpha_ref,
    beta_ref,
    synth_ref,
    adjoint_ref,
    alpha_scr,
    beta_scr,
    filter_scr,
    weighted_scr,
    sems,
):
    copies = [
        pltpu.make_async_copy(alpha_ref, alpha_scr, sems.at[0]),
        pltpu.make_async_copy(beta_ref, beta_scr, sems.at[1]),
    ]
    for copy in copies:
        copy.start()
    for copy in copies:
        copy.wait()
    radii = node_ref.shape[0]

    def gather(radius, carry):
        node = node_ref[radius]
        scale = radial_ref[node]
        alpha = alpha_scr[pl.ds(node, 1), :]
        beta = beta_scr[pl.ds(node, 1), :]
        filter_scr[pl.ds(radius, 1), :] = alpha
        filter_scr[pl.ds(radii + radius, 1), :] = beta
        weighted_scr[pl.ds(radius, 1), :] = scale * alpha
        weighted_scr[pl.ds(radii + radius, 1), :] = (2.0 * scale) * beta
        return carry

    lax.fori_loop(0, radii, gather, 0, unroll=8)
    high, low = two_parts(filter_scr[...].T)
    synth_ref[:, : 2 * radii] = high
    synth_ref[:, 2 * radii :] = low
    high, low = two_parts(weighted_scr[...])
    adjoint_ref[: 2 * radii, :] = high
    adjoint_ref[2 * radii :, :] = low


def filter_weights(radius_index, radial_weight, alpha_table, beta_table):
    radii = radius_index.shape[0]
    degrees = alpha_table.shape[1]
    return pl.pallas_call(
        weights_kernel,
        grid_spec=pltpu.PrefetchScalarGridSpec(
            num_scalar_prefetch=2,
            grid=(1,),
            in_specs=[hbm(), hbm()],
            out_specs=[whole((degrees, 4 * radii)), whole((4 * radii, degrees))],
            scratch_shapes=[pltpu.VMEM(alpha_table.shape, F32)] * 2
            + [pltpu.VMEM((2 * radii, degrees), F32)] * 2
            + [pltpu.SemaphoreType.DMA((2,))],
        ),
        out_shape=[
            jax.ShapeDtypeStruct((degrees, 4 * radii), BF16),
            jax.ShapeDtypeStruct((4 * radii, degrees), BF16),
        ],
        compiler_params=pltpu.CompilerParams(vmem_limit_bytes=56 * MIB),
        name="filter_weights",
    )(radius_index, radial_weight, alpha_table, beta_table)


def synth_kernel(
    first, order_ref, where_ref, coeffs_ref, weight_ref, legendre_ref, *refs
):
    keep_ref, send_ref, terms_even, terms_odd, sums_even, sums_odd = refs[-6:]
    step = pl.program_id(0)
    row = where_ref[0]
    base = where_ref[1] + first + step * SYNTH_BLOCK
    degrees = coeffs_ref.shape[2]
    cycles = legendre_ref.shape[1]
    owners = cycles // 4
    lanes = weight_ref.shape[1] // 2
    degree = row * degrees + lax.broadcasted_iota(jnp.int32, (1, degrees), 1)
    for group in range(SYNTH_BLOCK // 8):
        terms = terms_odd if group % 2 else terms_even
        sums = sums_odd if group % 2 else sums_even
        for place in range(8):
            slot = group * 8 + place
            live = degree >= order_ref[base + slot]
            values = legendre_ref[slot].astype(F32)
            for part in range(2):
                coeff = jnp.where(live, coeffs_ref[part, slot : slot + 1, :], 0.0)
                high, low = two_parts(values * coeff)
                start = (part * 8 + place) * cycles
                terms[0, start : start + cycles, :] = high
                terms[1, start : start + cycles, :] = low
        both = jnp.dot(terms[0], weight_ref[...], preferred_element_type=F32)
        rest = jnp.dot(terms[1], weight_ref[:, :lanes], preferred_element_type=F32)
        sums[...] = both[:, :lanes] + both[:, lanes:] + rest
        for part in range(2):
            for owner in range(owners):
                for away in range(4):
                    cycle = 4 * owner + (row ^ away)
                    piece = sums[pl.ds(part * 8 * cycles + cycle, 8, stride=cycles), :]
                    target = send_ref if away % 2 else keep_ref
                    target[
                        away // 2,
                        owner,
                        group * 8 : group * 8 + 8,
                        part * lanes : (part + 1) * lanes,
                    ] = piece


def synth(first, count, orders, where, coeffs, weight, legendre):
    cycles, degrees = legendre.shape[1:]
    steps = count // SYNTH_BLOCK
    start = first // SYNTH_BLOCK
    owners = cycles // 4
    lanes = weight.shape[1] // 2
    out = jax.ShapeDtypeStruct((2, owners, count, 2 * lanes), F32)
    out_spec = pl.BlockSpec((2, owners, SYNTH_BLOCK, 2 * lanes), lambda t, *_: (0, 0, t, 0))
    return pl.pallas_call(
        functools.partial(synth_kernel, first),
        grid_spec=pltpu.PrefetchScalarGridSpec(
            num_scalar_prefetch=2,
            grid=(steps,),
            in_specs=[
                pl.BlockSpec((2, SYNTH_BLOCK, degrees), lambda t, *_: (0, start + t, 0)),
                whole(weight.shape),
                pl.BlockSpec((SYNTH_BLOCK, cycles, degrees), lambda t, *_: (start + t, 0, 0)),
            ],
            out_specs=[out_spec, out_spec],
            scratch_shapes=[
                pltpu.VMEM((2, 16 * cycles, degrees), BF16),
                pltpu.VMEM((2, 16 * cycles, degrees), BF16),
                pltpu.VMEM((16 * cycles, lanes), F32),
                pltpu.VMEM((16 * cycles, lanes), F32),
            ],
        ),
        out_shape=[out, out],
        compiler_params=pltpu.CompilerParams(vmem_limit_bytes=48 * MIB),
        cost_estimate=pl.CostEstimate(
            flops=2 * count * cycles * degrees * lanes * 2 * 4,
            bytes_accessed=count * (cycles * degrees * 2 + 2 * cycles * lanes * 4),
            transcendentals=0,
        ),
        name="synth",
    )(orders, where, coeffs, weight, legendre)


def core_sum_kernel(keep_ref, other_ref, token_ref, out_ref):
    out_ref[...] = (keep_ref[0] + other_ref[0]).astype(BF16)


def core_sum(keep, other, order):
    shape = keep.shape[1:]
    half = pl.BlockSpec((1,) + shape, lambda t: (1, 0, 0, 0))
    return pl.pallas_call(
        core_sum_kernel,
        grid=(1,),
        in_specs=[half, half, pl.BlockSpec(memory_space=pltpu.SMEM)],
        out_specs=pl.BlockSpec(shape, lambda t: (0, 0, 0)),
        out_shape=jax.ShapeDtypeStruct(shape, BF16),
        compiler_params=pltpu.CompilerParams(vmem_limit_bytes=16 * MIB),
        cost_estimate=pl.CostEstimate(flops=4 * 10**10, bytes_accessed=MIB, transcendentals=0),
        name="core_sum",
    )(keep, other, order)


def full_sum_kernel(token_ref, *refs):
    out_ref = refs[-1]
    start = 0
    for index in range(0, len(refs) - 1, 3):
        keep_ref, other_ref, incoming_ref = refs[index : index + 3]
        count = incoming_ref.shape[1]
        total = keep_ref[0] + other_ref[0] + incoming_ref[...].astype(F32)
        out_ref[:, start : start + count] = total.astype(BF16)
        start += count


def full_sum(chunks, order):
    operands, specs, count = [], [pl.BlockSpec(memory_space=pltpu.SMEM)], 0
    for keep, other, incoming in chunks:
        shape = incoming.shape
        half = pl.BlockSpec((1,) + shape, lambda t: (0, 0, 0, 0))
        operands += [keep, other, incoming]
        specs += [half, half, pl.BlockSpec(shape, lambda t: (0, 0, 0))]
        count += shape[1]
    full = (shape[0], count, shape[2])
    return pl.pallas_call(
        full_sum_kernel,
        grid=(1,),
        in_specs=specs,
        out_specs=pl.BlockSpec(full, lambda t: (0, 0, 0)),
        out_shape=jax.ShapeDtypeStruct(full, BF16),
        compiler_params=pltpu.CompilerParams(vmem_limit_bytes=16 * MIB),
        cost_estimate=pl.CostEstimate(flops=4 * 10**10, bytes_accessed=MIB, transcendentals=0),
        name="full_sum",
    )(order, *operands)


def cycle_kernel(groups, sizes, offset_ref, where_ref, weight_ref, *refs):
    arrived = refs[:groups]
    places_ref, sorts_ref, unsorts_ref, spread_ref, pixel_ref, back_ref, gather_ref = refs[
        groups : groups + 7
    ]
    results = refs[groups + 7 : groups + 7 + len(sizes)]
    scratch = refs[groups + 7 + len(sizes) :]
    pieces = scratch[:groups]
    outs = scratch[groups : groups + len(sizes)]
    (
        place_ref,
        sort_ref,
        unsort_ref,
        spread_scr,
        gather_scr,
        sorted_scr,
        middle_scr,
        product_scr,
        back_scr,
        sems,
        input_sems,
        out_sems,
    ) = scratch[groups + len(sizes) :]
    device_count, blocks = place_ref.shape[:2]
    lanes = pieces[0].shape[2] // 2
    inputs = [
        pltpu.make_async_copy(source, target, input_sems.at[index])
        for index, (source, target) in enumerate(
            [
                *zip(arrived, pieces),
                (sorts_ref, sort_ref),
                (places_ref, place_ref),
                (unsorts_ref, unsort_ref),
            ]
        )
    ]
    for copy in inputs[:-1]:
        copy.start()
    turned = offset_ref[where_ref[0]]
    scale = weight_ref[where_ref[0]]
    lane = lax.broadcasted_iota(jnp.int32, (SIDE, lanes), 1)

    def spread_copy(block):
        rows = pl.ds(block * device_count, device_count)
        return pltpu.make_async_copy(
            spread_ref.at[turned, rows], spread_scr.at[rows], sems.at[block]
        )

    gather_copy = pltpu.make_async_copy(gather_ref.at[turned], gather_scr, sems.at[blocks])
    for block in range(blocks):
        spread_copy(block).start()
    gather_copy.start()
    inputs[-1].start()
    for copy in inputs[: groups + 1]:
        copy.wait()

    def sort_step(peer, carry):
        slots = jnp.concatenate([piece[peer] for piece in pieces], axis=0)
        sorted_scr[peer] = jnp.dot(
            sort_ref[peer], slots, preferred_element_type=F32
        ).astype(BF16)
        return carry

    lax.fori_loop(0, device_count, sort_step, 0, unroll=2)
    inputs[groups + 1].wait()

    def spread_step(block, carry):
        spread_copy(block).wait()
        rows = pl.ds(pl.multiple_of(block * 32, 32), 32)

        def one(spot):
            picked = jnp.zeros((32, 2 * lanes), BF16)
            for peer in range(device_count):
                place = place_ref[peer, block]
                picked = jnp.where(
                    place == lax.convert_element_type(spot, BF16),
                    sorted_scr[peer, rows, :],
                    picked,
                )
            low_order = block * device_count + spot
            column = jnp.concatenate([picked[:, :lanes], picked[:, lanes:]], axis=0)
            stage = jnp.dot(
                spread_scr[low_order],
                jnp.concatenate([column, column], axis=0),
                preferred_element_type=F32,
            )
            middle_scr[pl.ds(low_order * PADDED, 2 * SIDE), :] = stage

        if device_count <= 8:
            for spot in range(device_count):
                one(spot)
        else:
            lax.fori_loop(0, device_count, lambda s, x: (one(s), x)[1], 0)
        return carry

    lax.fori_loop(0, blocks, spread_step, 0)

    def pixel_step(step, total):
        for inner in range(8):
            first = step * 8 + inner
            column = jnp.concatenate(
                [
                    middle_scr[pl.ds(first, SIDE, stride=PADDED), :],
                    middle_scr[pl.ds(first + SIDE, SIDE, stride=PADDED), :],
                ],
                axis=0,
            )
            high, low = two_parts(column)
            stage = jnp.dot(
                pixel_ref[...], jnp.concatenate([high, low], axis=1), preferred_element_type=F32
            )
            field = stage[:SIDE, :lanes] + stage[:SIDE, lanes:] + stage[SIDE:, :lanes]
            other = pltpu.roll(field, lanes // 2, 1)
            product = other * jnp.where(lane < lanes // 2, other, field)
            product_scr[first] = product
            total = total + jnp.sum(product.reshape(8, 8, lanes), axis=0)
        return total

    total = lax.fori_loop(0, SIDE // 8, pixel_step, jnp.zeros((8, lanes), F32))
    mean = jnp.sum(total, axis=0, keepdims=True) * (1.0 / NPIX)

    def back_step(step, carry):
        for inner in range(8):
            first = step * 8 + inner
            high, low = two_parts(product_scr[first] - mean)
            back_scr[pl.ds(first * PADDED, 2 * SIDE), :] = jnp.dot(
                back_ref[...],
                jnp.concatenate([high, low, high, low], axis=0),
                preferred_element_type=F32,
            )
        return carry

    lax.fori_loop(0, SIDE // 8, back_step, 0)
    gather_copy.wait()

    def gather_step(block, carry):
        rows = pl.ds(pl.multiple_of(block * 32, 32), 32)

        def one(spot):
            low_order = block * device_count + spot
            column = jnp.concatenate(
                [
                    back_scr[pl.ds(low_order, SIDE, stride=PADDED), :],
                    back_scr[pl.ds(low_order + SIDE, SIDE, stride=PADDED), :],
                ],
                axis=0,
            )
            high, low = two_parts(column)
            stage = jnp.dot(
                gather_scr[low_order],
                jnp.concatenate([high, low], axis=1),
                preferred_element_type=F32,
            )
            value = stage[:SIDE, :lanes] + stage[:SIDE, lanes:] + stage[SIDE:, :lanes]
            value = (value * scale).astype(BF16)
            return jnp.concatenate([value[:32], value[32:]], axis=1)

        if device_count <= 8:
            found = [one(spot) for spot in range(device_count)]
            for peer in range(device_count):
                place = place_ref[peer, block]
                picked = found[0]
                for spot in range(1, device_count):
                    picked = jnp.where(place == spot, found[spot], picked)
                sorted_scr[peer, rows, :] = picked
        else:

            def spot_step(spot, carry):
                value = one(spot)
                for peer in range(device_count):
                    sorted_scr[peer, rows, :] = jnp.where(
                        place_ref[peer, block] == lax.convert_element_type(spot, BF16),
                        value,
                        sorted_scr[peer, rows, :],
                    )
                return carry

            lax.fori_loop(0, device_count, spot_step, 0)
        return carry

    lax.fori_loop(0, blocks, gather_step, 0)
    inputs[-1].wait()

    def result_copy(peer, index):
        return pltpu.make_async_copy(
            outs[index].at[peer], results[index].at[peer], out_sems.at[index, peer]
        )

    def unsort_step(peer, carry):
        slots = jnp.dot(
            unsort_ref[peer], sorted_scr[peer], preferred_element_type=F32
        ).astype(BF16)
        start = 0
        for index, size in enumerate(sizes):
            outs[index][peer] = slots[start : start + size]
            start += size
            result_copy(peer, index).start()
        return carry

    lax.fori_loop(0, device_count, unsort_step, 0, unroll=2)
    for index in range(len(sizes)):
        for peer in range(device_count):
            result_copy(peer, index).wait()


def cycle_work(pieces, sizes, places, sort, unsort, offset, where, cycle_weight):
    groups = len(pieces)
    device_count, count, lanes = pieces[0].shape
    out_shapes = [(device_count, size, lanes) for size in sizes]
    spread, pixel, back, gather = [jnp.asarray(table) for table in fourier_tables()]
    tables = [places, sort, unsort]
    return pl.pallas_call(
        functools.partial(cycle_kernel, groups, sizes),
        grid_spec=pltpu.PrefetchScalarGridSpec(
            num_scalar_prefetch=2,
            grid=(1,),
            in_specs=[pl.BlockSpec(memory_space=pltpu.SMEM)]
            + [anywhere()] * (groups + 4)
            + [whole(pixel.shape), whole(back.shape), anywhere()],
            out_specs=[anywhere()] * len(sizes),
            scratch_shapes=[pltpu.VMEM(piece.shape, BF16) for piece in pieces]
            + [pltpu.VMEM(shape, BF16) for shape in out_shapes]
            + [pltpu.VMEM(table.shape, BF16) for table in tables]
            + [
                pltpu.VMEM(spread.shape[1:], BF16),
                pltpu.VMEM(gather.shape[1:], BF16),
                pltpu.VMEM((device_count, groups * count, lanes), BF16),
                pltpu.VMEM((SIDE * PADDED, lanes // 2), F32),
                pltpu.VMEM((SIDE, SIDE, lanes // 2), F32),
                pltpu.VMEM((SIDE * PADDED, lanes // 2), F32),
                pltpu.SemaphoreType.DMA((places.shape[1] + 1,)),
                pltpu.SemaphoreType.DMA((groups + 3,)),
                pltpu.SemaphoreType.DMA((len(sizes), device_count)),
            ],
        ),
        out_shape=[jax.ShapeDtypeStruct(shape, BF16) for shape in out_shapes],
        compiler_params=pltpu.CompilerParams(vmem_limit_bytes=48 * MIB),
        cost_estimate=pl.CostEstimate(
            flops=4 * SIDE * 128 * 256 * 256 * 2, bytes_accessed=8 * MIB, transcendentals=0
        ),
        name="cycle_work",
    )(offset, where, cycle_weight, *pieces, *tables, spread, pixel, back, gather)


def adjoint_kernel(
    first, order_ref, where_ref, own_ref, core_ref, far_ref, corner_ref, weight_ref, legendre_ref, *refs
):
    out_ref, values_even, values_odd, terms_even, terms_odd = refs[-5:]
    step = pl.program_id(0)
    row = where_ref[0]
    base = where_ref[1] + first + step * BLOCK
    degrees = weight_ref.shape[1]
    cycles = legendre_ref.shape[1]
    owners = cycles // 4
    lanes = weight_ref.shape[0] // 2
    pitch = cycles + 8
    tiles = degrees // 128
    quarter = owners * 16
    degree = row * degrees + lax.broadcasted_iota(jnp.int32, (8, degrees), 1)
    sublane = lax.broadcasted_iota(jnp.int32, (8, degrees), 0)
    sources = (own_ref, core_ref, far_ref, corner_ref)
    for group in range(BLOCK // 16):
        values_scr = values_odd if group % 2 else values_even
        terms_scr = terms_odd if group % 2 else terms_even
        for place in range(16):
            wide = legendre_ref[group * 16 + place].astype(F32)
            for tile in range(tiles):
                values_scr[tile, place * pitch : place * pitch + cycles, :] = wide[
                    :, tile * 128 : tile * 128 + 128
                ]
        for part in range(2):
            for away in range(4):
                rows = sources[away][
                    :, group * 16 : group * 16 + 16, part * lanes : (part + 1) * lanes
                ].reshape(quarter, lanes)
                start = (part * 4 + away) * quarter
                terms_scr[start : start + quarter, :] = jnp.dot(
                    jnp.concatenate([rows, rows], axis=1),
                    weight_ref[...],
                    preferred_element_type=F32,
                )
        for half in range(2):
            total = [jnp.zeros((8, degrees), F32), jnp.zeros((8, degrees), F32)]
            for away in range(4):
                for owner in range(owners):
                    cycle = 4 * owner + (row ^ away)
                    factor = jnp.concatenate(
                        [
                            values_scr[tile, pl.ds(half * 8 * pitch + cycle, 8, stride=pitch), :]
                            for tile in range(tiles)
                        ],
                        axis=1,
                    )
                    for part in range(2):
                        at = (part * 4 + away) * quarter + owner * 16 + half * 8
                        total[part] = total[part] + terms_scr[at : at + 8, :] * factor
            lowest = jnp.zeros((8, degrees), jnp.int32)
            first_slot = group * 16 + half * 8
            for place in range(8):
                lowest = jnp.where(sublane == place, order_ref[base + first_slot + place], lowest)
            for part in range(2):
                out_ref[part, first_slot : first_slot + 8, :] = jnp.where(
                    degree >= lowest, total[part], 0.0
                )


def adjoint(first, orders, where, weight, pieces, legendre, earlier):
    orders_here, cycles, degrees = legendre.shape
    count = pieces[0].shape[1]
    steps = count // BLOCK
    start = first // BLOCK
    owners = cycles // 4
    lanes = weight.shape[0] // 2
    piece_spec = pl.BlockSpec((owners, BLOCK, 2 * lanes), lambda t, *_: (0, t, 0))
    out = jax.ShapeDtypeStruct((2, orders_here, degrees), F32)
    return pl.pallas_call(
        functools.partial(adjoint_kernel, first),
        grid_spec=pltpu.PrefetchScalarGridSpec(
            num_scalar_prefetch=2,
            grid=(steps,),
            in_specs=[piece_spec] * 4
            + [
                whole(weight.shape),
                pl.BlockSpec((BLOCK, cycles, degrees), lambda t, *_: (start + t, 0, 0)),
            ]
            + [anywhere()] * len(earlier),
            out_specs=pl.BlockSpec((2, BLOCK, degrees), lambda t, *_: (0, start + t, 0)),
            scratch_shapes=[
                pltpu.VMEM((degrees // 128, 16 * (cycles + 8), 128), F32),
                pltpu.VMEM((degrees // 128, 16 * (cycles + 8), 128), F32),
                pltpu.VMEM((32 * cycles, degrees), F32),
                pltpu.VMEM((32 * cycles, degrees), F32),
            ],
        ),
        out_shape=out,
        input_output_aliases={8: 0} if earlier else {},
        compiler_params=pltpu.CompilerParams(vmem_limit_bytes=48 * MIB),
        cost_estimate=pl.CostEstimate(
            flops=2 * count * cycles * degrees * lanes * 2 * 2,
            bytes_accessed=count * (cycles * degrees * 2 + 2 * cycles * lanes * 2),
            transcendentals=0,
        ),
        name="adjoint",
    )(orders, where, *pieces, weight, legendre, *earlier)


def slot_tables(orders, device_count):
    local_orders = orders.shape[0] // device_count
    blocks = local_orders // 32
    by_device = orders.reshape(device_count, local_orders)
    block = by_device // device_count
    position = 32 * (block % blocks) + block // blocks
    wanted = jnp.arange(local_orders, dtype=jnp.int32)
    sort = position[:, None, :] == wanted[None, :, None]
    unsort = position[:, :, None] == wanted[None, None, :]
    place = jnp.sum(jnp.where(sort, (by_device % device_count)[:, None, :], 0), axis=2)
    place = place.reshape(device_count, blocks, 32, 1)
    place = jnp.broadcast_to(place, (device_count, blocks, 32, 256))
    return place.astype(BF16), sort.astype(BF16), unsort.astype(BF16)


def body(
    coeffs,
    legendre,
    alpha_table,
    beta_table,
    radial_weight,
    radius_index,
    orders,
    cycle_offset,
    cycle_weight,
):
    row_id = lax.axis_index("row")
    ma_id = lax.axis_index("ma")
    device_count = lax.axis_size("ma")
    row_count = lax.axis_size("row")
    local_orders = coeffs.shape[1]
    where = jnp.stack([row_id, ma_id * local_orders]).astype(jnp.int32)
    places, sort, unsort = slot_tables(orders, device_count)
    synth_weight, adjoint_weight = filter_weights(
        radius_index, radial_weight, alpha_table, beta_table
    )
    core_pairs = [(i, i ^ 1) for i in range(row_count)]
    far_pairs = [(i, i ^ 2) for i in range(row_count)]
    units = local_orders // 32
    counts = (units // 4, units // 4, units // 2) if units >= 4 else (units // 2, units // 2)
    counts = [32 * count for count in counts]
    kept, others, outgoing, incoming, arrived = [], [], [], [], []

    def after(*values):
        return lax.optimization_barrier((where, *values))[0]

    def launch(chunk, token):
        first = sum(counts[:chunk])
        keep, send = synth(
            first, counts[chunk], orders, token, coeffs, synth_weight, legendre
        )
        kept.append(keep)
        others.append(lax.ppermute(send, "row", core_pairs))

    def pass_on(chunk, token):
        outgoing.append(core_sum(kept[chunk], others[chunk], token))
        incoming.append(lax.ppermute(outgoing[chunk], "row", far_pairs))

    def deliver(own, token):
        summed = full_sum(list(zip(kept[own], others[own], incoming[own])), token)
        arrived.append(lax.all_to_all(summed, "ma", split_axis=0, concat_axis=0, tiled=True))
        return summed

    launch(0, where)
    launch(1, where)
    pass_on(0, after(kept[1]))
    pass_on(1, after(outgoing[0]))
    if len(counts) == 3:
        launch(2, after(outgoing[1]))
        places, sort, unsort, token = lax.optimization_barrier(
            (places, sort, unsort, after(kept[2]))
        )
        pass_on(2, after(deliver(slice(0, 2), token)))
        deliver(slice(2, 3), after(outgoing[2]))
    else:
        deliver(slice(0, 1), after(outgoing[1]))
        deliver(slice(1, 2), after(outgoing[1]))
    early = 32 * ((5 * units) // 8)
    sizes = (early, local_orders - early)
    analysed = cycle_work(
        arrived, sizes, places, sort, unsort, cycle_offset, where, cycle_weight
    )
    own = [
        lax.all_to_all(piece, "ma", split_axis=0, concat_axis=0, tiled=True) for piece in analysed
    ]
    far = lax.ppermute(own[0], "row", far_pairs)
    far, second = lax.optimization_barrier((far, own[1]))
    gradient, first = [], 0
    for own_part, far_part in ((own[0], far), (second, None)):
        if far_part is None:
            far_part = lax.ppermute(own_part, "row", far_pairs)
        if gradient:
            far_part, gradient[-1] = lax.optimization_barrier((far_part, gradient[-1]))
        core = lax.ppermute(own_part, "row", core_pairs)
        corner = lax.ppermute(far_part, "row", core_pairs)
        gradient.append(
            adjoint(
                first,
                orders,
                where,
                adjoint_weight,
                (own_part, core, far_part, corner),
                legendre,
                gradient[-1:],
            )
        )
        first += own_part.shape[1]
    return gradient[-1]


def solution(mesh):
    in_specs = (
        P(None, "ma", "row"),
        P("ma", None, "row"),
        P(None, "row"),
        P(None, "row"),
        P(),
        P(),
        P(),
        P("ma"),
        P("ma"),
    )
    out_specs = P(None, "ma", "row")
    return jax.shard_map(body, mesh=mesh, in_specs=in_specs, out_specs=out_specs, check_vma=False)
```

```python
import functools
import math

import jax
import jax.numpy as jnp
import numpy as np
from jax import lax
from jax.experimental import pallas as pl
from jax.experimental.pallas import tpu as pltpu
from jax.sharding import PartitionSpec as P

NPIX = 4096
SIDE = 64
PADDED = 136
SYNTH_BLOCK = 16
BLOCK = 32
MIB = 1 << 20
F32 = jnp.float32
BF16 = jnp.bfloat16


def split_table(table):
    high = table.astype(jnp.bfloat16)
    low = (table - high.astype(np.float64)).astype(jnp.bfloat16)
    return high, low


@functools.lru_cache(maxsize=None)
def fourier_tables():
    first = np.arange(SIDE)
    spin = np.arange(2).reshape(2, 1, 1, 1, 1, 1)
    order = SIDE * np.arange(32)[None, :] + np.arange(SIDE)[:, None]
    order = order.reshape(1, SIDE, 1, 1, 1, 32)
    angle = (2 * first.reshape(1, 1, 1, SIDE, 1, 1) + spin) * order % (2 * NPIX) * (math.pi / NPIX)
    cosine, sine = np.cos(angle), np.sin(angle)
    row_part = np.arange(2).reshape(1, 1, 2, 1, 1, 1)
    col_part = np.arange(2).reshape(1, 1, 1, 1, 2, 1)
    same = (row_part == col_part).astype(np.float64)
    cross = np.where(row_part == 1, 1.0, -1.0) * (row_part != col_part)
    doubling = np.where(order == 0, 1.0, 2.0)
    spread = (doubling * (same * cosine + cross * sine)).reshape(2, SIDE, 2 * SIDE, SIDE)
    gather = (same * cosine + cross * sine).reshape(2, SIDE, 2 * SIDE, SIDE)
    gather = np.swapaxes(gather, 2, 3)
    spread_parts = np.concatenate(split_table(spread), axis=3)
    gather_parts = np.concatenate(split_table(gather), axis=2)
    square = first[:, None] * first[None, :] % SIDE * (2.0 * math.pi / SIDE)
    pixel = np.concatenate(split_table(np.concatenate([np.cos(square), -np.sin(square)], axis=1)), axis=0)
    back_high, back_low = split_table(np.concatenate([np.cos(square), -np.sin(square)], axis=0))
    back = np.concatenate([np.tile(back_high, (1, 2)), np.tile(back_low, (1, 2))], axis=0)
    return spread_parts, pixel, back, gather_parts


def two_parts(value):
    high = value.astype(BF16)
    low = (value - high.astype(F32)).astype(BF16)
    return high, low


def whole(shape):
    return pl.BlockSpec(shape, lambda t, *_: (0,) * len(shape))


def anywhere():
    return pl.BlockSpec(memory_space=pl.ANY)


def hbm():
    return pl.BlockSpec(memory_space=pltpu.HBM)


def weights_kernel(
    node_ref,
    radial_ref,
    alpha_ref,
    beta_ref,
    synth_ref,
    adjoint_ref,
    alpha_scr,
    beta_scr,
    filter_scr,
    weighted_scr,
    sems,
):
    copies = [
        pltpu.make_async_copy(alpha_ref, alpha_scr, sems.at[0]),
        pltpu.make_async_copy(beta_ref, beta_scr, sems.at[1]),
    ]
    for copy in copies:
        copy.start()
    for copy in copies:
        copy.wait()
    radii = node_ref.shape[0]

    def gather(radius, carry):
        node = node_ref[radius]
        scale = radial_ref[node]
        alpha = alpha_scr[pl.ds(node, 1), :]
        beta = beta_scr[pl.ds(node, 1), :]
        filter_scr[pl.ds(radius, 1), :] = alpha
        filter_scr[pl.ds(radii + radius, 1), :] = beta
        weighted_scr[pl.ds(radius, 1), :] = scale * alpha
        weighted_scr[pl.ds(radii + radius, 1), :] = (2.0 * scale) * beta
        return carry

    lax.fori_loop(0, radii, gather, 0, unroll=8)
    high, low = two_parts(filter_scr[...].T)
    synth_ref[:, : 2 * radii] = high
    synth_ref[:, 2 * radii :] = low
    high, low = two_parts(weighted_scr[...])
    adjoint_ref[: 2 * radii, :] = high
    adjoint_ref[2 * radii :, :] = low


def filter_weights(radius_index, radial_weight, alpha_table, beta_table):
    radii = radius_index.shape[0]
    degrees = alpha_table.shape[1]
    return pl.pallas_call(
        weights_kernel,
        grid_spec=pltpu.PrefetchScalarGridSpec(
            num_scalar_prefetch=2,
            grid=(1,),
            in_specs=[hbm(), hbm()],
            out_specs=[whole((degrees, 4 * radii)), whole((4 * radii, degrees))],
            scratch_shapes=[pltpu.VMEM(alpha_table.shape, F32)] * 2
            + [pltpu.VMEM((2 * radii, degrees), F32)] * 2
            + [pltpu.SemaphoreType.DMA((2,))],
        ),
        out_shape=[
            jax.ShapeDtypeStruct((degrees, 4 * radii), BF16),
            jax.ShapeDtypeStruct((4 * radii, degrees), BF16),
        ],
        compiler_params=pltpu.CompilerParams(vmem_limit_bytes=56 * MIB),
        name="filter_weights",
    )(radius_index, radial_weight, alpha_table, beta_table)


def synth_kernel(
    first, order_ref, where_ref, coeffs_ref, weight_ref, legendre_ref, *refs
):
    keep_ref, send_ref, terms_even, terms_odd, sums_even, sums_odd = refs[-6:]
    step = pl.program_id(0)
    row = where_ref[0]
    base = where_ref[1] + first + step * SYNTH_BLOCK
    degrees = coeffs_ref.shape[2]
    cycles = legendre_ref.shape[1]
    owners = cycles // 4
    lanes = weight_ref.shape[1] // 2
    degree = row * degrees + lax.broadcasted_iota(jnp.int32, (1, degrees), 1)
    half = 16 * cycles
    for group in range(SYNTH_BLOCK // 8):
        terms = terms_odd if group % 2 else terms_even
        sums = sums_odd if group % 2 else sums_even
        for place in range(8):
            slot = group * 8 + place
            live = degree >= order_ref[base + slot]
            values = legendre_ref[slot].astype(F32)
            for part in range(2):
                coeff = jnp.where(live, coeffs_ref[part, slot : slot + 1, :], 0.0)
                high, low = two_parts(values * coeff)
                start = (part * 8 + place) * cycles
                terms[start : start + cycles, :] = high
                terms[half + start : half + start + cycles, :] = low
        both = jnp.dot(terms[...], weight_ref[...], preferred_element_type=F32)
        sums[...] = both[:half, :lanes] + both[:half, lanes:] + both[half:, :lanes]
        for part in range(2):
            for owner in range(owners):
                for away in range(4):
                    cycle = 4 * owner + (row ^ away)
                    piece = sums[pl.ds(part * 8 * cycles + cycle, 8, stride=cycles), :]
                    target = send_ref if away % 2 else keep_ref
                    target[
                        away // 2,
                        owner,
                        group * 8 : group * 8 + 8,
                        part * lanes : (part + 1) * lanes,
                    ] = piece


def synth(first, count, orders, where, coeffs, weight, legendre):
    cycles, degrees = legendre.shape[1:]
    steps = count // SYNTH_BLOCK
    start = first // SYNTH_BLOCK
    owners = cycles // 4
    lanes = weight.shape[1] // 2
    out = jax.ShapeDtypeStruct((2, owners, count, 2 * lanes), F32)
    out_spec = pl.BlockSpec((2, owners, SYNTH_BLOCK, 2 * lanes), lambda t, *_: (0, 0, t, 0))
    return pl.pallas_call(
        functools.partial(synth_kernel, first),
        grid_spec=pltpu.PrefetchScalarGridSpec(
            num_scalar_prefetch=2,
            grid=(steps,),
            in_specs=[
                pl.BlockSpec((2, SYNTH_BLOCK, degrees), lambda t, *_: (0, start + t, 0)),
                whole(weight.shape),
                pl.BlockSpec((SYNTH_BLOCK, cycles, degrees), lambda t, *_: (start + t, 0, 0)),
            ],
            out_specs=[out_spec, out_spec],
            scratch_shapes=[
                pltpu.VMEM((32 * cycles, degrees), BF16),
                pltpu.VMEM((32 * cycles, degrees), BF16),
                pltpu.VMEM((16 * cycles, lanes), F32),
                pltpu.VMEM((16 * cycles, lanes), F32),
            ],
        ),
        out_shape=[out, out],
        compiler_params=pltpu.CompilerParams(vmem_limit_bytes=56 * MIB),
        cost_estimate=pl.CostEstimate(
            flops=2 * count * cycles * degrees * lanes * 2 * 4,
            bytes_accessed=count * (cycles * degrees * 2 + 2 * cycles * lanes * 4),
            transcendentals=0,
        ),
        name="synth",
    )(orders, where, coeffs, weight, legendre)


def core_sum_kernel(keep_ref, other_ref, token_ref, out_ref):
    out_ref[...] = (keep_ref[0] + other_ref[0]).astype(BF16)


def core_sum(keep, other, order):
    shape = keep.shape[1:]
    half = pl.BlockSpec((1,) + shape, lambda t: (1, 0, 0, 0))
    return pl.pallas_call(
        core_sum_kernel,
        grid=(1,),
        in_specs=[half, half, pl.BlockSpec(memory_space=pltpu.SMEM)],
        out_specs=pl.BlockSpec(shape, lambda t: (0, 0, 0)),
        out_shape=jax.ShapeDtypeStruct(shape, BF16),
        compiler_params=pltpu.CompilerParams(vmem_limit_bytes=16 * MIB),
        cost_estimate=pl.CostEstimate(flops=4 * 10**10, bytes_accessed=MIB, transcendentals=0),
        name="core_sum",
    )(keep, other, order)


def full_sum_kernel(token_ref, *refs):
    out_ref = refs[-1]
    start = 0
    for index in range(0, len(refs) - 1, 3):
        keep_ref, other_ref, incoming_ref = refs[index : index + 3]
        count = incoming_ref.shape[1]
        total = keep_ref[0] + other_ref[0] + incoming_ref[...].astype(F32)
        out_ref[:, start : start + count] = total.astype(BF16)
        start += count


def full_sum(chunks, order):
    operands, specs, count = [], [pl.BlockSpec(memory_space=pltpu.SMEM)], 0
    for keep, other, incoming in chunks:
        shape = incoming.shape
        half = pl.BlockSpec((1,) + shape, lambda t: (0, 0, 0, 0))
        operands += [keep, other, incoming]
        specs += [half, half, pl.BlockSpec(shape, lambda t: (0, 0, 0))]
        count += shape[1]
    full = (shape[0], count, shape[2])
    return pl.pallas_call(
        full_sum_kernel,
        grid=(1,),
        in_specs=specs,
        out_specs=pl.BlockSpec(full, lambda t: (0, 0, 0)),
        out_shape=jax.ShapeDtypeStruct(full, BF16),
        compiler_params=pltpu.CompilerParams(vmem_limit_bytes=16 * MIB),
        cost_estimate=pl.CostEstimate(flops=4 * 10**10, bytes_accessed=MIB, transcendentals=0),
        name="full_sum",
    )(order, *operands)


def cycle_kernel(groups, sizes, offset_ref, where_ref, weight_ref, *refs):
    pieces = refs[:groups]
    place_ref, sort_ref, unsort_ref, spread_ref, pixel_ref, back_ref, gather_ref = refs[
        groups : groups + 7
    ]
    outs = refs[groups + 7 : groups + 7 + len(sizes)]
    spread_scr, gather_scr, sorted_scr, middle_scr, product_scr, back_scr, sems = refs[-7:]
    device_count, blocks = place_ref.shape[:2]
    lanes = pieces[0].shape[2] // 2
    turned = offset_ref[where_ref[0]]
    scale = weight_ref[where_ref[0]]
    lane = lax.broadcasted_iota(jnp.int32, (SIDE, lanes), 1)

    def spread_copy(block):
        rows = pl.ds(block * device_count, device_count)
        return pltpu.make_async_copy(
            spread_ref.at[turned, rows], spread_scr.at[rows], sems.at[block]
        )

    gather_copy = pltpu.make_async_copy(gather_ref.at[turned], gather_scr, sems.at[blocks])
    for block in range(blocks):
        spread_copy(block).start()
    gather_copy.start()

    def sort_step(peer, carry):
        slots = jnp.concatenate([piece[peer] for piece in pieces], axis=0)
        sorted_scr[peer] = jnp.dot(
            sort_ref[peer], slots, preferred_element_type=F32
        ).astype(BF16)
        return carry

    lax.fori_loop(0, device_count, sort_step, 0, unroll=2)

    def spread_step(block, carry):
        spread_copy(block).wait()
        rows = pl.ds(pl.multiple_of(block * 32, 32), 32)

        def one(spot):
            picked = jnp.zeros((32, 2 * lanes), BF16)
            for peer in range(device_count):
                place = place_ref[peer, block]
                picked = jnp.where(
                    place == lax.convert_element_type(spot, BF16),
                    sorted_scr[peer, rows, :],
                    picked,
                )
            low_order = block * device_count + spot
            column = jnp.concatenate([picked[:, :lanes], picked[:, lanes:]], axis=0)
            stage = jnp.dot(
                spread_scr[low_order],
                jnp.concatenate([column, column], axis=0),
                preferred_element_type=F32,
            )
            middle_scr[pl.ds(low_order * PADDED, 2 * SIDE), :] = stage

        if device_count <= 8:
            for spot in range(device_count):
                one(spot)
        else:
            lax.fori_loop(0, device_count, lambda s, x: (one(s), x)[1], 0)
        return carry

    lax.fori_loop(0, blocks, spread_step, 0)

    def pixel_step(step, total):
        for inner in range(8):
            first = step * 8 + inner
            column = jnp.concatenate(
                [
                    middle_scr[pl.ds(first, SIDE, stride=PADDED), :],
                    middle_scr[pl.ds(first + SIDE, SIDE, stride=PADDED), :],
                ],
                axis=0,
            )
            high, low = two_parts(column)
            stage = jnp.dot(
                pixel_ref[...], jnp.concatenate([high, low], axis=1), preferred_element_type=F32
            )
            field = stage[:SIDE, :lanes] + stage[:SIDE, lanes:] + stage[SIDE:, :lanes]
            other = pltpu.roll(field, lanes // 2, 1)
            product = other * jnp.where(lane < lanes // 2, other, field)
            product_scr[first] = product
            total = total + jnp.sum(product.reshape(8, 8, lanes), axis=0)
        return total

    total = lax.fori_loop(0, SIDE // 8, pixel_step, jnp.zeros((8, lanes), F32))
    mean = jnp.sum(total, axis=0, keepdims=True) * (1.0 / NPIX)

    def back_step(step, carry):
        for inner in range(8):
            first = step * 8 + inner
            high, low = two_parts(product_scr[first] - mean)
            stage = jnp.dot(
                back_ref[...], jnp.concatenate([high, low], axis=0), preferred_element_type=F32
            )
            back_scr[pl.ds(first * PADDED, 2 * SIDE), :] = stage[: 2 * SIDE] + stage[2 * SIDE :]
        return carry

    lax.fori_loop(0, SIDE // 8, back_step, 0)
    gather_copy.wait()

    def gather_step(block, carry):
        rows = pl.ds(pl.multiple_of(block * 32, 32), 32)

        def one(spot):
            low_order = block * device_count + spot
            column = jnp.concatenate(
                [
                    back_scr[pl.ds(low_order, SIDE, stride=PADDED), :],
                    back_scr[pl.ds(low_order + SIDE, SIDE, stride=PADDED), :],
                ],
                axis=0,
            )
            high, low = two_parts(column)
            stage = jnp.dot(
                gather_scr[low_order],
                jnp.concatenate([high, low], axis=1),
                preferred_element_type=F32,
            )
            value = stage[:SIDE, :lanes] + stage[:SIDE, lanes:] + stage[SIDE:, :lanes]
            value = (value * scale).astype(BF16)
            return jnp.concatenate([value[:32], value[32:]], axis=1)

        if device_count <= 8:
            found = [one(spot) for spot in range(device_count)]
            for peer in range(device_count):
                place = place_ref[peer, block]
                picked = found[0]
                for spot in range(1, device_count):
                    picked = jnp.where(place == spot, found[spot], picked)
                sorted_scr[peer, rows, :] = picked
        else:

            def spot_step(spot, carry):
                value = one(spot)
                for peer in range(device_count):
                    sorted_scr[peer, rows, :] = jnp.where(
                        place_ref[peer, block] == lax.convert_element_type(spot, BF16),
                        value,
                        sorted_scr[peer, rows, :],
                    )
                return carry

            lax.fori_loop(0, device_count, spot_step, 0)
        return carry

    lax.fori_loop(0, blocks, gather_step, 0)

    def unsort_step(peer, carry):
        slots = jnp.dot(
            unsort_ref[peer], sorted_scr[peer], preferred_element_type=F32
        ).astype(BF16)
        start = 0
        for out, size in zip(outs, sizes):
            out[peer] = slots[start : start + size]
            start += size
        return carry

    lax.fori_loop(0, device_count, unsort_step, 0, unroll=2)


def cycle_work(pieces, sizes, places, sort, unsort, offset, where, cycle_weight):
    groups = len(pieces)
    device_count, count, lanes = pieces[0].shape
    out_shapes = [(device_count, size, lanes) for size in sizes]
    spread, pixel, back, gather = [jnp.asarray(table) for table in fourier_tables()]
    tables = [places, sort, unsort]
    return pl.pallas_call(
        functools.partial(cycle_kernel, groups, sizes),
        grid_spec=pltpu.PrefetchScalarGridSpec(
            num_scalar_prefetch=2,
            grid=(1,),
            in_specs=[pl.BlockSpec(memory_space=pltpu.SMEM)]
            + [whole(piece.shape) for piece in pieces]
            + [whole(table.shape) for table in tables]
            + [hbm(), whole(pixel.shape), whole(back.shape), hbm()],
            out_specs=[whole(shape) for shape in out_shapes],
            scratch_shapes=[
                pltpu.VMEM(spread.shape[1:], BF16),
                pltpu.VMEM(gather.shape[1:], BF16),
                pltpu.VMEM((device_count, groups * count, lanes), BF16),
                pltpu.VMEM((SIDE * PADDED, lanes // 2), F32),
                pltpu.VMEM((SIDE, SIDE, lanes // 2), F32),
                pltpu.VMEM((SIDE * PADDED, lanes // 2), F32),
                pltpu.SemaphoreType.DMA((places.shape[1] + 1,)),
            ],
        ),
        out_shape=[jax.ShapeDtypeStruct(shape, BF16) for shape in out_shapes],
        compiler_params=pltpu.CompilerParams(vmem_limit_bytes=48 * MIB),
        cost_estimate=pl.CostEstimate(
            flops=4 * SIDE * 128 * 256 * 256 * 2, bytes_accessed=8 * MIB, transcendentals=0
        ),
        name="cycle_work",
    )(offset, where, cycle_weight, *pieces, *tables, spread, pixel, back, gather)


def adjoint_kernel(
    first, order_ref, where_ref, own_ref, core_ref, far_ref, corner_ref, weight_ref, legendre_ref, *refs
):
    out_ref, values_even, values_odd, terms_even, terms_odd = refs[-5:]
    step = pl.program_id(0)
    row = where_ref[0]
    base = where_ref[1] + first + step * BLOCK
    degrees = weight_ref.shape[1]
    cycles = legendre_ref.shape[1]
    owners = cycles // 4
    lanes = weight_ref.shape[0] // 2
    pitch = cycles + 8
    tiles = degrees // 128
    quarter = owners * 16
    degree = row * degrees + lax.broadcasted_iota(jnp.int32, (8, degrees), 1)
    sublane = lax.broadcasted_iota(jnp.int32, (8, degrees), 0)
    sources = (own_ref, core_ref, far_ref, corner_ref)
    for group in range(BLOCK // 16):
        values_scr = values_odd if group % 2 else values_even
        terms_scr = terms_odd if group % 2 else terms_even
        for place in range(16):
            wide = legendre_ref[group * 16 + place].astype(F32)
            for tile in range(tiles):
                values_scr[tile, place * pitch : place * pitch + cycles, :] = wide[
                    :, tile * 128 : tile * 128 + 128
                ]
        rows = jnp.concatenate(
            [
                source[
                    :, group * 16 : group * 16 + 16, part * lanes : (part + 1) * lanes
                ].reshape(quarter, lanes)
                for part in range(2)
                for source in sources
            ],
            axis=0,
        )
        terms_scr[...] = jnp.dot(
            jnp.concatenate([rows, rows], axis=1), weight_ref[...], preferred_element_type=F32
        )
        for half in range(2):
            total = [jnp.zeros((8, degrees), F32), jnp.zeros((8, degrees), F32)]
            for away in range(4):
                for owner in range(owners):
                    cycle = 4 * owner + (row ^ away)
                    factor = jnp.concatenate(
                        [
                            values_scr[tile, pl.ds(half * 8 * pitch + cycle, 8, stride=pitch), :]
                            for tile in range(tiles)
                        ],
                        axis=1,
                    )
                    for part in range(2):
                        at = (part * 4 + away) * quarter + owner * 16 + half * 8
                        total[part] = total[part] + terms_scr[at : at + 8, :] * factor
            lowest = jnp.zeros((8, degrees), jnp.int32)
            first_slot = group * 16 + half * 8
            for place in range(8):
                lowest = jnp.where(sublane == place, order_ref[base + first_slot + place], lowest)
            for part in range(2):
                out_ref[part, first_slot : first_slot + 8, :] = jnp.where(
                    degree >= lowest, total[part], 0.0
                )


def adjoint(first, orders, where, weight, pieces, legendre, earlier):
    orders_here, cycles, degrees = legendre.shape
    count = pieces[0].shape[1]
    steps = count // BLOCK
    start = first // BLOCK
    owners = cycles // 4
    lanes = weight.shape[0] // 2
    piece_spec = pl.BlockSpec((owners, BLOCK, 2 * lanes), lambda t, *_: (0, t, 0))
    out = jax.ShapeDtypeStruct((2, orders_here, degrees), F32)
    return pl.pallas_call(
        functools.partial(adjoint_kernel, first),
        grid_spec=pltpu.PrefetchScalarGridSpec(
            num_scalar_prefetch=2,
            grid=(steps,),
            in_specs=[piece_spec] * 4
            + [
                whole(weight.shape),
                pl.BlockSpec((BLOCK, cycles, degrees), lambda t, *_: (start + t, 0, 0)),
            ]
            + [anywhere()] * len(earlier),
            out_specs=pl.BlockSpec((2, BLOCK, degrees), lambda t, *_: (0, start + t, 0)),
            scratch_shapes=[
                pltpu.VMEM((degrees // 128, 16 * (cycles + 8), 128), F32),
                pltpu.VMEM((degrees // 128, 16 * (cycles + 8), 128), F32),
                pltpu.VMEM((32 * cycles, degrees), F32),
                pltpu.VMEM((32 * cycles, degrees), F32),
            ],
        ),
        out_shape=out,
        input_output_aliases={8: 0} if earlier else {},
        compiler_params=pltpu.CompilerParams(vmem_limit_bytes=48 * MIB),
        cost_estimate=pl.CostEstimate(
            flops=2 * count * cycles * degrees * lanes * 2 * 2,
            bytes_accessed=count * (cycles * degrees * 2 + 2 * cycles * lanes * 2),
            transcendentals=0,
        ),
        name="adjoint",
    )(orders, where, *pieces, weight, legendre, *earlier)


def slot_tables(orders, device_count):
    local_orders = orders.shape[0] // device_count
    blocks = local_orders // 32
    by_device = orders.reshape(device_count, local_orders)
    block = by_device // device_count
    position = 32 * (block % blocks) + block // blocks
    wanted = jnp.arange(local_orders, dtype=jnp.int32)
    sort = position[:, None, :] == wanted[None, :, None]
    unsort = position[:, :, None] == wanted[None, None, :]
    place = jnp.sum(jnp.where(sort, (by_device % device_count)[:, None, :], 0), axis=2)
    place = place.reshape(device_count, blocks, 32, 1)
    place = jnp.broadcast_to(place, (device_count, blocks, 32, 256))
    return place.astype(BF16), sort.astype(BF16), unsort.astype(BF16)


def body(
    coeffs,
    legendre,
    alpha_table,
    beta_table,
    radial_weight,
    radius_index,
    orders,
    cycle_offset,
    cycle_weight,
):
    row_id = lax.axis_index("row")
    ma_id = lax.axis_index("ma")
    device_count = lax.axis_size("ma")
    row_count = lax.axis_size("row")
    local_orders = coeffs.shape[1]
    where = jnp.stack([row_id, ma_id * local_orders]).astype(jnp.int32)
    synth_weight, adjoint_weight = filter_weights(
        radius_index, radial_weight, alpha_table, beta_table
    )
    core_pairs = [(i, i ^ 1) for i in range(row_count)]
    far_pairs = [(i, i ^ 2) for i in range(row_count)]
    units = local_orders // 32
    counts = (units // 4, units // 4, units // 2) if units >= 4 else (units // 2, units // 2)
    counts = [32 * count for count in counts]
    kept, others, outgoing, incoming, arrived = [], [], [], [], []

    def after(*values):
        return lax.optimization_barrier((where, *values))[0]

    def launch(chunk, token):
        first = sum(counts[:chunk])
        keep, send = synth(
            first, counts[chunk], orders, token, coeffs, synth_weight, legendre
        )
        kept.append(keep)
        others.append(lax.ppermute(send, "row", core_pairs))

    def pass_on(chunk, token):
        outgoing.append(core_sum(kept[chunk], others[chunk], token))
        incoming.append(lax.ppermute(outgoing[chunk], "row", far_pairs))

    def deliver(own, token):
        summed = full_sum(list(zip(kept[own], others[own], incoming[own])), token)
        arrived.append(lax.all_to_all(summed, "ma", split_axis=0, concat_axis=0, tiled=True))
        return summed

    launch(0, where)
    launch(1, where)
    pass_on(0, after(kept[1]))
    pass_on(1, after(outgoing[0]))
    if len(counts) == 3:
        launch(2, after(outgoing[1]))
        pass_on(2, after(deliver(slice(0, 2), after(kept[2]))))
        tables = slot_tables(lax.optimization_barrier((orders, outgoing[2]))[0], device_count)
        places, sort, unsort, token = lax.optimization_barrier((*tables, where))
        deliver(slice(2, 3), token)
    else:
        deliver(slice(0, 1), after(outgoing[1]))
        deliver(slice(1, 2), after(outgoing[1]))
        places, sort, unsort = slot_tables(orders, device_count)
    early = 32 * (units // 2)
    sizes = (early, local_orders - early)
    analysed = cycle_work(
        arrived, sizes, places, sort, unsort, cycle_offset, where, cycle_weight
    )
    own = [
        lax.all_to_all(piece, "ma", split_axis=0, concat_axis=0, tiled=True) for piece in analysed
    ]
    far = lax.ppermute(own[0], "row", far_pairs)
    far, second = lax.optimization_barrier((far, own[1]))
    gradient, first = [], 0
    for own_part, far_part in ((own[0], far), (second, None)):
        if far_part is None:
            far_part = lax.ppermute(own_part, "row", far_pairs)
        if gradient:
            far_part, gradient[-1] = lax.optimization_barrier((far_part, gradient[-1]))
        core = lax.ppermute(own_part, "row", core_pairs)
        corner = lax.ppermute(far_part, "row", core_pairs)
        gradient.append(
            adjoint(
                first,
                orders,
                where,
                adjoint_weight,
                (own_part, core, far_part, corner),
                legendre,
                gradient[-1:],
            )
        )
        first += own_part.shape[1]
    return gradient[-1]


def solution(mesh):
    in_specs = (
        P(None, "ma", "row"),
        P("ma", None, "row"),
        P(None, "row"),
        P(None, "row"),
        P(),
        P(),
        P(),
        P("ma"),
        P("ma"),
    )
    out_specs = P(None, "ma", "row")
    return jax.shard_map(body, mesh=mesh, in_specs=in_specs, out_specs=out_specs, check_vma=False)
```

```python
import functools
import math

import jax
import jax.numpy as jnp
import numpy as np
from jax import lax
from jax.experimental import pallas as pl
from jax.experimental.pallas import tpu as pltpu
from jax.sharding import PartitionSpec as P

NPIX = 4096
SIDE = 64
PADDED = 136
SYNTH_BLOCK = 16
BLOCK = 32
MIB = 1 << 20
F32 = jnp.float32
BF16 = jnp.bfloat16


def split_table(table):
    high = table.astype(jnp.bfloat16)
    low = (table - high.astype(np.float64)).astype(jnp.bfloat16)
    return high, low


@functools.lru_cache(maxsize=None)
def fourier_tables():
    first = np.arange(SIDE)
    spin = np.arange(2).reshape(2, 1, 1, 1, 1, 1)
    order = SIDE * np.arange(32)[None, :] + np.arange(SIDE)[:, None]
    order = order.reshape(1, SIDE, 1, 1, 1, 32)
    angle = (2 * first.reshape(1, 1, 1, SIDE, 1, 1) + spin) * order % (2 * NPIX) * (math.pi / NPIX)
    cosine, sine = np.cos(angle), np.sin(angle)
    row_part = np.arange(2).reshape(1, 1, 2, 1, 1, 1)
    col_part = np.arange(2).reshape(1, 1, 1, 1, 2, 1)
    same = (row_part == col_part).astype(np.float64)
    cross = np.where(row_part == 1, 1.0, -1.0) * (row_part != col_part)
    doubling = np.where(order == 0, 1.0, 2.0)
    spread = (doubling * (same * cosine + cross * sine)).reshape(2, SIDE, 2 * SIDE, SIDE)
    gather = (same * cosine + cross * sine).reshape(2, SIDE, 2 * SIDE, SIDE)
    gather = np.swapaxes(gather, 2, 3)
    spread_parts = np.concatenate(split_table(spread), axis=3)
    gather_parts = np.concatenate(split_table(gather), axis=2)
    square = first[:, None] * first[None, :] % SIDE * (2.0 * math.pi / SIDE)
    pixel = np.concatenate(split_table(np.concatenate([np.cos(square), -np.sin(square)], axis=1)), axis=0)
    back_high, back_low = split_table(np.concatenate([np.cos(square), -np.sin(square)], axis=0))
    back = np.concatenate([np.tile(back_high, (1, 2)), np.tile(back_low, (1, 2))], axis=0)
    return spread_parts, pixel, back, gather_parts


def two_parts(value):
    high = value.astype(BF16)
    low = (value - high.astype(F32)).astype(BF16)
    return high, low


def whole(shape):
    return pl.BlockSpec(shape, lambda t, *_: (0,) * len(shape))


def anywhere():
    return pl.BlockSpec(memory_space=pl.ANY)


def hbm():
    return pl.BlockSpec(memory_space=pltpu.HBM)


def weights_kernel(
    node_ref,
    radial_ref,
    alpha_ref,
    beta_ref,
    synth_ref,
    adjoint_ref,
    alpha_scr,
    beta_scr,
    filter_scr,
    weighted_scr,
    sems,
):
    copies = [
        pltpu.make_async_copy(alpha_ref, alpha_scr, sems.at[0]),
        pltpu.make_async_copy(beta_ref, beta_scr, sems.at[1]),
    ]
    for copy in copies:
        copy.start()
    for copy in copies:
        copy.wait()
    radii = node_ref.shape[0]

    def gather(radius, carry):
        node = node_ref[radius]
        scale = radial_ref[node]
        alpha = alpha_scr[pl.ds(node, 1), :]
        beta = beta_scr[pl.ds(node, 1), :]
        filter_scr[pl.ds(radius, 1), :] = alpha
        filter_scr[pl.ds(radii + radius, 1), :] = beta
        weighted_scr[pl.ds(radius, 1), :] = scale * alpha
        weighted_scr[pl.ds(radii + radius, 1), :] = (2.0 * scale) * beta
        return carry

    lax.fori_loop(0, radii, gather, 0, unroll=8)
    high, low = two_parts(filter_scr[...].T)
    synth_ref[:, : 2 * radii] = high
    synth_ref[:, 2 * radii :] = low
    high, low = two_parts(weighted_scr[...])
    adjoint_ref[: 2 * radii, :] = high
    adjoint_ref[2 * radii :, :] = low


def filter_weights(radius_index, radial_weight, alpha_table, beta_table):
    radii = radius_index.shape[0]
    degrees = alpha_table.shape[1]
    return pl.pallas_call(
        weights_kernel,
        grid_spec=pltpu.PrefetchScalarGridSpec(
            num_scalar_prefetch=2,
            grid=(1,),
            in_specs=[hbm(), hbm()],
            out_specs=[whole((degrees, 4 * radii)), whole((4 * radii, degrees))],
            scratch_shapes=[pltpu.VMEM(alpha_table.shape, F32)] * 2
            + [pltpu.VMEM((2 * radii, degrees), F32)] * 2
            + [pltpu.SemaphoreType.DMA((2,))],
        ),
        out_shape=[
            jax.ShapeDtypeStruct((degrees, 4 * radii), BF16),
            jax.ShapeDtypeStruct((4 * radii, degrees), BF16),
        ],
        compiler_params=pltpu.CompilerParams(vmem_limit_bytes=56 * MIB),
        name="filter_weights",
    )(radius_index, radial_weight, alpha_table, beta_table)


def synth_kernel(
    first, order_ref, where_ref, coeffs_ref, weight_ref, legendre_ref, *refs
):
    keep_ref, send_ref, terms_even, terms_odd, sums_even, sums_odd = refs[-6:]
    step = pl.program_id(0)
    row = where_ref[0]
    base = where_ref[1] + first + step * SYNTH_BLOCK
    degrees = coeffs_ref.shape[2]
    cycles = legendre_ref.shape[1]
    owners = cycles // 4
    lanes = weight_ref.shape[1] // 2
    degree = row * degrees + lax.broadcasted_iota(jnp.int32, (1, degrees), 1)
    half = 16 * cycles
    for group in range(SYNTH_BLOCK // 8):
        terms = terms_odd if group % 2 else terms_even
        sums = sums_odd if group % 2 else sums_even
        for place in range(8):
            slot = group * 8 + place
            live = degree >= order_ref[base + slot]
            values = legendre_ref[slot].astype(F32)
            for part in range(2):
                coeff = jnp.where(live, coeffs_ref[part, slot : slot + 1, :], 0.0)
                high, low = two_parts(values * coeff)
                start = (part * 8 + place) * cycles
                terms[start : start + cycles, :] = high
                terms[half + start : half + start + cycles, :] = low
        both = jnp.dot(terms[:half], weight_ref[...], preferred_element_type=F32)
        rest = jnp.dot(terms[half:], weight_ref[:, :lanes], preferred_element_type=F32)
        sums[...] = both[:, :lanes] + both[:, lanes:] + rest
        for part in range(2):
            for owner in range(owners):
                for away in range(4):
                    cycle = 4 * owner + (row ^ away)
                    piece = sums[pl.ds(part * 8 * cycles + cycle, 8, stride=cycles), :]
                    target = send_ref if away % 2 else keep_ref
                    target[
                        away // 2,
                        owner,
                        group * 8 : group * 8 + 8,
                        part * lanes : (part + 1) * lanes,
                    ] = piece


def synth(first, count, grant, orders, where, coeffs, weight, legendre):
    cycles, degrees = legendre.shape[1:]
    steps = count // SYNTH_BLOCK
    start = first // SYNTH_BLOCK
    owners = cycles // 4
    lanes = weight.shape[1] // 2
    out = jax.ShapeDtypeStruct((2, owners, count, 2 * lanes), F32)
    out_spec = pl.BlockSpec((2, owners, SYNTH_BLOCK, 2 * lanes), lambda t, *_: (0, 0, t, 0))
    return pl.pallas_call(
        functools.partial(synth_kernel, first),
        grid_spec=pltpu.PrefetchScalarGridSpec(
            num_scalar_prefetch=2,
            grid=(steps,),
            in_specs=[
                pl.BlockSpec((2, SYNTH_BLOCK, degrees), lambda t, *_: (0, start + t, 0)),
                whole(weight.shape),
                pl.BlockSpec((SYNTH_BLOCK, cycles, degrees), lambda t, *_: (start + t, 0, 0)),
            ],
            out_specs=[out_spec, out_spec],
            scratch_shapes=[
                pltpu.VMEM((32 * cycles, degrees), BF16),
                pltpu.VMEM((32 * cycles, degrees), BF16),
                pltpu.VMEM((16 * cycles, lanes), F32),
                pltpu.VMEM((16 * cycles, lanes), F32),
            ],
        ),
        out_shape=[out, out],
        compiler_params=pltpu.CompilerParams(vmem_limit_bytes=grant * MIB),
        cost_estimate=pl.CostEstimate(
            flops=2 * count * cycles * degrees * lanes * 2 * 4,
            bytes_accessed=count * (cycles * degrees * 2 + 2 * cycles * lanes * 4),
            transcendentals=0,
        ),
        name="synth",
    )(orders, where, coeffs, weight, legendre)


def core_sum_kernel(keep_ref, other_ref, token_ref, out_ref):
    out_ref[...] = (keep_ref[0] + other_ref[0]).astype(BF16)


def core_sum(keep, other, order):
    shape = keep.shape[1:]
    half = pl.BlockSpec((1,) + shape, lambda t: (1, 0, 0, 0))
    return pl.pallas_call(
        core_sum_kernel,
        grid=(1,),
        in_specs=[half, half, pl.BlockSpec(memory_space=pltpu.SMEM)],
        out_specs=pl.BlockSpec(shape, lambda t: (0, 0, 0)),
        out_shape=jax.ShapeDtypeStruct(shape, BF16),
        compiler_params=pltpu.CompilerParams(vmem_limit_bytes=16 * MIB),
        cost_estimate=pl.CostEstimate(flops=4 * 10**10, bytes_accessed=MIB, transcendentals=0),
        name="core_sum",
    )(keep, other, order)


def full_sum_kernel(token_ref, *refs):
    out_ref = refs[-1]
    start = 0
    for index in range(0, len(refs) - 1, 3):
        keep_ref, other_ref, incoming_ref = refs[index : index + 3]
        count = incoming_ref.shape[1]
        total = keep_ref[0] + other_ref[0] + incoming_ref[...].astype(F32)
        out_ref[:, start : start + count] = total.astype(BF16)
        start += count


def full_sum(chunks, order):
    operands, specs, count = [], [pl.BlockSpec(memory_space=pltpu.SMEM)], 0
    for keep, other, incoming in chunks:
        shape = incoming.shape
        half = pl.BlockSpec((1,) + shape, lambda t: (0, 0, 0, 0))
        operands += [keep, other, incoming]
        specs += [half, half, pl.BlockSpec(shape, lambda t: (0, 0, 0))]
        count += shape[1]
    full = (shape[0], count, shape[2])
    return pl.pallas_call(
        full_sum_kernel,
        grid=(1,),
        in_specs=specs,
        out_specs=pl.BlockSpec(full, lambda t: (0, 0, 0)),
        out_shape=jax.ShapeDtypeStruct(full, BF16),
        compiler_params=pltpu.CompilerParams(vmem_limit_bytes=16 * MIB),
        cost_estimate=pl.CostEstimate(flops=4 * 10**10, bytes_accessed=MIB, transcendentals=0),
        name="full_sum",
    )(order, *operands)


def cycle_kernel(groups, sizes, offset_ref, where_ref, weight_ref, *refs):
    pieces = refs[:groups]
    place_ref, sort_ref, unsort_ref, spread_ref, pixel_ref, back_ref, gather_ref = refs[
        groups : groups + 7
    ]
    outs = refs[groups + 7 : groups + 7 + len(sizes)]
    spread_scr, gather_scr, sorted_scr, middle_scr, product_scr, back_scr, sems = refs[-7:]
    device_count, blocks = place_ref.shape[:2]
    lanes = pieces[0].shape[2] // 2
    turned = offset_ref[where_ref[0]]
    scale = weight_ref[where_ref[0]]
    lane = lax.broadcasted_iota(jnp.int32, (SIDE, lanes), 1)

    def spread_copy(block):
        rows = pl.ds(block * device_count, device_count)
        return pltpu.make_async_copy(
            spread_ref.at[turned, rows], spread_scr.at[rows], sems.at[block]
        )

    gather_copy = pltpu.make_async_copy(gather_ref.at[turned], gather_scr, sems.at[blocks])
    for block in range(blocks):
        spread_copy(block).start()
    gather_copy.start()

    def sort_step(peer, carry):
        slots = jnp.concatenate([piece[peer] for piece in pieces], axis=0)
        sorted_scr[peer] = jnp.dot(
            sort_ref[peer], slots, preferred_element_type=F32
        ).astype(BF16)
        return carry

    lax.fori_loop(0, device_count, sort_step, 0, unroll=2)

    def spread_step(block, carry):
        spread_copy(block).wait()
        rows = pl.ds(pl.multiple_of(block * 32, 32), 32)

        def one(spot):
            picked = jnp.zeros((32, 2 * lanes), BF16)
            for peer in range(device_count):
                place = place_ref[peer, block]
                picked = jnp.where(
                    place == lax.convert_element_type(spot, BF16),
                    sorted_scr[peer, rows, :],
                    picked,
                )
            low_order = block * device_count + spot
            column = jnp.concatenate([picked[:, :lanes], picked[:, lanes:]], axis=0)
            stage = jnp.dot(
                spread_scr[low_order],
                jnp.concatenate([column, column], axis=0),
                preferred_element_type=F32,
            )
            middle_scr[pl.ds(low_order * PADDED, 2 * SIDE), :] = stage

        if device_count <= 8:
            for spot in range(device_count):
                one(spot)
        else:
            lax.fori_loop(0, device_count, lambda s, x: (one(s), x)[1], 0)
        return carry

    lax.fori_loop(0, blocks, spread_step, 0)

    def pixel_step(step, total):
        for inner in range(8):
            first = step * 8 + inner
            column = jnp.concatenate(
                [
                    middle_scr[pl.ds(first, SIDE, stride=PADDED), :],
                    middle_scr[pl.ds(first + SIDE, SIDE, stride=PADDED), :],
                ],
                axis=0,
            )
            high, low = two_parts(column)
            stage = jnp.dot(
                pixel_ref[...], jnp.concatenate([high, low], axis=1), preferred_element_type=F32
            )
            field = stage[:SIDE, :lanes] + stage[:SIDE, lanes:] + stage[SIDE:, :lanes]
            other = pltpu.roll(field, lanes // 2, 1)
            product = other * jnp.where(lane < lanes // 2, other, field)
            product_scr[first] = product
            total = total + jnp.sum(product.reshape(8, 8, lanes), axis=0)
        return total

    total = lax.fori_loop(0, SIDE // 8, pixel_step, jnp.zeros((8, lanes), F32))
    mean = jnp.sum(total, axis=0, keepdims=True) * (1.0 / NPIX)

    def back_step(step, carry):
        for inner in range(8):
            first = step * 8 + inner
            high, low = two_parts(product_scr[first] - mean)
            stage = jnp.dot(
                back_ref[...], jnp.concatenate([high, low], axis=0), preferred_element_type=F32
            )
            back_scr[pl.ds(first * PADDED, 2 * SIDE), :] = stage[: 2 * SIDE] + stage[2 * SIDE :]
        return carry

    lax.fori_loop(0, SIDE // 8, back_step, 0)
    gather_copy.wait()

    def gather_step(block, carry):
        rows = pl.ds(pl.multiple_of(block * 32, 32), 32)

        def one(spot):
            low_order = block * device_count + spot
            column = jnp.concatenate(
                [
                    back_scr[pl.ds(low_order, SIDE, stride=PADDED), :],
                    back_scr[pl.ds(low_order + SIDE, SIDE, stride=PADDED), :],
                ],
                axis=0,
            )
            high, low = two_parts(column)
            stage = jnp.dot(
                gather_scr[low_order],
                jnp.concatenate([high, low], axis=1),
                preferred_element_type=F32,
            )
            value = stage[:SIDE, :lanes] + stage[:SIDE, lanes:] + stage[SIDE:, :lanes]
            value = (value * scale).astype(BF16)
            return jnp.concatenate([value[:32], value[32:]], axis=1)

        if device_count <= 8:
            found = [one(spot) for spot in range(device_count)]
            for peer in range(device_count):
                place = place_ref[peer, block]
                picked = found[0]
                for spot in range(1, device_count):
                    picked = jnp.where(place == spot, found[spot], picked)
                sorted_scr[peer, rows, :] = picked
        else:

            def spot_step(spot, carry):
                value = one(spot)
                for peer in range(device_count):
                    sorted_scr[peer, rows, :] = jnp.where(
                        place_ref[peer, block] == lax.convert_element_type(spot, BF16),
                        value,
                        sorted_scr[peer, rows, :],
                    )
                return carry

            lax.fori_loop(0, device_count, spot_step, 0)
        return carry

    lax.fori_loop(0, blocks, gather_step, 0)

    def unsort_step(peer, carry):
        slots = jnp.dot(
            unsort_ref[peer], sorted_scr[peer], preferred_element_type=F32
        ).astype(BF16)
        start = 0
        for out, size in zip(outs, sizes):
            out[peer] = slots[start : start + size]
            start += size
        return carry

    lax.fori_loop(0, device_count, unsort_step, 0, unroll=2)


def cycle_work(pieces, sizes, places, sort, unsort, offset, where, cycle_weight):
    groups = len(pieces)
    device_count, _, lanes = pieces[0].shape
    count = sum(piece.shape[1] for piece in pieces)
    out_shapes = [(device_count, size, lanes) for size in sizes]
    spread, pixel, back, gather = [jnp.asarray(table) for table in fourier_tables()]
    tables = [places, sort, unsort]
    return pl.pallas_call(
        functools.partial(cycle_kernel, groups, sizes),
        grid_spec=pltpu.PrefetchScalarGridSpec(
            num_scalar_prefetch=2,
            grid=(1,),
            in_specs=[pl.BlockSpec(memory_space=pltpu.SMEM)]
            + [whole(piece.shape) for piece in pieces]
            + [whole(table.shape) for table in tables]
            + [hbm(), whole(pixel.shape), whole(back.shape), hbm()],
            out_specs=[whole(shape) for shape in out_shapes],
            scratch_shapes=[
                pltpu.VMEM(spread.shape[1:], BF16),
                pltpu.VMEM(gather.shape[1:], BF16),
                pltpu.VMEM((device_count, count, lanes), BF16),
                pltpu.VMEM((SIDE * PADDED, lanes // 2), F32),
                pltpu.VMEM((SIDE, SIDE, lanes // 2), F32),
                pltpu.VMEM((SIDE * PADDED, lanes // 2), F32),
                pltpu.SemaphoreType.DMA((places.shape[1] + 1,)),
            ],
        ),
        out_shape=[jax.ShapeDtypeStruct(shape, BF16) for shape in out_shapes],
        compiler_params=pltpu.CompilerParams(vmem_limit_bytes=48 * MIB),
        cost_estimate=pl.CostEstimate(
            flops=4 * SIDE * 128 * 256 * 256 * 2, bytes_accessed=8 * MIB, transcendentals=0
        ),
        name="cycle_work",
    )(offset, where, cycle_weight, *pieces, *tables, spread, pixel, back, gather)


def adjoint_kernel(
    first, order_ref, where_ref, own_ref, core_ref, far_ref, corner_ref, weight_ref, legendre_ref, *refs
):
    out_ref, values_even, values_odd, terms_even, terms_odd = refs[-5:]
    step = pl.program_id(0)
    row = where_ref[0]
    base = where_ref[1] + first + step * BLOCK
    degrees = weight_ref.shape[1]
    cycles = legendre_ref.shape[1]
    owners = cycles // 4
    lanes = weight_ref.shape[0] // 2
    pitch = cycles + 8
    tiles = degrees // 128
    quarter = owners * 16
    degree = row * degrees + lax.broadcasted_iota(jnp.int32, (8, degrees), 1)
    sublane = lax.broadcasted_iota(jnp.int32, (8, degrees), 0)
    sources = (own_ref, core_ref, far_ref, corner_ref)
    for group in range(BLOCK // 16):
        values_scr = values_odd if group % 2 else values_even
        terms_scr = terms_odd if group % 2 else terms_even
        for place in range(16):
            wide = legendre_ref[group * 16 + place].astype(F32)
            for tile in range(tiles):
                values_scr[tile, place * pitch : place * pitch + cycles, :] = wide[
                    :, tile * 128 : tile * 128 + 128
                ]
        rows = jnp.concatenate(
            [
                source[
                    :, group * 16 : group * 16 + 16, part * lanes : (part + 1) * lanes
                ].reshape(quarter, lanes)
                for part in range(2)
                for source in sources
            ],
            axis=0,
        )
        terms_scr[...] = jnp.dot(
            jnp.concatenate([rows, rows], axis=1), weight_ref[...], preferred_element_type=F32
        )
        for half in range(2):
            total = [jnp.zeros((8, degrees), F32), jnp.zeros((8, degrees), F32)]
            for away in range(4):
                for owner in range(owners):
                    cycle = 4 * owner + (row ^ away)
                    factor = jnp.concatenate(
                        [
                            values_scr[tile, pl.ds(half * 8 * pitch + cycle, 8, stride=pitch), :]
                            for tile in range(tiles)
                        ],
                        axis=1,
                    )
                    for part in range(2):
                        at = (part * 4 + away) * quarter + owner * 16 + half * 8
                        total[part] = total[part] + terms_scr[at : at + 8, :] * factor
            lowest = jnp.zeros((8, degrees), jnp.int32)
            first_slot = group * 16 + half * 8
            for place in range(8):
                lowest = jnp.where(sublane == place, order_ref[base + first_slot + place], lowest)
            for part in range(2):
                out_ref[part, first_slot : first_slot + 8, :] = jnp.where(
                    degree >= lowest, total[part], 0.0
                )


def adjoint(first, orders, where, weight, pieces, legendre, earlier):
    orders_here, cycles, degrees = legendre.shape
    count = pieces[0].shape[1]
    steps = count // BLOCK
    start = first // BLOCK
    owners = cycles // 4
    lanes = weight.shape[0] // 2
    piece_spec = pl.BlockSpec((owners, BLOCK, 2 * lanes), lambda t, *_: (0, t, 0))
    out = jax.ShapeDtypeStruct((2, orders_here, degrees), F32)
    return pl.pallas_call(
        functools.partial(adjoint_kernel, first),
        grid_spec=pltpu.PrefetchScalarGridSpec(
            num_scalar_prefetch=2,
            grid=(steps,),
            in_specs=[piece_spec] * 4
            + [
                whole(weight.shape),
                pl.BlockSpec((BLOCK, cycles, degrees), lambda t, *_: (start + t, 0, 0)),
            ]
            + [anywhere()] * len(earlier),
            out_specs=pl.BlockSpec((2, BLOCK, degrees), lambda t, *_: (0, start + t, 0)),
            scratch_shapes=[
                pltpu.VMEM((degrees // 128, 16 * (cycles + 8), 128), F32),
                pltpu.VMEM((degrees // 128, 16 * (cycles + 8), 128), F32),
                pltpu.VMEM((32 * cycles, degrees), F32),
                pltpu.VMEM((32 * cycles, degrees), F32),
            ],
        ),
        out_shape=out,
        input_output_aliases={8: 0} if earlier else {},
        compiler_params=pltpu.CompilerParams(vmem_limit_bytes=48 * MIB),
        cost_estimate=pl.CostEstimate(
            flops=2 * count * cycles * degrees * lanes * 2 * 2,
            bytes_accessed=count * (cycles * degrees * 2 + 2 * cycles * lanes * 2),
            transcendentals=0,
        ),
        name="adjoint",
    )(orders, where, *pieces, weight, legendre, *earlier)


def slot_tables(orders, device_count):
    local_orders = orders.shape[0] // device_count
    blocks = local_orders // 32
    by_device = orders.reshape(device_count, local_orders)
    block = by_device // device_count
    position = 32 * (block % blocks) + block // blocks
    wanted = jnp.arange(local_orders, dtype=jnp.int32)
    sort = position[:, None, :] == wanted[None, :, None]
    unsort = position[:, :, None] == wanted[None, None, :]
    place = jnp.sum(jnp.where(sort, (by_device % device_count)[:, None, :], 0), axis=2)
    place = place.reshape(device_count, blocks, 32, 1)
    place = jnp.broadcast_to(place, (device_count, blocks, 32, 256))
    return place.astype(BF16), sort.astype(BF16), unsort.astype(BF16)


def body(
    coeffs,
    legendre,
    alpha_table,
    beta_table,
    radial_weight,
    radius_index,
    orders,
    cycle_offset,
    cycle_weight,
):
    row_id = lax.axis_index("row")
    ma_id = lax.axis_index("ma")
    device_count = lax.axis_size("ma")
    row_count = lax.axis_size("row")
    local_orders = coeffs.shape[1]
    where = jnp.stack([row_id, ma_id * local_orders]).astype(jnp.int32)
    synth_weight, adjoint_weight = filter_weights(
        radius_index, radial_weight, alpha_table, beta_table
    )
    core_pairs = [(i, i ^ 1) for i in range(row_count)]
    far_pairs = [(i, i ^ 2) for i in range(row_count)]
    units = local_orders // 32
    counts = (2, (units - 2) // 2, (units - 1) // 2) if units > 4 else (units // 2, units // 2)
    counts = [32 * count for count in counts]
    kept, others, outgoing, incoming, arrived = [], [], [], [], []

    def after(*values):
        return lax.optimization_barrier((where, *values))[0]

    def launch(chunk, token):
        first = sum(counts[:chunk])
        grant = 44 if chunk == 2 else 56
        keep, send = synth(
            first, counts[chunk], grant, orders, token, coeffs, synth_weight, legendre
        )
        kept.append(keep)
        others.append(lax.ppermute(send, "row", core_pairs))

    def pass_on(chunk, token):
        outgoing.append(core_sum(kept[chunk], others[chunk], token))
        incoming.append(lax.ppermute(outgoing[chunk], "row", far_pairs))

    def deliver(own, token):
        summed = full_sum(list(zip(kept[own], others[own], incoming[own])), token)
        arrived.append(lax.all_to_all(summed, "ma", split_axis=0, concat_axis=0, tiled=True))
        return summed

    launch(0, where)
    launch(1, where)
    pass_on(0, after(kept[1]))
    pass_on(1, after(outgoing[0]))
    if len(counts) == 3:
        launch(2, after(outgoing[1]))
        pass_on(2, after(deliver(slice(0, 2), after(kept[2]))))
        tables = slot_tables(lax.optimization_barrier((orders, outgoing[2]))[0], device_count)
        places, sort, unsort, token = lax.optimization_barrier((*tables, where))
        deliver(slice(2, 3), token)
    else:
        deliver(slice(0, 1), after(outgoing[1]))
        deliver(slice(1, 2), after(outgoing[1]))
        places, sort, unsort = slot_tables(orders, device_count)
    early = 32 * ((5 * units) // 8)
    sizes = (early, local_orders - early)
    analysed = cycle_work(
        arrived, sizes, places, sort, unsort, cycle_offset, where, cycle_weight
    )
    own = [
        lax.all_to_all(piece, "ma", split_axis=0, concat_axis=0, tiled=True) for piece in analysed
    ]
    far = lax.ppermute(own[0], "row", far_pairs)
    far, second = lax.optimization_barrier((far, own[1]))
    gradient, first = [], 0
    for own_part, far_part in ((own[0], far), (second, None)):
        if far_part is None:
            far_part = lax.ppermute(own_part, "row", far_pairs)
        if gradient:
            far_part, gradient[-1] = lax.optimization_barrier((far_part, gradient[-1]))
        core = lax.ppermute(own_part, "row", core_pairs)
        corner = lax.ppermute(far_part, "row", core_pairs)
        gradient.append(
            adjoint(
                first,
                orders,
                where,
                adjoint_weight,
                (own_part, core, far_part, corner),
                legendre,
                gradient[-1:],
            )
        )
        first += own_part.shape[1]
    return gradient[-1]


def solution(mesh):
    in_specs = (
        P(None, "ma", "row"),
        P("ma", None, "row"),
        P(None, "row"),
        P(None, "row"),
        P(),
        P(),
        P(),
        P("ma"),
        P("ma"),
    )
    out_specs = P(None, "ma", "row")
    return jax.shard_map(body, mesh=mesh, in_specs=in_specs, out_specs=out_specs, check_vma=False)
```

```python
import functools
import math

import jax
import jax.numpy as jnp
import numpy as np
from jax import lax
from jax.experimental import pallas as pl
from jax.experimental.pallas import tpu as pltpu
from jax.sharding import PartitionSpec as P

NPIX = 4096
SIDE = 64
PADDED = 136
SYNTH_BLOCK = 16
BLOCK = 32
MIB = 1 << 20
F32 = jnp.float32
BF16 = jnp.bfloat16


def split_table(table):
    high = table.astype(jnp.bfloat16)
    low = (table - high.astype(np.float64)).astype(jnp.bfloat16)
    return high, low


@functools.lru_cache(maxsize=None)
def fourier_tables():
    first = np.arange(SIDE)
    spin = np.arange(2).reshape(2, 1, 1, 1, 1, 1)
    order = SIDE * np.arange(32)[None, :] + np.arange(SIDE)[:, None]
    order = order.reshape(1, SIDE, 1, 1, 1, 32)
    angle = (2 * first.reshape(1, 1, 1, SIDE, 1, 1) + spin) * order % (2 * NPIX) * (math.pi / NPIX)
    cosine, sine = np.cos(angle), np.sin(angle)
    row_part = np.arange(2).reshape(1, 1, 2, 1, 1, 1)
    col_part = np.arange(2).reshape(1, 1, 1, 1, 2, 1)
    same = (row_part == col_part).astype(np.float64)
    cross = np.where(row_part == 1, 1.0, -1.0) * (row_part != col_part)
    doubling = np.where(order == 0, 1.0, 2.0)
    spread = (doubling * (same * cosine + cross * sine)).reshape(2, SIDE, 2 * SIDE, SIDE)
    gather = (same * cosine + cross * sine).reshape(2, SIDE, 2 * SIDE, SIDE)
    gather = np.swapaxes(gather, 2, 3)
    spread_parts = np.concatenate(split_table(spread), axis=3)
    gather_parts = np.concatenate(split_table(gather), axis=2)
    square = first[:, None] * first[None, :] % SIDE * (2.0 * math.pi / SIDE)
    pixel = np.concatenate(split_table(np.concatenate([np.cos(square), -np.sin(square)], axis=1)), axis=0)
    back_high, back_low = split_table(np.concatenate([np.cos(square), -np.sin(square)], axis=0))
    back = np.concatenate([np.tile(back_high, (1, 2)), np.tile(back_low, (1, 2))], axis=0)
    return spread_parts, pixel, back, gather_parts


def two_parts(value):
    high = value.astype(BF16)
    low = (value - high.astype(F32)).astype(BF16)
    return high, low


def whole(shape):
    return pl.BlockSpec(shape, lambda t, *_: (0,) * len(shape))


def anywhere():
    return pl.BlockSpec(memory_space=pl.ANY)


def hbm():
    return pl.BlockSpec(memory_space=pltpu.HBM)


def weights_kernel(
    node_ref,
    radial_ref,
    alpha_ref,
    beta_ref,
    synth_ref,
    adjoint_ref,
    alpha_scr,
    beta_scr,
    filter_scr,
    weighted_scr,
    sems,
):
    copies = [
        pltpu.make_async_copy(alpha_ref, alpha_scr, sems.at[0]),
        pltpu.make_async_copy(beta_ref, beta_scr, sems.at[1]),
    ]
    for copy in copies:
        copy.start()
    for copy in copies:
        copy.wait()
    radii = node_ref.shape[0]

    def gather(radius, carry):
        node = node_ref[radius]
        scale = radial_ref[node]
        alpha = alpha_scr[pl.ds(node, 1), :]
        beta = beta_scr[pl.ds(node, 1), :]
        filter_scr[pl.ds(radius, 1), :] = alpha
        filter_scr[pl.ds(radii + radius, 1), :] = beta
        weighted_scr[pl.ds(radius, 1), :] = scale * alpha
        weighted_scr[pl.ds(radii + radius, 1), :] = (2.0 * scale) * beta
        return carry

    lax.fori_loop(0, radii, gather, 0, unroll=8)
    high, low = two_parts(filter_scr[...].T)
    synth_ref[:, : 2 * radii] = high
    synth_ref[:, 2 * radii :] = low
    high, low = two_parts(weighted_scr[...])
    adjoint_ref[: 2 * radii, :] = high
    adjoint_ref[2 * radii :, :] = low


def filter_weights(radius_index, radial_weight, alpha_table, beta_table):
    radii = radius_index.shape[0]
    degrees = alpha_table.shape[1]
    return pl.pallas_call(
        weights_kernel,
        grid_spec=pltpu.PrefetchScalarGridSpec(
            num_scalar_prefetch=2,
            grid=(1,),
            in_specs=[hbm(), hbm()],
            out_specs=[whole((degrees, 4 * radii)), whole((4 * radii, degrees))],
            scratch_shapes=[pltpu.VMEM(alpha_table.shape, F32)] * 2
            + [pltpu.VMEM((2 * radii, degrees), F32)] * 2
            + [pltpu.SemaphoreType.DMA((2,))],
        ),
        out_shape=[
            jax.ShapeDtypeStruct((degrees, 4 * radii), BF16),
            jax.ShapeDtypeStruct((4 * radii, degrees), BF16),
        ],
        compiler_params=pltpu.CompilerParams(vmem_limit_bytes=56 * MIB),
        name="filter_weights",
    )(radius_index, radial_weight, alpha_table, beta_table)


def synth_kernel(
    first, order_ref, where_ref, coeffs_ref, weight_ref, legendre_ref, *refs
):
    keep_ref, send_ref, terms_even, terms_odd, sums_even, sums_odd = refs[-6:]
    step = pl.program_id(0)
    row = where_ref[0]
    base = where_ref[1] + first + step * SYNTH_BLOCK
    degrees = coeffs_ref.shape[2]
    cycles = legendre_ref.shape[1]
    owners = cycles // 4
    lanes = weight_ref.shape[1] // 2
    degree = row * degrees + lax.broadcasted_iota(jnp.int32, (1, degrees), 1)
    half = 16 * cycles
    for group in range(SYNTH_BLOCK // 8):
        terms = terms_odd if group % 2 else terms_even
        sums = sums_odd if group % 2 else sums_even
        for place in range(8):
            slot = group * 8 + place
            live = degree >= order_ref[base + slot]
            values = legendre_ref[slot].astype(F32)
            for part in range(2):
                coeff = jnp.where(live, coeffs_ref[part, slot : slot + 1, :], 0.0)
                high, low = two_parts(values * coeff)
                start = (part * 8 + place) * cycles
                terms[start : start + cycles, :] = high
                terms[half + start : half + start + cycles, :] = low
        both = jnp.dot(terms[:half], weight_ref[...], preferred_element_type=F32)
        rest = jnp.dot(terms[half:], weight_ref[:, :lanes], preferred_element_type=F32)
        sums[...] = both[:, :lanes] + both[:, lanes:] + rest
        for part in range(2):
            for owner in range(owners):
                for away in range(4):
                    cycle = 4 * owner + (row ^ away)
                    piece = sums[pl.ds(part * 8 * cycles + cycle, 8, stride=cycles), :]
                    target = send_ref if away % 2 else keep_ref
                    target[
                        away // 2,
                        owner,
                        group * 8 : group * 8 + 8,
                        part * lanes : (part + 1) * lanes,
                    ] = piece


def synth(first, count, grant, orders, where, coeffs, weight, legendre):
    cycles, degrees = legendre.shape[1:]
    steps = count // SYNTH_BLOCK
    start = first // SYNTH_BLOCK
    owners = cycles // 4
    lanes = weight.shape[1] // 2
    out = jax.ShapeDtypeStruct((2, owners, count, 2 * lanes), F32)
    out_spec = pl.BlockSpec((2, owners, SYNTH_BLOCK, 2 * lanes), lambda t, *_: (0, 0, t, 0))
    return pl.pallas_call(
        functools.partial(synth_kernel, first),
        grid_spec=pltpu.PrefetchScalarGridSpec(
            num_scalar_prefetch=2,
            grid=(steps,),
            in_specs=[
                pl.BlockSpec((2, SYNTH_BLOCK, degrees), lambda t, *_: (0, start + t, 0)),
                whole(weight.shape),
                pl.BlockSpec((SYNTH_BLOCK, cycles, degrees), lambda t, *_: (start + t, 0, 0)),
            ],
            out_specs=[out_spec, out_spec],
            scratch_shapes=[
                pltpu.VMEM((32 * cycles, degrees), BF16),
                pltpu.VMEM((32 * cycles, degrees), BF16),
                pltpu.VMEM((16 * cycles, lanes), F32),
                pltpu.VMEM((16 * cycles, lanes), F32),
            ],
        ),
        out_shape=[out, out],
        compiler_params=pltpu.CompilerParams(vmem_limit_bytes=grant * MIB),
        cost_estimate=pl.CostEstimate(
            flops=2 * count * cycles * degrees * lanes * 2 * 4,
            bytes_accessed=count * (cycles * degrees * 2 + 2 * cycles * lanes * 4),
            transcendentals=0,
        ),
        name="synth",
    )(orders, where, coeffs, weight, legendre)


def core_sum_kernel(keep_ref, other_ref, token_ref, out_ref):
    out_ref[...] = (keep_ref[0] + other_ref[0]).astype(BF16)


def core_sum(keep, other, order):
    shape = keep.shape[1:]
    half = pl.BlockSpec((1,) + shape, lambda t: (1, 0, 0, 0))
    return pl.pallas_call(
        core_sum_kernel,
        grid=(1,),
        in_specs=[half, half, pl.BlockSpec(memory_space=pltpu.SMEM)],
        out_specs=pl.BlockSpec(shape, lambda t: (0, 0, 0)),
        out_shape=jax.ShapeDtypeStruct(shape, BF16),
        compiler_params=pltpu.CompilerParams(vmem_limit_bytes=16 * MIB),
        cost_estimate=pl.CostEstimate(flops=4 * 10**10, bytes_accessed=MIB, transcendentals=0),
        name="core_sum",
    )(keep, other, order)


def full_sum_kernel(token_ref, *refs):
    out_ref = refs[-1]
    start = 0
    for index in range(0, len(refs) - 1, 3):
        keep_ref, other_ref, incoming_ref = refs[index : index + 3]
        count = incoming_ref.shape[1]
        total = keep_ref[0] + other_ref[0] + incoming_ref[...].astype(F32)
        out_ref[:, start : start + count] = total.astype(BF16)
        start += count


def full_sum(chunks, order):
    operands, specs, count = [], [pl.BlockSpec(memory_space=pltpu.SMEM)], 0
    for keep, other, incoming in chunks:
        shape = incoming.shape
        half = pl.BlockSpec((1,) + shape, lambda t: (0, 0, 0, 0))
        operands += [keep, other, incoming]
        specs += [half, half, pl.BlockSpec(shape, lambda t: (0, 0, 0))]
        count += shape[1]
    full = (shape[0], count, shape[2])
    return pl.pallas_call(
        full_sum_kernel,
        grid=(1,),
        in_specs=specs,
        out_specs=pl.BlockSpec(full, lambda t: (0, 0, 0)),
        out_shape=jax.ShapeDtypeStruct(full, BF16),
        compiler_params=pltpu.CompilerParams(vmem_limit_bytes=16 * MIB),
        cost_estimate=pl.CostEstimate(flops=4 * 10**10, bytes_accessed=MIB, transcendentals=0),
        name="full_sum",
    )(order, *operands)


def cycle_kernel(groups, sizes, offset_ref, where_ref, weight_ref, *refs):
    pieces = refs[:groups]
    place_ref, sort_ref, unsort_ref, spread_ref, pixel_ref, back_ref, gather_ref = refs[
        groups : groups + 7
    ]
    outs = refs[groups + 7 : groups + 7 + len(sizes)]
    spread_scr, gather_scr, sorted_scr, middle_scr, product_scr, back_scr, sems = refs[-7:]
    device_count, blocks = place_ref.shape[:2]
    lanes = pieces[0].shape[2] // 2
    turned = offset_ref[where_ref[0]]
    scale = weight_ref[where_ref[0]]
    lane = lax.broadcasted_iota(jnp.int32, (SIDE, lanes), 1)

    def spread_copy(block):
        rows = pl.ds(block * device_count, device_count)
        return pltpu.make_async_copy(
            spread_ref.at[turned, rows], spread_scr.at[rows], sems.at[block]
        )

    gather_copy = pltpu.make_async_copy(gather_ref.at[turned], gather_scr, sems.at[blocks])
    for block in range(blocks):
        spread_copy(block).start()
    gather_copy.start()

    def sort_step(peer, carry):
        slots = jnp.concatenate([piece[peer] for piece in pieces], axis=0)
        sorted_scr[peer] = jnp.dot(
            sort_ref[peer], slots, preferred_element_type=F32
        ).astype(BF16)
        return carry

    lax.fori_loop(0, device_count, sort_step, 0, unroll=2)

    def spread_step(block, carry):
        spread_copy(block).wait()
        rows = pl.ds(pl.multiple_of(block * 32, 32), 32)

        def one(spot):
            picked = jnp.zeros((32, 2 * lanes), BF16)
            for peer in range(device_count):
                place = place_ref[peer, block]
                picked = jnp.where(
                    place == lax.convert_element_type(spot, BF16),
                    sorted_scr[peer, rows, :],
                    picked,
                )
            low_order = block * device_count + spot
            column = jnp.concatenate([picked[:, :lanes], picked[:, lanes:]], axis=0)
            stage = jnp.dot(
                spread_scr[low_order],
                jnp.concatenate([column, column], axis=0),
                preferred_element_type=F32,
            )
            middle_scr[pl.ds(low_order * PADDED, 2 * SIDE), :] = stage

        if device_count <= 8:
            for spot in range(device_count):
                one(spot)
        else:
            lax.fori_loop(0, device_count, lambda s, x: (one(s), x)[1], 0)
        return carry

    lax.fori_loop(0, blocks, spread_step, 0)

    def pixel_step(step, total):
        for inner in range(8):
            first = step * 8 + inner
            column = jnp.concatenate(
                [
                    middle_scr[pl.ds(first, SIDE, stride=PADDED), :],
                    middle_scr[pl.ds(first + SIDE, SIDE, stride=PADDED), :],
                ],
                axis=0,
            )
            high, low = two_parts(column)
            stage = jnp.dot(
                pixel_ref[...], jnp.concatenate([high, low], axis=1), preferred_element_type=F32
            )
            field = stage[:SIDE, :lanes] + stage[:SIDE, lanes:] + stage[SIDE:, :lanes]
            other = pltpu.roll(field, lanes // 2, 1)
            product = other * jnp.where(lane < lanes // 2, other, field)
            product_scr[first] = product
            total = total + jnp.sum(product.reshape(8, 8, lanes), axis=0)
        return total

    total = lax.fori_loop(0, SIDE // 8, pixel_step, jnp.zeros((8, lanes), F32))
    mean = jnp.sum(total, axis=0, keepdims=True) * (1.0 / NPIX)

    def back_step(step, carry):
        for inner in range(8):
            first = step * 8 + inner
            high, low = two_parts(product_scr[first] - mean)
            stage = jnp.dot(
                back_ref[...], jnp.concatenate([high, low], axis=0), preferred_element_type=F32
            )
            back_scr[pl.ds(first * PADDED, 2 * SIDE), :] = stage[: 2 * SIDE] + stage[2 * SIDE :]
        return carry

    lax.fori_loop(0, SIDE // 8, back_step, 0)
    gather_copy.wait()

    def gather_step(block, carry):
        rows = pl.ds(pl.multiple_of(block * 32, 32), 32)

        def one(spot):
            low_order = block * device_count + spot
            column = jnp.concatenate(
                [
                    back_scr[pl.ds(low_order, SIDE, stride=PADDED), :],
                    back_scr[pl.ds(low_order + SIDE, SIDE, stride=PADDED), :],
                ],
                axis=0,
            )
            high, low = two_parts(column)
            stage = jnp.dot(
                gather_scr[low_order],
                jnp.concatenate([high, low], axis=1),
                preferred_element_type=F32,
            )
            value = stage[:SIDE, :lanes] + stage[:SIDE, lanes:] + stage[SIDE:, :lanes]
            value = (value * scale).astype(BF16)
            return jnp.concatenate([value[:32], value[32:]], axis=1)

        if device_count <= 8:
            found = [one(spot) for spot in range(device_count)]
            for peer in range(device_count):
                place = place_ref[peer, block]
                picked = found[0]
                for spot in range(1, device_count):
                    picked = jnp.where(place == spot, found[spot], picked)
                sorted_scr[peer, rows, :] = picked
        else:

            def spot_step(spot, carry):
                value = one(spot)
                for peer in range(device_count):
                    sorted_scr[peer, rows, :] = jnp.where(
                        place_ref[peer, block] == lax.convert_element_type(spot, BF16),
                        value,
                        sorted_scr[peer, rows, :],
                    )
                return carry

            lax.fori_loop(0, device_count, spot_step, 0)
        return carry

    lax.fori_loop(0, blocks, gather_step, 0)

    def unsort_step(peer, carry):
        slots = jnp.dot(
            unsort_ref[peer], sorted_scr[peer], preferred_element_type=F32
        ).astype(BF16)
        start = 0
        for out, size in zip(outs, sizes):
            out[peer] = slots[start : start + size]
            start += size
        return carry

    lax.fori_loop(0, device_count, unsort_step, 0, unroll=2)


def cycle_work(pieces, sizes, places, sort, unsort, offset, where, cycle_weight):
    groups = len(pieces)
    device_count, _, lanes = pieces[0].shape
    count = sum(piece.shape[1] for piece in pieces)
    out_shapes = [(device_count, size, lanes) for size in sizes]
    spread, pixel, back, gather = [jnp.asarray(table) for table in fourier_tables()]
    tables = [places, sort, unsort]
    return pl.pallas_call(
        functools.partial(cycle_kernel, groups, sizes),
        grid_spec=pltpu.PrefetchScalarGridSpec(
            num_scalar_prefetch=2,
            grid=(1,),
            in_specs=[pl.BlockSpec(memory_space=pltpu.SMEM)]
            + [whole(piece.shape) for piece in pieces]
            + [whole(table.shape) for table in tables]
            + [hbm(), whole(pixel.shape), whole(back.shape), hbm()],
            out_specs=[whole(shape) for shape in out_shapes],
            scratch_shapes=[
                pltpu.VMEM(spread.shape[1:], BF16),
                pltpu.VMEM(gather.shape[1:], BF16),
                pltpu.VMEM((device_count, count, lanes), BF16),
                pltpu.VMEM((SIDE * PADDED, lanes // 2), F32),
                pltpu.VMEM((SIDE, SIDE, lanes // 2), F32),
                pltpu.VMEM((SIDE * PADDED, lanes // 2), F32),
                pltpu.SemaphoreType.DMA((places.shape[1] + 1,)),
            ],
        ),
        out_shape=[jax.ShapeDtypeStruct(shape, BF16) for shape in out_shapes],
        compiler_params=pltpu.CompilerParams(vmem_limit_bytes=48 * MIB),
        cost_estimate=pl.CostEstimate(
            flops=4 * SIDE * 128 * 256 * 256 * 2, bytes_accessed=8 * MIB, transcendentals=0
        ),
        name="cycle_work",
    )(offset, where, cycle_weight, *pieces, *tables, spread, pixel, back, gather)


def adjoint_kernel(
    first, order_ref, where_ref, own_ref, core_ref, far_ref, corner_ref, weight_ref, legendre_ref, *refs
):
    out_ref, values_even, values_odd, terms_even, terms_odd = refs[-5:]
    step = pl.program_id(0)
    row = where_ref[0]
    base = where_ref[1] + first + step * BLOCK
    degrees = weight_ref.shape[1]
    cycles = legendre_ref.shape[1]
    owners = cycles // 4
    lanes = weight_ref.shape[0] // 2
    pitch = cycles + 8
    tiles = degrees // 128
    quarter = owners * 16
    degree = row * degrees + lax.broadcasted_iota(jnp.int32, (8, degrees), 1)
    sublane = lax.broadcasted_iota(jnp.int32, (8, degrees), 0)
    sources = (own_ref, core_ref, far_ref, corner_ref)
    for group in range(BLOCK // 16):
        values_scr = values_odd if group % 2 else values_even
        terms_scr = terms_odd if group % 2 else terms_even
        for place in range(16):
            wide = legendre_ref[group * 16 + place].astype(F32)
            for tile in range(tiles):
                values_scr[tile, place * pitch : place * pitch + cycles, :] = wide[
                    :, tile * 128 : tile * 128 + 128
                ]
        rows = jnp.concatenate(
            [
                source[
                    :, group * 16 : group * 16 + 16, part * lanes : (part + 1) * lanes
                ].reshape(quarter, lanes)
                for part in range(2)
                for source in sources
            ],
            axis=0,
        )
        terms_scr[...] = jnp.dot(
            jnp.concatenate([rows, rows], axis=1), weight_ref[...], preferred_element_type=F32
        )
        for half in range(2):
            total = [jnp.zeros((8, degrees), F32), jnp.zeros((8, degrees), F32)]
            for away in range(4):
                for owner in range(owners):
                    cycle = 4 * owner + (row ^ away)
                    factor = jnp.concatenate(
                        [
                            values_scr[tile, pl.ds(half * 8 * pitch + cycle, 8, stride=pitch), :]
                            for tile in range(tiles)
                        ],
                        axis=1,
                    )
                    for part in range(2):
                        at = (part * 4 + away) * quarter + owner * 16 + half * 8
                        total[part] = total[part] + terms_scr[at : at + 8, :] * factor
            lowest = jnp.zeros((8, degrees), jnp.int32)
            first_slot = group * 16 + half * 8
            for place in range(8):
                lowest = jnp.where(sublane == place, order_ref[base + first_slot + place], lowest)
            for part in range(2):
                out_ref[part, first_slot : first_slot + 8, :] = jnp.where(
                    degree >= lowest, total[part], 0.0
                )


def adjoint(first, orders, where, weight, pieces, legendre, earlier):
    orders_here, cycles, degrees = legendre.shape
    count = pieces[0].shape[1]
    steps = count // BLOCK
    start = first // BLOCK
    owners = cycles // 4
    lanes = weight.shape[0] // 2
    piece_spec = pl.BlockSpec((owners, BLOCK, 2 * lanes), lambda t, *_: (0, t, 0))
    out = jax.ShapeDtypeStruct((2, orders_here, degrees), F32)
    return pl.pallas_call(
        functools.partial(adjoint_kernel, first),
        grid_spec=pltpu.PrefetchScalarGridSpec(
            num_scalar_prefetch=2,
            grid=(steps,),
            in_specs=[piece_spec] * 4
            + [
                whole(weight.shape),
                pl.BlockSpec((BLOCK, cycles, degrees), lambda t, *_: (start + t, 0, 0)),
            ]
            + [anywhere()] * len(earlier),
            out_specs=pl.BlockSpec((2, BLOCK, degrees), lambda t, *_: (0, start + t, 0)),
            scratch_shapes=[
                pltpu.VMEM((degrees // 128, 16 * (cycles + 8), 128), F32),
                pltpu.VMEM((degrees // 128, 16 * (cycles + 8), 128), F32),
                pltpu.VMEM((32 * cycles, degrees), F32),
                pltpu.VMEM((32 * cycles, degrees), F32),
            ],
        ),
        out_shape=out,
        input_output_aliases={8: 0} if earlier else {},
        compiler_params=pltpu.CompilerParams(vmem_limit_bytes=48 * MIB),
        cost_estimate=pl.CostEstimate(
            flops=2 * count * cycles * degrees * lanes * 2 * 2,
            bytes_accessed=count * (cycles * degrees * 2 + 2 * cycles * lanes * 2),
            transcendentals=0,
        ),
        name="adjoint",
    )(orders, where, *pieces, weight, legendre, *earlier)


def slot_tables(orders, device_count):
    local_orders = orders.shape[0] // device_count
    blocks = local_orders // 32
    by_device = orders.reshape(device_count, local_orders)
    block = by_device // device_count
    position = 32 * (block % blocks) + block // blocks
    wanted = jnp.arange(local_orders, dtype=jnp.int32)
    sort = position[:, None, :] == wanted[None, :, None]
    unsort = position[:, :, None] == wanted[None, None, :]
    place = jnp.sum(jnp.where(sort, (by_device % device_count)[:, None, :], 0), axis=2)
    place = place.reshape(device_count, blocks, 32, 1)
    place = jnp.broadcast_to(place, (device_count, blocks, 32, 256))
    return place.astype(BF16), sort.astype(BF16), unsort.astype(BF16)


def body(
    coeffs,
    legendre,
    alpha_table,
    beta_table,
    radial_weight,
    radius_index,
    orders,
    cycle_offset,
    cycle_weight,
):
    row_id = lax.axis_index("row")
    ma_id = lax.axis_index("ma")
    device_count = lax.axis_size("ma")
    row_count = lax.axis_size("row")
    local_orders = coeffs.shape[1]
    where = jnp.stack([row_id, ma_id * local_orders]).astype(jnp.int32)
    synth_weight, adjoint_weight = filter_weights(
        radius_index, radial_weight, alpha_table, beta_table
    )
    core_pairs = [(i, i ^ 1) for i in range(row_count)]
    far_pairs = [(i, i ^ 2) for i in range(row_count)]
    units = local_orders // 32
    counts = (2, (units - 2) // 2, (units - 1) // 2) if units > 4 else (units // 2, units // 2)
    counts = [32 * count for count in counts]
    kept, others, outgoing, incoming, arrived = [], [], [], [], []

    def after(*values):
        return lax.optimization_barrier((where, *values))[0]

    def launch(chunk, token):
        first = sum(counts[:chunk])
        grant = 56
        keep, send = synth(
            first, counts[chunk], grant, orders, token, coeffs, synth_weight, legendre
        )
        kept.append(keep)
        others.append(lax.ppermute(send, "row", core_pairs))

    def pass_on(chunk, token):
        outgoing.append(core_sum(kept[chunk], others[chunk], token))
        incoming.append(lax.ppermute(outgoing[chunk], "row", far_pairs))

    def deliver(own, token):
        summed = full_sum(list(zip(kept[own], others[own], incoming[own])), token)
        arrived.append(lax.all_to_all(summed, "ma", split_axis=0, concat_axis=0, tiled=True))
        return summed

    launch(0, where)
    launch(1, where)
    pass_on(0, after(kept[1]))
    pass_on(1, after(outgoing[0]))
    if len(counts) == 3:
        launch(2, after(outgoing[1], incoming[0]))
        pass_on(2, after(deliver(slice(0, 2), after(kept[2]))))
        tables = slot_tables(lax.optimization_barrier((orders, outgoing[2]))[0], device_count)
        places, sort, unsort, token = lax.optimization_barrier((*tables, where))
        deliver(slice(2, 3), token)
    else:
        deliver(slice(0, 1), after(outgoing[1]))
        deliver(slice(1, 2), after(outgoing[1]))
        places, sort, unsort = slot_tables(orders, device_count)
    early = 32 * (units // 2)
    sizes = (early, local_orders - early)
    analysed = cycle_work(
        arrived, sizes, places, sort, unsort, cycle_offset, where, cycle_weight
    )
    own = [
        lax.all_to_all(piece, "ma", split_axis=0, concat_axis=0, tiled=True) for piece in analysed
    ]
    far = lax.ppermute(own[0], "row", far_pairs)
    far, second = lax.optimization_barrier((far, own[1]))
    gradient, first = [], 0
    for own_part, far_part in ((own[0], far), (second, None)):
        if far_part is None:
            far_part = lax.ppermute(own_part, "row", far_pairs)
        if gradient:
            far_part, gradient[-1] = lax.optimization_barrier((far_part, gradient[-1]))
        core = lax.ppermute(own_part, "row", core_pairs)
        corner = lax.ppermute(far_part, "row", core_pairs)
        gradient.append(
            adjoint(
                first,
                orders,
                where,
                adjoint_weight,
                (own_part, core, far_part, corner),
                legendre,
                gradient[-1:],
            )
        )
        first += own_part.shape[1]
    return gradient[-1]


def solution(mesh):
    in_specs = (
        P(None, "ma", "row"),
        P("ma", None, "row"),
        P(None, "row"),
        P(None, "row"),
        P(),
        P(),
        P(),
        P("ma"),
        P("ma"),
    )
    out_specs = P(None, "ma", "row")
    return jax.shard_map(body, mesh=mesh, in_specs=in_specs, out_specs=out_specs, check_vma=False)
```

```python
import functools
import math

import jax
import jax.numpy as jnp
import numpy as np
from jax import lax
from jax.experimental import pallas as pl
from jax.experimental.pallas import tpu as pltpu
from jax.sharding import PartitionSpec as P

NPIX = 4096
SIDE = 64
PADDED = 136
SYNTH_BLOCK = 16
BLOCK = 32
MIB = 1 << 20
F32 = jnp.float32
BF16 = jnp.bfloat16


def split_table(table):
    high = table.astype(jnp.bfloat16)
    low = (table - high.astype(np.float64)).astype(jnp.bfloat16)
    return high, low


@functools.lru_cache(maxsize=None)
def fourier_tables():
    first = np.arange(SIDE)
    spin = np.arange(2).reshape(2, 1, 1, 1, 1, 1)
    order = SIDE * np.arange(32)[None, :] + np.arange(SIDE)[:, None]
    order = order.reshape(1, SIDE, 1, 1, 1, 32)
    angle = (2 * first.reshape(1, 1, 1, SIDE, 1, 1) + spin) * order % (2 * NPIX) * (math.pi / NPIX)
    cosine, sine = np.cos(angle), np.sin(angle)
    row_part = np.arange(2).reshape(1, 1, 2, 1, 1, 1)
    col_part = np.arange(2).reshape(1, 1, 1, 1, 2, 1)
    same = (row_part == col_part).astype(np.float64)
    cross = np.where(row_part == 1, 1.0, -1.0) * (row_part != col_part)
    doubling = np.where(order == 0, 1.0, 2.0)
    spread = (doubling * (same * cosine + cross * sine)).reshape(2, SIDE, 2 * SIDE, SIDE)
    gather = (same * cosine + cross * sine).reshape(2, SIDE, 2 * SIDE, SIDE)
    gather = np.swapaxes(gather, 2, 3)
    spread_parts = np.concatenate(split_table(spread), axis=3)
    gather_parts = np.concatenate(split_table(gather), axis=2)
    square = first[:, None] * first[None, :] % SIDE * (2.0 * math.pi / SIDE)
    pixel = np.concatenate(split_table(np.concatenate([np.cos(square), -np.sin(square)], axis=1)), axis=0)
    back_high, back_low = split_table(np.concatenate([np.cos(square), -np.sin(square)], axis=0))
    back = np.concatenate([np.tile(back_high, (1, 2)), np.tile(back_low, (1, 2))], axis=0)
    return spread_parts, pixel, back, gather_parts


def two_parts(value):
    high = value.astype(BF16)
    low = (value - high.astype(F32)).astype(BF16)
    return high, low


def whole(shape):
    return pl.BlockSpec(shape, lambda t, *_: (0,) * len(shape))


def anywhere():
    return pl.BlockSpec(memory_space=pl.ANY)


def hbm():
    return pl.BlockSpec(memory_space=pltpu.HBM)


def weights_kernel(
    node_ref,
    radial_ref,
    alpha_ref,
    beta_ref,
    synth_ref,
    adjoint_ref,
    alpha_scr,
    beta_scr,
    filter_scr,
    weighted_scr,
    sems,
):
    copies = [
        pltpu.make_async_copy(alpha_ref, alpha_scr, sems.at[0]),
        pltpu.make_async_copy(beta_ref, beta_scr, sems.at[1]),
    ]
    for copy in copies:
        copy.start()
    for copy in copies:
        copy.wait()
    radii = node_ref.shape[0]

    def gather(radius, carry):
        node = node_ref[radius]
        scale = radial_ref[node]
        alpha = alpha_scr[pl.ds(node, 1), :]
        beta = beta_scr[pl.ds(node, 1), :]
        filter_scr[pl.ds(radius, 1), :] = alpha
        filter_scr[pl.ds(radii + radius, 1), :] = beta
        weighted_scr[pl.ds(radius, 1), :] = scale * alpha
        weighted_scr[pl.ds(radii + radius, 1), :] = (2.0 * scale) * beta
        return carry

    lax.fori_loop(0, radii, gather, 0, unroll=8)
    high, low = two_parts(filter_scr[...].T)
    synth_ref[:, : 2 * radii] = high
    synth_ref[:, 2 * radii :] = low
    high, low = two_parts(weighted_scr[...])
    adjoint_ref[: 2 * radii, :] = high
    adjoint_ref[2 * radii :, :] = low


def filter_weights(radius_index, radial_weight, alpha_table, beta_table):
    radii = radius_index.shape[0]
    degrees = alpha_table.shape[1]
    return pl.pallas_call(
        weights_kernel,
        grid_spec=pltpu.PrefetchScalarGridSpec(
            num_scalar_prefetch=2,
            grid=(1,),
            in_specs=[hbm(), hbm()],
            out_specs=[whole((degrees, 4 * radii)), whole((4 * radii, degrees))],
            scratch_shapes=[pltpu.VMEM(alpha_table.shape, F32)] * 2
            + [pltpu.VMEM((2 * radii, degrees), F32)] * 2
            + [pltpu.SemaphoreType.DMA((2,))],
        ),
        out_shape=[
            jax.ShapeDtypeStruct((degrees, 4 * radii), BF16),
            jax.ShapeDtypeStruct((4 * radii, degrees), BF16),
        ],
        compiler_params=pltpu.CompilerParams(vmem_limit_bytes=56 * MIB),
        name="filter_weights",
    )(radius_index, radial_weight, alpha_table, beta_table)


def synth_kernel(
    first, order_ref, where_ref, coeffs_ref, weight_ref, legendre_ref, *refs
):
    keep_ref, send_ref, terms_even, terms_odd, sums_even, sums_odd = refs[-6:]
    step = pl.program_id(0)
    row = where_ref[0] >> 12
    base = (where_ref[0] & 4095) + first + step * SYNTH_BLOCK
    degrees = coeffs_ref.shape[2]
    cycles = legendre_ref.shape[1]
    owners = cycles // 4
    lanes = weight_ref.shape[1] // 2
    degree = row * degrees + lax.broadcasted_iota(jnp.int32, (1, degrees), 1)
    half = 16 * cycles
    for group in range(SYNTH_BLOCK // 8):
        terms = terms_odd if group % 2 else terms_even
        sums = sums_odd if group % 2 else sums_even
        for place in range(8):
            slot = group * 8 + place
            live = degree >= order_ref[base + slot]
            values = legendre_ref[slot].astype(F32)
            for part in range(2):
                coeff = jnp.where(live, coeffs_ref[part, slot : slot + 1, :], 0.0)
                high, low = two_parts(values * coeff)
                start = (part * 8 + place) * cycles
                terms[start : start + cycles, :] = high
                terms[half + start : half + start + cycles, :] = low
        both = jnp.dot(terms[...], weight_ref[...], preferred_element_type=F32)
        sums[...] = both[:half, :lanes] + both[:half, lanes:] + both[half:, :lanes]
        for part in range(2):
            for owner in range(owners):
                for away in range(4):
                    cycle = 4 * owner + (row ^ away)
                    piece = sums[pl.ds(part * 8 * cycles + cycle, 8, stride=cycles), :]
                    target = send_ref if away % 2 else keep_ref
                    target[
                        away // 2,
                        owner,
                        group * 8 : group * 8 + 8,
                        part * lanes : (part + 1) * lanes,
                    ] = piece


def synth(first, count, orders, where, coeffs, weight, legendre):
    cycles, degrees = legendre.shape[1:]
    steps = count // SYNTH_BLOCK
    start = first // SYNTH_BLOCK
    owners = cycles // 4
    lanes = weight.shape[1] // 2
    out = jax.ShapeDtypeStruct((2, owners, count, 2 * lanes), F32)
    out_spec = pl.BlockSpec((2, owners, SYNTH_BLOCK, 2 * lanes), lambda t, *_: (0, 0, t, 0))
    return pl.pallas_call(
        functools.partial(synth_kernel, first),
        grid_spec=pltpu.PrefetchScalarGridSpec(
            num_scalar_prefetch=2,
            grid=(steps,),
            in_specs=[
                pl.BlockSpec((2, SYNTH_BLOCK, degrees), lambda t, *_: (0, start + t, 0)),
                whole(weight.shape),
                pl.BlockSpec((SYNTH_BLOCK, cycles, degrees), lambda t, *_: (start + t, 0, 0)),
            ],
            out_specs=[out_spec, out_spec],
            scratch_shapes=[
                pltpu.VMEM((32 * cycles, degrees), BF16),
                pltpu.VMEM((32 * cycles, degrees), BF16),
                pltpu.VMEM((16 * cycles, lanes), F32),
                pltpu.VMEM((16 * cycles, lanes), F32),
            ],
        ),
        out_shape=[out, out],
        compiler_params=pltpu.CompilerParams(vmem_limit_bytes=56 * MIB),
        cost_estimate=pl.CostEstimate(
            flops=2 * count * cycles * degrees * lanes * 2 * 4,
            bytes_accessed=count * (cycles * degrees * 2 + 2 * cycles * lanes * 4),
            transcendentals=0,
        ),
        name="synth",
    )(orders, where, coeffs, weight, legendre)


def core_sum_kernel(keep_ref, other_ref, token_ref, out_ref):
    out_ref[...] = (keep_ref[0] + other_ref[0]).astype(BF16)


def core_sum(keep, other, order):
    shape = keep.shape[1:]
    half = pl.BlockSpec((1,) + shape, lambda t: (1, 0, 0, 0))
    return pl.pallas_call(
        core_sum_kernel,
        grid=(1,),
        in_specs=[half, half, pl.BlockSpec(memory_space=pltpu.SMEM)],
        out_specs=pl.BlockSpec(shape, lambda t: (0, 0, 0)),
        out_shape=jax.ShapeDtypeStruct(shape, BF16),
        compiler_params=pltpu.CompilerParams(vmem_limit_bytes=16 * MIB),
        cost_estimate=pl.CostEstimate(flops=4 * 10**10, bytes_accessed=MIB, transcendentals=0),
        name="core_sum",
    )(keep, other, order)


def own_sum_kernel(keep_ref, other_ref, token_ref, out_ref):
    out_ref[...] = keep_ref[0] + other_ref[0]


def own_sum(keep, other, token):
    shape = keep.shape[1:]
    half = pl.BlockSpec((1,) + shape, lambda t: (0, 0, 0, 0))
    return pl.pallas_call(
        own_sum_kernel,
        grid=(1,),
        in_specs=[half, half, pl.BlockSpec(memory_space=pltpu.SMEM)],
        out_specs=pl.BlockSpec(shape, lambda t: (0, 0, 0)),
        out_shape=jax.ShapeDtypeStruct(shape, F32),
        compiler_params=pltpu.CompilerParams(vmem_limit_bytes=16 * MIB),
        cost_estimate=pl.CostEstimate(flops=10**7, bytes_accessed=MIB, transcendentals=0),
        name="own_sum",
    )(keep, other, token)


def last_sum_kernel(own_ref, incoming_ref, token_ref, out_ref):
    out_ref[...] = (own_ref[...] + incoming_ref[...].astype(F32)).astype(BF16)


def last_sum(own, incoming, token):
    return pl.pallas_call(
        last_sum_kernel,
        grid=(1,),
        in_specs=[whole(own.shape), whole(own.shape), pl.BlockSpec(memory_space=pltpu.SMEM)],
        out_specs=whole(own.shape),
        out_shape=jax.ShapeDtypeStruct(own.shape, BF16),
        compiler_params=pltpu.CompilerParams(vmem_limit_bytes=16 * MIB),
        cost_estimate=pl.CostEstimate(flops=4 * 10**10, bytes_accessed=MIB, transcendentals=0),
        name="last_sum",
    )(own, incoming, token)


def full_sum_kernel(token_ref, *refs):
    out_ref = refs[-1]
    start = 0
    for index in range(0, len(refs) - 1, 3):
        keep_ref, other_ref, incoming_ref = refs[index : index + 3]
        count = incoming_ref.shape[1]
        total = keep_ref[0] + other_ref[0] + incoming_ref[...].astype(F32)
        out_ref[:, start : start + count] = total.astype(BF16)
        start += count


def full_sum(chunks, order):
    operands, specs, count = [], [pl.BlockSpec(memory_space=pltpu.SMEM)], 0
    for keep, other, incoming in chunks:
        shape = incoming.shape
        half = pl.BlockSpec((1,) + shape, lambda t: (0, 0, 0, 0))
        operands += [keep, other, incoming]
        specs += [half, half, pl.BlockSpec(shape, lambda t: (0, 0, 0))]
        count += shape[1]
    full = (shape[0], count, shape[2])
    return pl.pallas_call(
        full_sum_kernel,
        grid=(1,),
        in_specs=specs,
        out_specs=pl.BlockSpec(full, lambda t: (0, 0, 0)),
        out_shape=jax.ShapeDtypeStruct(full, BF16),
        compiler_params=pltpu.CompilerParams(vmem_limit_bytes=16 * MIB),
        cost_estimate=pl.CostEstimate(flops=4 * 10**10, bytes_accessed=MIB, transcendentals=0),
        name="full_sum",
    )(order, *operands)


def cycle_kernel(groups, sizes, offset_ref, where_ref, weight_ref, *refs):
    pieces = refs[:groups]
    place_ref, sort_ref, unsort_ref, spread_ref, pixel_ref, back_ref, gather_ref = refs[
        groups : groups + 7
    ]
    outs = refs[groups + 7 : groups + 7 + len(sizes)]
    spread_scr, gather_scr, sorted_scr, middle_scr, product_scr, back_scr, sems = refs[-7:]
    device_count, blocks = place_ref.shape[:2]
    lanes = pieces[0].shape[2] // 2
    turned = offset_ref[where_ref[0] >> 12]
    scale = weight_ref[where_ref[0] >> 12]
    lane = lax.broadcasted_iota(jnp.int32, (SIDE, lanes), 1)

    def spread_copy(block):
        rows = pl.ds(block * device_count, device_count)
        return pltpu.make_async_copy(
            spread_ref.at[turned, rows], spread_scr.at[rows], sems.at[block]
        )

    gather_copy = pltpu.make_async_copy(gather_ref.at[turned], gather_scr, sems.at[blocks])
    for block in range(blocks):
        spread_copy(block).start()
    gather_copy.start()

    def sort_step(peer, carry):
        slots = jnp.concatenate([piece[peer] for piece in pieces], axis=0)
        sorted_scr[peer] = jnp.dot(
            sort_ref[peer], slots, preferred_element_type=F32
        ).astype(BF16)
        return carry

    lax.fori_loop(0, device_count, sort_step, 0, unroll=2)

    def spread_step(block, carry):
        spread_copy(block).wait()
        rows = pl.ds(pl.multiple_of(block * 32, 32), 32)

        def one(spot):
            picked = jnp.zeros((32, 2 * lanes), BF16)
            for peer in range(device_count):
                place = place_ref[peer, block]
                picked = jnp.where(
                    place == lax.convert_element_type(spot, BF16),
                    sorted_scr[peer, rows, :],
                    picked,
                )
            low_order = block * device_count + spot
            column = jnp.concatenate([picked[:, :lanes], picked[:, lanes:]], axis=0)
            stage = jnp.dot(
                spread_scr[low_order],
                jnp.concatenate([column, column], axis=0),
                preferred_element_type=F32,
            )
            middle_scr[pl.ds(low_order * PADDED, 2 * SIDE), :] = stage

        if device_count <= 8:
            for spot in range(device_count):
                one(spot)
        else:
            lax.fori_loop(0, device_count, lambda s, x: (one(s), x)[1], 0)
        return carry

    lax.fori_loop(0, blocks, spread_step, 0)

    def pixel_step(step, total):
        for inner in range(8):
            first = step * 8 + inner
            column = jnp.concatenate(
                [
                    middle_scr[pl.ds(first, SIDE, stride=PADDED), :],
                    middle_scr[pl.ds(first + SIDE, SIDE, stride=PADDED), :],
                ],
                axis=0,
            )
            high, low = two_parts(column)
            stage = jnp.dot(
                pixel_ref[...], jnp.concatenate([high, low], axis=1), preferred_element_type=F32
            )
            field = stage[:SIDE, :lanes] + stage[:SIDE, lanes:] + stage[SIDE:, :lanes]
            other = pltpu.roll(field, lanes // 2, 1)
            product = other * jnp.where(lane < lanes // 2, other, field)
            product_scr[first] = product
            total = total + jnp.sum(product.reshape(8, 8, lanes), axis=0)
        return total

    total = lax.fori_loop(0, SIDE // 8, pixel_step, jnp.zeros((8, lanes), F32))
    mean = jnp.sum(total, axis=0, keepdims=True) * (1.0 / NPIX)

    def back_step(step, carry):
        for inner in range(8):
            first = step * 8 + inner
            high, low = two_parts(product_scr[first] - mean)
            stage = jnp.dot(
                back_ref[...], jnp.concatenate([high, low], axis=0), preferred_element_type=F32
            )
            back_scr[pl.ds(first * PADDED, 2 * SIDE), :] = stage[: 2 * SIDE] + stage[2 * SIDE :]
        return carry

    lax.fori_loop(0, SIDE // 8, back_step, 0)
    gather_copy.wait()

    def gather_step(block, carry):
        rows = pl.ds(pl.multiple_of(block * 32, 32), 32)

        def one(spot):
            low_order = block * device_count + spot
            column = jnp.concatenate(
                [
                    back_scr[pl.ds(low_order, SIDE, stride=PADDED), :],
                    back_scr[pl.ds(low_order + SIDE, SIDE, stride=PADDED), :],
                ],
                axis=0,
            )
            high, low = two_parts(column)
            stage = jnp.dot(
                gather_scr[low_order],
                jnp.concatenate([high, low], axis=1),
                preferred_element_type=F32,
            )
            value = stage[:SIDE, :lanes] + stage[:SIDE, lanes:] + stage[SIDE:, :lanes]
            value = (value * scale).astype(BF16)
            return jnp.concatenate([value[:32], value[32:]], axis=1)

        if device_count <= 8:
            found = [one(spot) for spot in range(device_count)]
            for peer in range(device_count):
                place = place_ref[peer, block]
                picked = found[0]
                for spot in range(1, device_count):
                    picked = jnp.where(place == spot, found[spot], picked)
                sorted_scr[peer, rows, :] = picked
        else:

            def spot_step(spot, carry):
                value = one(spot)
                for peer in range(device_count):
                    sorted_scr[peer, rows, :] = jnp.where(
                        place_ref[peer, block] == lax.convert_element_type(spot, BF16),
                        value,
                        sorted_scr[peer, rows, :],
                    )
                return carry

            lax.fori_loop(0, device_count, spot_step, 0)
        return carry

    lax.fori_loop(0, blocks, gather_step, 0)

    def unsort_step(peer, carry):
        slots = jnp.dot(
            unsort_ref[peer], sorted_scr[peer], preferred_element_type=F32
        ).astype(BF16)
        start = 0
        for out, size in zip(outs, sizes):
            out[peer] = slots[start : start + size]
            start += size
        return carry

    lax.fori_loop(0, device_count, unsort_step, 0, unroll=2)


def cycle_work(pieces, sizes, places, sort, unsort, offset, where, cycle_weight):
    groups = len(pieces)
    device_count, count, lanes = pieces[0].shape
    out_shapes = [(device_count, size, lanes) for size in sizes]
    spread, pixel, back, gather = [jnp.asarray(table) for table in fourier_tables()]
    tables = [places, sort, unsort]
    return pl.pallas_call(
        functools.partial(cycle_kernel, groups, sizes),
        grid_spec=pltpu.PrefetchScalarGridSpec(
            num_scalar_prefetch=2,
            grid=(1,),
            in_specs=[pl.BlockSpec(memory_space=pltpu.SMEM)]
            + [whole(piece.shape) for piece in pieces]
            + [whole(table.shape) for table in tables]
            + [hbm(), whole(pixel.shape), whole(back.shape), hbm()],
            out_specs=[whole(shape) for shape in out_shapes],
            scratch_shapes=[
                pltpu.VMEM(spread.shape[1:], BF16),
                pltpu.VMEM(gather.shape[1:], BF16),
                pltpu.VMEM((device_count, groups * count, lanes), BF16),
                pltpu.VMEM((SIDE * PADDED, lanes // 2), F32),
                pltpu.VMEM((SIDE, SIDE, lanes // 2), F32),
                pltpu.VMEM((SIDE * PADDED, lanes // 2), F32),
                pltpu.SemaphoreType.DMA((places.shape[1] + 1,)),
            ],
        ),
        out_shape=[jax.ShapeDtypeStruct(shape, BF16) for shape in out_shapes],
        compiler_params=pltpu.CompilerParams(vmem_limit_bytes=48 * MIB),
        cost_estimate=pl.CostEstimate(
            flops=4 * SIDE * 128 * 256 * 256 * 2, bytes_accessed=8 * MIB, transcendentals=0
        ),
        name="cycle_work",
    )(offset, where, cycle_weight, *pieces, *tables, spread, pixel, back, gather)


def adjoint_kernel(
    first, order_ref, where_ref, own_ref, core_ref, far_ref, corner_ref, weight_ref, legendre_ref, *refs
):
    out_ref, values_even, values_odd, terms_even, terms_odd = refs[-5:]
    step = pl.program_id(0)
    row = where_ref[0] >> 12
    base = (where_ref[0] & 4095) + first + step * BLOCK
    degrees = weight_ref.shape[1]
    cycles = legendre_ref.shape[1]
    owners = cycles // 4
    lanes = weight_ref.shape[0] // 2
    pitch = cycles + 8
    tiles = degrees // 128
    quarter = owners * 16
    degree = row * degrees + lax.broadcasted_iota(jnp.int32, (8, degrees), 1)
    sublane = lax.broadcasted_iota(jnp.int32, (8, degrees), 0)
    sources = (own_ref, core_ref, far_ref, corner_ref)
    for group in range(BLOCK // 16):
        values_scr = values_odd if group % 2 else values_even
        terms_scr = terms_odd if group % 2 else terms_even
        for place in range(16):
            wide = legendre_ref[group * 16 + place].astype(F32)
            for tile in range(tiles):
                values_scr[tile, place * pitch : place * pitch + cycles, :] = wide[
                    :, tile * 128 : tile * 128 + 128
                ]
        rows = jnp.concatenate(
            [
                source[
                    :, group * 16 : group * 16 + 16, part * lanes : (part + 1) * lanes
                ].reshape(quarter, lanes)
                for part in range(2)
                for source in sources
            ],
            axis=0,
        )
        terms_scr[...] = jnp.dot(
            jnp.concatenate([rows, rows], axis=1), weight_ref[...], preferred_element_type=F32
        )
        for half in range(2):
            total = [jnp.zeros((8, degrees), F32), jnp.zeros((8, degrees), F32)]
            for away in range(4):
                for owner in range(owners):
                    cycle = 4 * owner + (row ^ away)
                    factor = jnp.concatenate(
                        [
                            values_scr[tile, pl.ds(half * 8 * pitch + cycle, 8, stride=pitch), :]
                            for tile in range(tiles)
                        ],
                        axis=1,
                    )
                    for part in range(2):
                        at = (part * 4 + away) * quarter + owner * 16 + half * 8
                        total[part] = total[part] + terms_scr[at : at + 8, :] * factor
            lowest = jnp.zeros((8, degrees), jnp.int32)
            first_slot = group * 16 + half * 8
            for place in range(8):
                lowest = jnp.where(sublane == place, order_ref[base + first_slot + place], lowest)
            for part in range(2):
                out_ref[part, first_slot : first_slot + 8, :] = jnp.where(
                    degree >= lowest, total[part], 0.0
                )


def adjoint(first, orders, where, weight, pieces, legendre, earlier):
    orders_here, cycles, degrees = legendre.shape
    count = pieces[0].shape[1]
    steps = count // BLOCK
    start = first // BLOCK
    owners = cycles // 4
    lanes = weight.shape[0] // 2
    piece_spec = pl.BlockSpec((owners, BLOCK, 2 * lanes), lambda t, *_: (0, t, 0))
    out = jax.ShapeDtypeStruct((2, orders_here, degrees), F32)
    return pl.pallas_call(
        functools.partial(adjoint_kernel, first),
        grid_spec=pltpu.PrefetchScalarGridSpec(
            num_scalar_prefetch=2,
            grid=(steps,),
            in_specs=[piece_spec] * 4
            + [
                whole(weight.shape),
                pl.BlockSpec((BLOCK, cycles, degrees), lambda t, *_: (start + t, 0, 0)),
            ]
            + [anywhere()] * len(earlier),
            out_specs=pl.BlockSpec((2, BLOCK, degrees), lambda t, *_: (0, start + t, 0)),
            scratch_shapes=[
                pltpu.VMEM((degrees // 128, 16 * (cycles + 8), 128), F32),
                pltpu.VMEM((degrees // 128, 16 * (cycles + 8), 128), F32),
                pltpu.VMEM((32 * cycles, degrees), F32),
                pltpu.VMEM((32 * cycles, degrees), F32),
            ],
        ),
        out_shape=out,
        input_output_aliases={8: 0} if earlier else {},
        compiler_params=pltpu.CompilerParams(vmem_limit_bytes=48 * MIB),
        cost_estimate=pl.CostEstimate(
            flops=2 * count * cycles * degrees * lanes * 2 * 2,
            bytes_accessed=count * (cycles * degrees * 2 + 2 * cycles * lanes * 2),
            transcendentals=0,
        ),
        name="adjoint",
    )(orders, where, *pieces, weight, legendre, *earlier)


def slot_tables(orders, device_count):
    local_orders = orders.shape[0] // device_count
    blocks = local_orders // 32
    by_device = orders.reshape(device_count, local_orders)
    block = by_device // device_count
    position = 32 * (block % blocks) + block // blocks
    wanted = jnp.arange(local_orders, dtype=jnp.int32)
    sort = position[:, None, :] == wanted[None, :, None]
    unsort = position[:, :, None] == wanted[None, None, :]
    place = jnp.sum(jnp.where(sort, (by_device % device_count)[:, None, :], 0), axis=2)
    place = place.reshape(device_count, blocks, 32, 1)
    place = jnp.broadcast_to(place, (device_count, blocks, 32, 256))
    return place.astype(BF16), sort.astype(BF16), unsort.astype(BF16)


def body(
    coeffs,
    legendre,
    alpha_table,
    beta_table,
    radial_weight,
    radius_index,
    orders,
    cycle_offset,
    cycle_weight,
):
    row_id = lax.axis_index("row")
    ma_id = lax.axis_index("ma")
    device_count = lax.axis_size("ma")
    row_count = lax.axis_size("row")
    local_orders = coeffs.shape[1]
    where = (row_id * 4096 + ma_id * local_orders).astype(jnp.int32).reshape(1)
    synth_weight, adjoint_weight = filter_weights(
        radius_index, radial_weight, alpha_table, beta_table
    )
    core_pairs = [(i, i ^ 1) for i in range(row_count)]
    far_pairs = [(i, i ^ 2) for i in range(row_count)]
    units = local_orders // 32
    counts = (units // 4, units // 4, units // 2) if units >= 4 else (units // 2, units // 2)
    counts = [32 * count for count in counts]
    kept, others, outgoing, incoming, arrived = [], [], [], [], []

    def after(*values):
        return lax.optimization_barrier((where, *values))[0]

    def launch(chunk, token):
        first = sum(counts[:chunk])
        keep, send = synth(
            first, counts[chunk], orders, token, coeffs, synth_weight, legendre
        )
        kept.append(keep)
        others.append(lax.ppermute(send, "row", core_pairs))

    def pass_on(chunk, token):
        outgoing.append(core_sum(kept[chunk], others[chunk], token))
        incoming.append(lax.ppermute(outgoing[chunk], "row", far_pairs))

    def deliver(own, token):
        summed = full_sum(list(zip(kept[own], others[own], incoming[own])), token)
        arrived.append(lax.all_to_all(summed, "ma", split_axis=0, concat_axis=0, tiled=True))
        return summed

    launch(0, where)
    launch(1, where)
    pass_on(0, after(kept[1]))
    pass_on(1, after(outgoing[0]))
    if len(counts) == 3:
        launch(2, after(outgoing[1]))
        pass_on(2, after(deliver(slice(0, 2), after(kept[2]))))
        tables = slot_tables(lax.optimization_barrier((orders, outgoing[2]))[0], device_count)
        half = own_sum(kept[2], others[2], after(outgoing[2]))
        places, sort, unsort, half, token = lax.optimization_barrier((*tables, half, where))
        summed = last_sum(half, incoming[2], token)
        arrived.append(lax.all_to_all(summed, "ma", split_axis=0, concat_axis=0, tiled=True))
    else:
        deliver(slice(0, 1), after(outgoing[1]))
        deliver(slice(1, 2), after(outgoing[1]))
        places, sort, unsort = slot_tables(orders, device_count)
    early = 32 * (units // 2)
    sizes = (early, local_orders - early)
    analysed = cycle_work(
        arrived, sizes, places, sort, unsort, cycle_offset, where, cycle_weight
    )
    own = [
        lax.all_to_all(piece, "ma", split_axis=0, concat_axis=0, tiled=True) for piece in analysed
    ]
    far = lax.ppermute(own[0], "row", far_pairs)
    far, second = lax.optimization_barrier((far, own[1]))
    gradient, first = [], 0
    for own_part, far_part in ((own[0], far), (second, None)):
        if far_part is None:
            far_part = lax.ppermute(own_part, "row", far_pairs)
        if gradient:
            far_part, gradient[-1] = lax.optimization_barrier((far_part, gradient[-1]))
        core = lax.ppermute(own_part, "row", core_pairs)
        corner = lax.ppermute(far_part, "row", core_pairs)
        gradient.append(
            adjoint(
                first,
                orders,
                where,
                adjoint_weight,
                (own_part, core, far_part, corner),
                legendre,
                gradient[-1:],
            )
        )
        first += own_part.shape[1]
    return gradient[-1]


def solution(mesh):
    in_specs = (
        P(None, "ma", "row"),
        P("ma", None, "row"),
        P(None, "row"),
        P(None, "row"),
        P(),
        P(),
        P(),
        P("ma"),
        P("ma"),
    )
    out_specs = P(None, "ma", "row")
    return jax.shard_map(body, mesh=mesh, in_specs=in_specs, out_specs=out_specs, check_vma=False)
```

```python
import functools
import math

import jax
import jax.numpy as jnp
import numpy as np
from jax import lax
from jax.experimental import pallas as pl
from jax.experimental.pallas import tpu as pltpu
from jax.sharding import PartitionSpec as P

NPIX = 4096
SIDE = 64
PADDED = 136
SYNTH_BLOCK = 16
BLOCK = 32
MIB = 1 << 20
F32 = jnp.float32
BF16 = jnp.bfloat16


def split_table(table):
    high = table.astype(jnp.bfloat16)
    low = (table - high.astype(np.float64)).astype(jnp.bfloat16)
    return high, low


@functools.lru_cache(maxsize=None)
def fourier_tables():
    first = np.arange(SIDE)
    spin = np.arange(2).reshape(2, 1, 1, 1, 1, 1)
    order = SIDE * np.arange(32)[None, :] + np.arange(SIDE)[:, None]
    order = order.reshape(1, SIDE, 1, 1, 1, 32)
    angle = (2 * first.reshape(1, 1, 1, SIDE, 1, 1) + spin) * order % (2 * NPIX) * (math.pi / NPIX)
    cosine, sine = np.cos(angle), np.sin(angle)
    row_part = np.arange(2).reshape(1, 1, 2, 1, 1, 1)
    col_part = np.arange(2).reshape(1, 1, 1, 1, 2, 1)
    same = (row_part == col_part).astype(np.float64)
    cross = np.where(row_part == 1, 1.0, -1.0) * (row_part != col_part)
    doubling = np.where(order == 0, 1.0, 2.0)
    spread = (doubling * (same * cosine + cross * sine)).reshape(2, SIDE, 2 * SIDE, SIDE)
    gather = (same * cosine + cross * sine).reshape(2, SIDE, 2 * SIDE, SIDE)
    gather = np.swapaxes(gather, 2, 3)
    spread_parts = np.concatenate(split_table(spread), axis=3)
    gather_parts = np.concatenate(split_table(gather), axis=2)
    square = first[:, None] * first[None, :] % SIDE * (2.0 * math.pi / SIDE)
    pixel = np.concatenate(split_table(np.concatenate([np.cos(square), -np.sin(square)], axis=1)), axis=0)
    back_high, back_low = split_table(np.concatenate([np.cos(square), -np.sin(square)], axis=0))
    back = np.concatenate([np.tile(back_high, (1, 2)), np.tile(back_low, (1, 2))], axis=0)
    return spread_parts, pixel, back, gather_parts


def two_parts(value):
    high = value.astype(BF16)
    low = (value - high.astype(F32)).astype(BF16)
    return high, low


def whole(shape):
    return pl.BlockSpec(shape, lambda t, *_: (0,) * len(shape))


def anywhere():
    return pl.BlockSpec(memory_space=pl.ANY)


def hbm():
    return pl.BlockSpec(memory_space=pltpu.HBM)


def weights_kernel(
    node_ref,
    radial_ref,
    alpha_ref,
    beta_ref,
    synth_ref,
    adjoint_ref,
    alpha_scr,
    beta_scr,
    filter_scr,
    weighted_scr,
    sems,
):
    copies = [
        pltpu.make_async_copy(alpha_ref, alpha_scr, sems.at[0]),
        pltpu.make_async_copy(beta_ref, beta_scr, sems.at[1]),
    ]
    for copy in copies:
        copy.start()
    for copy in copies:
        copy.wait()
    radii = node_ref.shape[0]

    def gather(radius, carry):
        node = node_ref[radius]
        scale = radial_ref[node]
        alpha = alpha_scr[pl.ds(node, 1), :]
        beta = beta_scr[pl.ds(node, 1), :]
        filter_scr[pl.ds(radius, 1), :] = alpha
        filter_scr[pl.ds(radii + radius, 1), :] = beta
        weighted_scr[pl.ds(radius, 1), :] = scale * alpha
        weighted_scr[pl.ds(radii + radius, 1), :] = (2.0 * scale) * beta
        return carry

    lax.fori_loop(0, radii, gather, 0, unroll=8)
    high, low = two_parts(filter_scr[...].T)
    synth_ref[:, : 2 * radii] = high
    synth_ref[:, 2 * radii :] = low
    high, low = two_parts(weighted_scr[...])
    adjoint_ref[: 2 * radii, :] = high
    adjoint_ref[2 * radii :, :] = low


def filter_weights(radius_index, radial_weight, alpha_table, beta_table):
    radii = radius_index.shape[0]
    degrees = alpha_table.shape[1]
    return pl.pallas_call(
        weights_kernel,
        grid_spec=pltpu.PrefetchScalarGridSpec(
            num_scalar_prefetch=2,
            grid=(1,),
            in_specs=[hbm(), hbm()],
            out_specs=[whole((degrees, 4 * radii)), whole((4 * radii, degrees))],
            scratch_shapes=[pltpu.VMEM(alpha_table.shape, F32)] * 2
            + [pltpu.VMEM((2 * radii, degrees), F32)] * 2
            + [pltpu.SemaphoreType.DMA((2,))],
        ),
        out_shape=[
            jax.ShapeDtypeStruct((degrees, 4 * radii), BF16),
            jax.ShapeDtypeStruct((4 * radii, degrees), BF16),
        ],
        compiler_params=pltpu.CompilerParams(vmem_limit_bytes=56 * MIB),
        name="filter_weights",
    )(radius_index, radial_weight, alpha_table, beta_table)


def synth_kernel(
    first, order_ref, where_ref, coeffs_ref, weight_ref, legendre_ref, *refs
):
    keep_ref, send_ref, terms_even, terms_odd, sums_even, sums_odd = refs[-6:]
    step = pl.program_id(0)
    row = where_ref[0] >> 12
    base = (where_ref[0] & 4095) + first + step * SYNTH_BLOCK
    degrees = coeffs_ref.shape[2]
    cycles = legendre_ref.shape[1]
    owners = cycles // 4
    lanes = weight_ref.shape[1] // 2
    degree = row * degrees + lax.broadcasted_iota(jnp.int32, (1, degrees), 1)
    half = 16 * cycles
    for group in range(SYNTH_BLOCK // 8):
        terms = terms_odd if group % 2 else terms_even
        sums = sums_odd if group % 2 else sums_even
        for place in range(8):
            slot = group * 8 + place
            live = degree >= order_ref[base + slot]
            values = legendre_ref[slot].astype(F32)
            for part in range(2):
                coeff = jnp.where(live, coeffs_ref[part, slot : slot + 1, :], 0.0)
                high, low = two_parts(values * coeff)
                start = (part * 8 + place) * cycles
                terms[start : start + cycles, :] = high
                terms[half + start : half + start + cycles, :] = low
        both = jnp.dot(terms[...], weight_ref[...], preferred_element_type=F32)
        sums[...] = both[:half, :lanes] + both[:half, lanes:] + both[half:, :lanes]
        for part in range(2):
            for owner in range(owners):
                for away in range(4):
                    cycle = 4 * owner + (row ^ away)
                    piece = sums[pl.ds(part * 8 * cycles + cycle, 8, stride=cycles), :]
                    target = send_ref if away % 2 else keep_ref
                    target[
                        away // 2,
                        owner,
                        group * 8 : group * 8 + 8,
                        part * lanes : (part + 1) * lanes,
                    ] = piece


def synth(first, count, orders, where, coeffs, weight, legendre):
    cycles, degrees = legendre.shape[1:]
    steps = count // SYNTH_BLOCK
    start = first // SYNTH_BLOCK
    owners = cycles // 4
    lanes = weight.shape[1] // 2
    out = jax.ShapeDtypeStruct((2, owners, count, 2 * lanes), F32)
    out_spec = pl.BlockSpec((2, owners, SYNTH_BLOCK, 2 * lanes), lambda t, *_: (0, 0, t, 0))
    return pl.pallas_call(
        functools.partial(synth_kernel, first),
        grid_spec=pltpu.PrefetchScalarGridSpec(
            num_scalar_prefetch=2,
            grid=(steps,),
            in_specs=[
                pl.BlockSpec((2, SYNTH_BLOCK, degrees), lambda t, *_: (0, start + t, 0)),
                whole(weight.shape),
                pl.BlockSpec((SYNTH_BLOCK, cycles, degrees), lambda t, *_: (start + t, 0, 0)),
            ],
            out_specs=[out_spec, out_spec],
            scratch_shapes=[
                pltpu.VMEM((32 * cycles, degrees), BF16),
                pltpu.VMEM((32 * cycles, degrees), BF16),
                pltpu.VMEM((16 * cycles, lanes), F32),
                pltpu.VMEM((16 * cycles, lanes), F32),
            ],
        ),
        out_shape=[out, out],
        compiler_params=pltpu.CompilerParams(vmem_limit_bytes=56 * MIB),
        cost_estimate=pl.CostEstimate(
            flops=2 * count * cycles * degrees * lanes * 2 * 4,
            bytes_accessed=count * (cycles * degrees * 2 + 2 * cycles * lanes * 4),
            transcendentals=0,
        ),
        name="synth",
    )(orders, where, coeffs, weight, legendre)


def core_sum_kernel(keep_ref, other_ref, token_ref, out_ref):
    out_ref[...] = (keep_ref[0] + other_ref[0]).astype(BF16)


def core_sum(keep, other, order):
    shape = keep.shape[1:]
    half = pl.BlockSpec((1,) + shape, lambda t: (1, 0, 0, 0))
    return pl.pallas_call(
        core_sum_kernel,
        grid=(1,),
        in_specs=[half, half, pl.BlockSpec(memory_space=pltpu.SMEM)],
        out_specs=pl.BlockSpec(shape, lambda t: (0, 0, 0)),
        out_shape=jax.ShapeDtypeStruct(shape, BF16),
        compiler_params=pltpu.CompilerParams(vmem_limit_bytes=16 * MIB),
        cost_estimate=pl.CostEstimate(flops=4 * 10**10, bytes_accessed=MIB, transcendentals=0),
        name="core_sum",
    )(keep, other, order)


def own_sum_kernel(keep_ref, other_ref, token_ref, out_ref):
    out_ref[...] = keep_ref[0] + other_ref[0]


def own_sum(keep, other, token):
    shape = keep.shape[1:]
    half = pl.BlockSpec((1,) + shape, lambda t: (0, 0, 0, 0))
    return pl.pallas_call(
        own_sum_kernel,
        grid=(1,),
        in_specs=[half, half, pl.BlockSpec(memory_space=pltpu.SMEM)],
        out_specs=pl.BlockSpec(shape, lambda t: (0, 0, 0)),
        out_shape=jax.ShapeDtypeStruct(shape, F32),
        compiler_params=pltpu.CompilerParams(vmem_limit_bytes=16 * MIB),
        cost_estimate=pl.CostEstimate(flops=10**7, bytes_accessed=MIB, transcendentals=0),
        name="own_sum",
    )(keep, other, token)


def last_sum_kernel(own_ref, incoming_ref, token_ref, out_ref):
    out_ref[...] = (own_ref[...] + incoming_ref[...].astype(F32)).astype(BF16)


def last_sum(own, incoming, token):
    return pl.pallas_call(
        last_sum_kernel,
        grid=(1,),
        in_specs=[whole(own.shape), whole(own.shape), pl.BlockSpec(memory_space=pltpu.SMEM)],
        out_specs=whole(own.shape),
        out_shape=jax.ShapeDtypeStruct(own.shape, BF16),
        compiler_params=pltpu.CompilerParams(vmem_limit_bytes=16 * MIB),
        cost_estimate=pl.CostEstimate(flops=4 * 10**10, bytes_accessed=MIB, transcendentals=0),
        name="last_sum",
    )(own, incoming, token)


def full_sum_kernel(token_ref, *refs):
    out_ref = refs[-1]
    start = 0
    for index in range(0, len(refs) - 1, 3):
        keep_ref, other_ref, incoming_ref = refs[index : index + 3]
        count = incoming_ref.shape[1]
        total = keep_ref[0] + other_ref[0] + incoming_ref[...].astype(F32)
        out_ref[:, start : start + count] = total.astype(BF16)
        start += count


def full_sum(chunks, order):
    operands, specs, count = [], [pl.BlockSpec(memory_space=pltpu.SMEM)], 0
    for keep, other, incoming in chunks:
        shape = incoming.shape
        half = pl.BlockSpec((1,) + shape, lambda t: (0, 0, 0, 0))
        operands += [keep, other, incoming]
        specs += [half, half, pl.BlockSpec(shape, lambda t: (0, 0, 0))]
        count += shape[1]
    full = (shape[0], count, shape[2])
    return pl.pallas_call(
        full_sum_kernel,
        grid=(1,),
        in_specs=specs,
        out_specs=pl.BlockSpec(full, lambda t: (0, 0, 0)),
        out_shape=jax.ShapeDtypeStruct(full, BF16),
        compiler_params=pltpu.CompilerParams(vmem_limit_bytes=16 * MIB),
        cost_estimate=pl.CostEstimate(flops=4 * 10**10, bytes_accessed=MIB, transcendentals=0),
        name="full_sum",
    )(order, *operands)


def cycle_kernel(groups, sizes, offset_ref, where_ref, weight_ref, *refs):
    pieces = refs[:groups]
    place_ref, sort_ref, unsort_ref, spread_ref, pixel_ref, back_ref, gather_ref = refs[
        groups : groups + 7
    ]
    outs = refs[groups + 7 : groups + 7 + len(sizes)]
    spread_scr, gather_scr, sorted_scr, middle_scr, product_scr, back_scr, sems = refs[-7:]
    device_count, blocks = place_ref.shape[:2]
    lanes = pieces[0].shape[2] // 2
    turned = offset_ref[where_ref[0] >> 12]
    scale = weight_ref[where_ref[0] >> 12]
    lane = lax.broadcasted_iota(jnp.int32, (SIDE, lanes), 1)

    def spread_copy(block):
        rows = pl.ds(block * device_count, device_count)
        return pltpu.make_async_copy(
            spread_ref.at[turned, rows], spread_scr.at[rows], sems.at[block]
        )

    gather_copy = pltpu.make_async_copy(gather_ref.at[turned], gather_scr, sems.at[blocks])
    for block in range(blocks):
        spread_copy(block).start()
    gather_copy.start()

    def sort_step(peer, carry):
        slots = jnp.concatenate([piece[peer] for piece in pieces], axis=0)
        sorted_scr[peer] = jnp.dot(
            sort_ref[peer], slots, preferred_element_type=F32
        ).astype(BF16)
        return carry

    lax.fori_loop(0, device_count, sort_step, 0, unroll=2)

    def spread_step(block, carry):
        spread_copy(block).wait()
        rows = pl.ds(pl.multiple_of(block * 32, 32), 32)

        def one(spot):
            picked = jnp.zeros((32, 2 * lanes), BF16)
            for peer in range(device_count):
                place = place_ref[peer, block]
                picked = jnp.where(
                    place == lax.convert_element_type(spot, BF16),
                    sorted_scr[peer, rows, :],
                    picked,
                )
            low_order = block * device_count + spot
            column = jnp.concatenate([picked[:, :lanes], picked[:, lanes:]], axis=0)
            stage = jnp.dot(
                spread_scr[low_order],
                jnp.concatenate([column, column], axis=0),
                preferred_element_type=F32,
            )
            middle_scr[pl.ds(low_order * PADDED, 2 * SIDE), :] = stage

        if device_count <= 8:
            for spot in range(device_count):
                one(spot)
        else:
            lax.fori_loop(0, device_count, lambda s, x: (one(s), x)[1], 0)
        return carry

    lax.fori_loop(0, blocks, spread_step, 0)

    def pixel_step(step, total):
        for inner in range(8):
            first = step * 8 + inner
            column = jnp.concatenate(
                [
                    middle_scr[pl.ds(first, SIDE, stride=PADDED), :],
                    middle_scr[pl.ds(first + SIDE, SIDE, stride=PADDED), :],
                ],
                axis=0,
            )
            high, low = two_parts(column)
            stage = jnp.dot(
                pixel_ref[...], jnp.concatenate([high, low], axis=1), preferred_element_type=F32
            )
            field = stage[:SIDE, :lanes] + stage[:SIDE, lanes:] + stage[SIDE:, :lanes]
            other = pltpu.roll(field, lanes // 2, 1)
            product = other * jnp.where(lane < lanes // 2, other, field)
            product_scr[first] = product
            total = total + jnp.sum(product.reshape(8, 8, lanes), axis=0)
        return total

    total = lax.fori_loop(0, SIDE // 8, pixel_step, jnp.zeros((8, lanes), F32))
    mean = jnp.sum(total, axis=0, keepdims=True) * (1.0 / NPIX)

    def back_step(step, carry):
        for inner in range(8):
            first = step * 8 + inner
            high, low = two_parts(product_scr[first] - mean)
            stage = jnp.dot(
                back_ref[...], jnp.concatenate([high, low], axis=0), preferred_element_type=F32
            )
            back_scr[pl.ds(first * PADDED, 2 * SIDE), :] = stage[: 2 * SIDE] + stage[2 * SIDE :]
        return carry

    lax.fori_loop(0, SIDE // 8, back_step, 0)
    gather_copy.wait()

    def gather_step(block, carry):
        rows = pl.ds(pl.multiple_of(block * 32, 32), 32)

        def one(spot):
            low_order = block * device_count + spot
            column = jnp.concatenate(
                [
                    back_scr[pl.ds(low_order, SIDE, stride=PADDED), :],
                    back_scr[pl.ds(low_order + SIDE, SIDE, stride=PADDED), :],
                ],
                axis=0,
            )
            high, low = two_parts(column)
            stage = jnp.dot(
                gather_scr[low_order],
                jnp.concatenate([high, low], axis=1),
                preferred_element_type=F32,
            )
            value = stage[:SIDE, :lanes] + stage[:SIDE, lanes:] + stage[SIDE:, :lanes]
            value = (value * scale).astype(BF16)
            return jnp.concatenate([value[:32], value[32:]], axis=1)

        if device_count <= 8:
            found = [one(spot) for spot in range(device_count)]
            for peer in range(device_count):
                place = place_ref[peer, block]
                picked = found[0]
                for spot in range(1, device_count):
                    picked = jnp.where(place == spot, found[spot], picked)
                sorted_scr[peer, rows, :] = picked
        else:

            def spot_step(spot, carry):
                value = one(spot)
                for peer in range(device_count):
                    sorted_scr[peer, rows, :] = jnp.where(
                        place_ref[peer, block] == lax.convert_element_type(spot, BF16),
                        value,
                        sorted_scr[peer, rows, :],
                    )
                return carry

            lax.fori_loop(0, device_count, spot_step, 0)
        return carry

    lax.fori_loop(0, blocks, gather_step, 0)

    def unsort_step(peer, carry):
        slots = jnp.dot(
            unsort_ref[peer], sorted_scr[peer], preferred_element_type=F32
        ).astype(BF16)
        start = 0
        for out, size in zip(outs, sizes):
            out[peer] = slots[start : start + size]
            start += size
        return carry

    lax.fori_loop(0, device_count, unsort_step, 0, unroll=2)


def cycle_work(pieces, sizes, places, sort, unsort, offset, where, cycle_weight):
    groups = len(pieces)
    device_count, _, lanes = pieces[0].shape
    count = sum(piece.shape[1] for piece in pieces)
    out_shapes = [(device_count, size, lanes) for size in sizes]
    spread, pixel, back, gather = [jnp.asarray(table) for table in fourier_tables()]
    tables = [places, sort, unsort]
    return pl.pallas_call(
        functools.partial(cycle_kernel, groups, sizes),
        grid_spec=pltpu.PrefetchScalarGridSpec(
            num_scalar_prefetch=2,
            grid=(1,),
            in_specs=[pl.BlockSpec(memory_space=pltpu.SMEM)]
            + [whole(piece.shape) for piece in pieces]
            + [whole(table.shape) for table in tables]
            + [hbm(), whole(pixel.shape), whole(back.shape), hbm()],
            out_specs=[whole(shape) for shape in out_shapes],
            scratch_shapes=[
                pltpu.VMEM(spread.shape[1:], BF16),
                pltpu.VMEM(gather.shape[1:], BF16),
                pltpu.VMEM((device_count, count, lanes), BF16),
                pltpu.VMEM((SIDE * PADDED, lanes // 2), F32),
                pltpu.VMEM((SIDE, SIDE, lanes // 2), F32),
                pltpu.VMEM((SIDE * PADDED, lanes // 2), F32),
                pltpu.SemaphoreType.DMA((places.shape[1] + 1,)),
            ],
        ),
        out_shape=[jax.ShapeDtypeStruct(shape, BF16) for shape in out_shapes],
        compiler_params=pltpu.CompilerParams(vmem_limit_bytes=48 * MIB),
        cost_estimate=pl.CostEstimate(
            flops=4 * SIDE * 128 * 256 * 256 * 2, bytes_accessed=8 * MIB, transcendentals=0
        ),
        name="cycle_work",
    )(offset, where, cycle_weight, *pieces, *tables, spread, pixel, back, gather)


def adjoint_kernel(
    first, order_ref, where_ref, own_ref, core_ref, far_ref, corner_ref, weight_ref, legendre_ref, *refs
):
    out_ref, values_even, values_odd, terms_even, terms_odd = refs[-5:]
    step = pl.program_id(0)
    row = where_ref[0] >> 12
    base = (where_ref[0] & 4095) + first + step * BLOCK
    degrees = weight_ref.shape[1]
    cycles = legendre_ref.shape[1]
    owners = cycles // 4
    lanes = weight_ref.shape[0] // 2
    pitch = cycles + 8
    tiles = degrees // 128
    quarter = owners * 16
    degree = row * degrees + lax.broadcasted_iota(jnp.int32, (8, degrees), 1)
    sublane = lax.broadcasted_iota(jnp.int32, (8, degrees), 0)
    sources = (own_ref, core_ref, far_ref, corner_ref)
    for group in range(BLOCK // 16):
        values_scr = values_odd if group % 2 else values_even
        terms_scr = terms_odd if group % 2 else terms_even
        for place in range(16):
            wide = legendre_ref[group * 16 + place].astype(F32)
            for tile in range(tiles):
                values_scr[tile, place * pitch : place * pitch + cycles, :] = wide[
                    :, tile * 128 : tile * 128 + 128
                ]
        rows = jnp.concatenate(
            [
                source[
                    :, group * 16 : group * 16 + 16, part * lanes : (part + 1) * lanes
                ].reshape(quarter, lanes)
                for part in range(2)
                for source in sources
            ],
            axis=0,
        )
        terms_scr[...] = jnp.dot(
            jnp.concatenate([rows, rows], axis=1), weight_ref[...], preferred_element_type=F32
        )
        for half in range(2):
            total = [jnp.zeros((8, degrees), F32), jnp.zeros((8, degrees), F32)]
            for away in range(4):
                for owner in range(owners):
                    cycle = 4 * owner + (row ^ away)
                    factor = jnp.concatenate(
                        [
                            values_scr[tile, pl.ds(half * 8 * pitch + cycle, 8, stride=pitch), :]
                            for tile in range(tiles)
                        ],
                        axis=1,
                    )
                    for part in range(2):
                        at = (part * 4 + away) * quarter + owner * 16 + half * 8
                        total[part] = total[part] + terms_scr[at : at + 8, :] * factor
            lowest = jnp.zeros((8, degrees), jnp.int32)
            first_slot = group * 16 + half * 8
            for place in range(8):
                lowest = jnp.where(sublane == place, order_ref[base + first_slot + place], lowest)
            for part in range(2):
                out_ref[part, first_slot : first_slot + 8, :] = jnp.where(
                    degree >= lowest, total[part], 0.0
                )


def adjoint(first, orders, where, weight, pieces, legendre, earlier):
    orders_here, cycles, degrees = legendre.shape
    count = pieces[0].shape[1]
    steps = count // BLOCK
    start = first // BLOCK
    owners = cycles // 4
    lanes = weight.shape[0] // 2
    piece_spec = pl.BlockSpec((owners, BLOCK, 2 * lanes), lambda t, *_: (0, t, 0))
    out = jax.ShapeDtypeStruct((2, orders_here, degrees), F32)
    return pl.pallas_call(
        functools.partial(adjoint_kernel, first),
        grid_spec=pltpu.PrefetchScalarGridSpec(
            num_scalar_prefetch=2,
            grid=(steps,),
            in_specs=[piece_spec] * 4
            + [
                whole(weight.shape),
                pl.BlockSpec((BLOCK, cycles, degrees), lambda t, *_: (start + t, 0, 0)),
            ]
            + [anywhere()] * len(earlier),
            out_specs=pl.BlockSpec((2, BLOCK, degrees), lambda t, *_: (0, start + t, 0)),
            scratch_shapes=[
                pltpu.VMEM((degrees // 128, 16 * (cycles + 8), 128), F32),
                pltpu.VMEM((degrees // 128, 16 * (cycles + 8), 128), F32),
                pltpu.VMEM((32 * cycles, degrees), F32),
                pltpu.VMEM((32 * cycles, degrees), F32),
            ],
        ),
        out_shape=out,
        input_output_aliases={8: 0} if earlier else {},
        compiler_params=pltpu.CompilerParams(vmem_limit_bytes=48 * MIB),
        cost_estimate=pl.CostEstimate(
            flops=2 * count * cycles * degrees * lanes * 2 * 2,
            bytes_accessed=count * (cycles * degrees * 2 + 2 * cycles * lanes * 2),
            transcendentals=0,
        ),
        name="adjoint",
    )(orders, where, *pieces, weight, legendre, *earlier)


def slot_tables(orders, device_count):
    local_orders = orders.shape[0] // device_count
    blocks = local_orders // 32
    by_device = orders.reshape(device_count, local_orders)
    block = by_device // device_count
    position = 32 * (block % blocks) + block // blocks
    wanted = jnp.arange(local_orders, dtype=jnp.int32)
    sort = position[:, None, :] == wanted[None, :, None]
    unsort = position[:, :, None] == wanted[None, None, :]
    place = jnp.sum(jnp.where(sort, (by_device % device_count)[:, None, :], 0), axis=2)
    place = place.reshape(device_count, blocks, 32, 1)
    place = jnp.broadcast_to(place, (device_count, blocks, 32, 256))
    return place.astype(BF16), sort.astype(BF16), unsort.astype(BF16)


def body(
    coeffs,
    legendre,
    alpha_table,
    beta_table,
    radial_weight,
    radius_index,
    orders,
    cycle_offset,
    cycle_weight,
):
    row_id = lax.axis_index("row")
    ma_id = lax.axis_index("ma")
    device_count = lax.axis_size("ma")
    row_count = lax.axis_size("row")
    local_orders = coeffs.shape[1]
    where = (row_id * 4096 + ma_id * local_orders).astype(jnp.int32).reshape(1)
    synth_weight, adjoint_weight = filter_weights(
        radius_index, radial_weight, alpha_table, beta_table
    )
    core_pairs = [(i, i ^ 1) for i in range(row_count)]
    far_pairs = [(i, i ^ 2) for i in range(row_count)]
    units = local_orders // 32
    if local_orders >= 256:
        counts = [5 * local_orders // 16, 5 * local_orders // 16, 6 * local_orders // 16]
    else:
        counts = [local_orders // 2, local_orders // 2]
    kept, others, outgoing, incoming, arrived = [], [], [], [], []

    def after(*values):
        return lax.optimization_barrier((where, *values))[0]

    def launch(chunk, token):
        first = sum(counts[:chunk])
        keep, send = synth(
            first, counts[chunk], orders, token, coeffs, synth_weight, legendre
        )
        kept.append(keep)
        others.append(lax.ppermute(send, "row", core_pairs))

    def pass_on(chunk, token):
        outgoing.append(core_sum(kept[chunk], others[chunk], token))
        incoming.append(lax.ppermute(outgoing[chunk], "row", far_pairs))

    def deliver(own, token):
        summed = full_sum(list(zip(kept[own], others[own], incoming[own])), token)
        arrived.append(lax.all_to_all(summed, "ma", split_axis=0, concat_axis=0, tiled=True))
        return summed

    launch(0, where)
    launch(1, where)
    pass_on(0, after(kept[1]))
    pass_on(1, after(outgoing[0]))
    if len(counts) == 3:
        launch(2, after(outgoing[1]))
        pass_on(2, after(deliver(slice(0, 2), after(kept[2]))))
        tables = slot_tables(lax.optimization_barrier((orders, outgoing[2]))[0], device_count)
        half = own_sum(kept[2], others[2], after(outgoing[2]))
        places, sort, unsort, half, token = lax.optimization_barrier((*tables, half, where))
        summed = last_sum(half, incoming[2], token)
        arrived.append(lax.all_to_all(summed, "ma", split_axis=0, concat_axis=0, tiled=True))
    else:
        deliver(slice(0, 1), after(outgoing[1]))
        deliver(slice(1, 2), after(outgoing[1]))
        places, sort, unsort = slot_tables(orders, device_count)
    early = 32 * (units // 2)
    sizes = (early, local_orders - early)
    analysed = cycle_work(
        arrived, sizes, places, sort, unsort, cycle_offset, where, cycle_weight
    )
    own = [
        lax.all_to_all(piece, "ma", split_axis=0, concat_axis=0, tiled=True) for piece in analysed
    ]
    far = lax.ppermute(own[0], "row", far_pairs)
    far, second = lax.optimization_barrier((far, own[1]))
    gradient, first = [], 0
    for own_part, far_part in ((own[0], far), (second, None)):
        if far_part is None:
            far_part = lax.ppermute(own_part, "row", far_pairs)
        if gradient:
            far_part, gradient[-1] = lax.optimization_barrier((far_part, gradient[-1]))
        core = lax.ppermute(own_part, "row", core_pairs)
        corner = lax.ppermute(far_part, "row", core_pairs)
        gradient.append(
            adjoint(
                first,
                orders,
                where,
                adjoint_weight,
                (own_part, core, far_part, corner),
                legendre,
                gradient[-1:],
            )
        )
        first += own_part.shape[1]
    return gradient[-1]


def solution(mesh):
    in_specs = (
        P(None, "ma", "row"),
        P("ma", None, "row"),
        P(None, "row"),
        P(None, "row"),
        P(),
        P(),
        P(),
        P("ma"),
        P("ma"),
    )
    out_specs = P(None, "ma", "row")
    return jax.shard_map(body, mesh=mesh, in_specs=in_specs, out_specs=out_specs, check_vma=False)
```
